32 devices in a mesh: fibre: 8 (over z, core), rest: 4 (over y, x).
Axes of the slice: x: 2, y: 2, z: 4, core: 2. Of those that a mesh axis runs over, the one named last changes fastest.
Arguments:
- slab: float32 [672, 65536], P('fibre', 'rest'), may hold values from -6 to 6
- start_basis: float32 [672, 96], replicated, may hold values from -6 to 6
Outputs:
- factor: float32 [672, 96], replicated
- core: float32 [96, 65536], P('fibre', 'rest')
The draws below stay inside these ranges and needn't reach their ends.
All inputs are finite; a program needn't handle non-finite values.
Results may differ from the reference program's by a relative error of at most 0.00023.
Values sent between devices are 32-bit elements; how exact they have to be, the bound alone decides.
No kernel may reach another device: no remote copies, remote signals or barrier semaphores. Data moves between devices by JAX's collectives and lax.ppermute only.
A program may use at most 64 MiB of HBM per device.

```python
import jax
import jax.numpy as jnp
from jax import lax

I1 = 672
RANK = 96
ITERS = 3
COLS = 65536


def block_levels(key, shape, split, smallest, top_value):
    gain = 1.0
    for axis_at, shards_of in split:
        draws = jax.random.uniform(jax.random.fold_in(jax.random.fold_in(key, 6), axis_at), (shards_of,), jnp.float32, smallest / len(split), top_value / len(split))
        gain = gain * jnp.repeat(jnp.exp(draws), shape[axis_at] // shards_of).reshape((-1,) + (1,) * (len(shape) - 1 - axis_at))
    return gain


def gaussian(own_key, dims, scale, reach, pieces=(), dtype=jnp.bfloat16):
    result = jax.random.normal(own_key, dims, jnp.float32) * scale
    if len(pieces) > 0:
        result = block_levels(own_key, dims, pieces, -0.22, 0.18) * result
    return jnp.clip(result, min=-reach, max=reach).astype(dtype)


def setup_inputs(seed: int = 0) -> dict:
    key_of = jax.random.split(jax.random.key(seed), 3)
    slab = gaussian(key_of[0], (I1, COLS), 1.0, 6.0, ((0, 8), (1, 4)), jnp.float32)
    start_basis = gaussian(key_of[1], (I1, RANK), 1.0, 6.0, (), jnp.float32)
    return {"slab": slab, "start_basis": start_basis}


def reference(slab, start_basis):
    hp = lax.Precision.HIGHEST
    gram = jnp.dot(slab.astype(jnp.float32), slab.T.astype(jnp.float32), precision=hp, preferred_element_type=jnp.float32)
    basis = start_basis
    for step in range(ITERS):
        image = jnp.dot(gram.astype(jnp.float32), basis.astype(jnp.float32), precision=hp, preferred_element_type=jnp.float32)
        small = jnp.dot(image.T.astype(jnp.float32), image.astype(jnp.float32), precision=hp, preferred_element_type=jnp.float32)
        lower = jnp.linalg.cholesky(small)
        basis = lax.linalg.triangular_solve(lower, image, left_side=False, lower=True, transpose_a=True)
    core = jnp.dot(basis.T.astype(jnp.float32), slab.astype(jnp.float32), precision=hp, preferred_element_type=jnp.float32)
    return (basis, core)
```

```python
import jax
import jax.numpy as jnp
from jax import lax
from jax.sharding import PartitionSpec as P

ITERS = 3
HIGH = lax.Precision.HIGH
HIGHEST = lax.Precision.HIGHEST


def orthonormal(image, small):
    lower = jnp.linalg.cholesky(small)
    return lax.linalg.triangular_solve(lower, image, left_side=False, lower=True, transpose_a=True)


def swap(x, axis, size, bits):
    return lax.ppermute(x, axis, [(i, i ^ bits) for i in range(size)])


def in_order(core, mine, other, axis):
    return jnp.where(core == 0, jnp.concatenate([mine, other], axis), jnp.concatenate([other, mine], axis))


def pack(gram):
    h = gram.shape[0] // 2
    upper = lax.broadcasted_iota(jnp.int32, (h, h), 0) <= lax.broadcasted_iota(jnp.int32, (h, h), 1)
    low = gram[h:, h:]
    tri = jnp.where(upper, gram[:h, :h], low)
    eye = lax.broadcasted_iota(jnp.int32, (h, h), 0) == lax.broadcasted_iota(jnp.int32, (h, h), 1)
    diag = jnp.sum(jnp.where(eye, low, 0.0), axis=0, keepdims=True)
    return jnp.concatenate([gram[:h, h:], tri, diag], 0)


def unpack(packed, n):
    h = n // 2
    row = lax.broadcasted_iota(jnp.int32, (h, h), 0)
    col = lax.broadcasted_iota(jnp.int32, (h, h), 1)
    cross, tri, diag = packed[:h], packed[h : 2 * h], packed[2 * h : 2 * h + 1]
    top = jnp.where(row <= col, tri, tri.T)
    low = jnp.where(row > col, tri, jnp.where(row == col, diag, tri.T))
    return jnp.concatenate([jnp.concatenate([top, cross], 1), jnp.concatenate([cross.T, low], 1)], 0)


def sum_everywhere(packed, fibre, rest):
    f, r = lax.axis_index("fibre"), lax.axis_index("rest")
    core = f % 2
    piece = -(-packed.shape[0] // (2 * rest * 8)) * 8
    half = piece * rest
    padded = jnp.pad(packed, ((0, 2 * half - packed.shape[0]), (0, 0)))
    width = packed.shape[1]
    mine = lax.dynamic_slice(padded, (core * half, 0), (half, width))
    theirs = lax.dynamic_slice(padded, ((1 - core) * half, 0), (half, width))
    mine = mine + swap(theirs, "fibre", fibre, 1)
    total = lax.dynamic_slice(mine, (r * piece, 0), (piece, width))
    for bits in range(1, rest):
        part = lax.dynamic_slice(mine, ((r ^ bits) * piece, 0), (piece, width))
        total = total + swap(part, "rest", rest, bits)
    terms = [total] + [swap(total, "fibre", fibre, 2 * bits) for bits in range(1, fibre // 2)]
    while len(terms) > 1:
        terms = [terms[i] + terms[i + 1] for i in range(0, len(terms), 2)]
    total = terms[0]
    out = jnp.zeros((rest, piece, width), jnp.float32)
    for bits in range(rest):
        got = swap(total, "rest", rest, bits) if bits else total
        out = lax.dynamic_update_slice(out, got[None], (r ^ bits, 0, 0))
    out = out.reshape(half, width)
    return in_order(core, out, swap(out, "fibre", fibre, 1), 0)


def shards(fibre, rest, slab, start_basis):
    rows, cols = slab.shape
    zs = fibre // 2
    f = lax.axis_index("fibre")
    z, core = f // 2, f % 2
    half = cols // 2
    part = half // zs
    chunks = [(0, part * 3 // 4), (part * 3 // 4, part // 4)]
    order = list(range(zs - 1, -1, -1))
    gram = 0.0
    fibres = []
    for start, width in chunks:
        whole = jnp.zeros((zs, 2 * rows, width), jnp.float32)
        for bits in order:
            at = (z ^ bits) * part + start
            mine = lax.dynamic_slice(slab, (0, core * half + at), (rows, width))
            theirs = lax.dynamic_slice(slab, (0, (1 - core) * half + at), (rows, width))
            block = in_order(core, mine, swap(theirs, "fibre", fibre, 1), 0)
            if bits:
                block = swap(block, "fibre", fibre, 2 * bits)
            whole = lax.dynamic_update_slice(whole, block[None], (z ^ bits, 0, 0))
        whole = whole.reshape(zs * 2 * rows, width)
        fibres.append(whole)
        gram = gram + jnp.dot(whole, whole.T, precision=HIGH, preferred_element_type=jnp.float32)
    n = gram.shape[0]
    gram = unpack(sum_everywhere(pack(gram), fibre, rest), n)
    basis = start_basis
    for step in range(ITERS):
        image = jnp.dot(gram, basis, precision=HIGHEST, preferred_element_type=jnp.float32)
        small = jnp.dot(image.T, image, precision=HIGHEST, preferred_element_type=jnp.float32)
        basis = orthonormal(image, small)
    rank = basis.shape[1]
    own = rank // fibre
    out = jnp.zeros((own, cols), jnp.float32)
    for (start, width), whole in zip(chunks, fibres):
        share = jnp.dot(basis.T, whole, precision=HIGH, preferred_element_type=jnp.float32)
        for bits in order:
            block = lax.dynamic_slice(share, ((z ^ bits) * 2 * own, 0), (2 * own, width))
            if bits:
                block = swap(block, "fibre", fibre, 2 * bits)
            mine = lax.dynamic_slice(block, (core * own, 0), (own, width))
            theirs = lax.dynamic_slice(block, ((1 - core) * own, 0), (own, width))
            other = swap(theirs, "fibre", fibre, 1)
            at = (z ^ bits) * part + start
            out = lax.dynamic_update_slice(out, mine, (0, core * half + at))
            out = lax.dynamic_update_slice(out, other, (0, (1 - core) * half + at))
    return (basis, out)


def solution(mesh):
    fibre, rest = mesh.shape["fibre"], mesh.shape["rest"]
    return jax.shard_map(
        lambda slab, start_basis: shards(fibre, rest, slab, start_basis),
        mesh=mesh,
        in_specs=(P("fibre", "rest"), P()),
        out_specs=(P(), P("fibre", "rest")),
        check_vma=False,
    )
```

```python
import functools

import jax
import jax.numpy as jnp
from jax import lax
from jax.experimental import pallas as pl
from jax.experimental.pallas import tpu as pltpu
from jax.sharding import PartitionSpec as P

ITERS = 3
HIGH = lax.Precision.HIGH
HIGHEST = lax.Precision.HIGHEST


def swap(x, axis, size, bits):
    return lax.ppermute(x, axis, [(i, i ^ bits) for i in range(size)])


def in_order(core, mine, other, axis):
    return jnp.where(core == 0, jnp.concatenate([mine, other], axis), jnp.concatenate([other, mine], axis))


def pack(gram):
    h = gram.shape[0] // 2
    upper = lax.broadcasted_iota(jnp.int32, (h, h), 0) <= lax.broadcasted_iota(jnp.int32, (h, h), 1)
    low = gram[h:, h:]
    tri = jnp.where(upper, gram[:h, :h], low)
    eye = lax.broadcasted_iota(jnp.int32, (h, h), 0) == lax.broadcasted_iota(jnp.int32, (h, h), 1)
    diag = jnp.sum(jnp.where(eye, low, 0.0), axis=0, keepdims=True)
    return jnp.concatenate([gram[:h, h:], tri, diag], 0)


def unpack(packed, n):
    h = n // 2
    row = lax.broadcasted_iota(jnp.int32, (h, h), 0)
    col = lax.broadcasted_iota(jnp.int32, (h, h), 1)
    cross, tri, diag = packed[:h], packed[h : 2 * h], packed[2 * h : 2 * h + 1]
    top = jnp.where(row <= col, tri, tri.T)
    low = jnp.where(row > col, tri, jnp.where(row == col, diag, tri.T))
    return jnp.concatenate([jnp.concatenate([top, cross], 1), jnp.concatenate([cross.T, low], 1)], 0)


def sum_everywhere(packed, fibre, rest):
    f, r = lax.axis_index("fibre"), lax.axis_index("rest")
    core = f % 2
    piece = -(-packed.shape[0] // (2 * rest * 8)) * 8
    half = piece * rest
    padded = jnp.pad(packed, ((0, 2 * half - packed.shape[0]), (0, 0)))
    width = packed.shape[1]
    mine = lax.dynamic_slice(padded, (core * half, 0), (half, width))
    theirs = lax.dynamic_slice(padded, ((1 - core) * half, 0), (half, width))
    mine = mine + swap(theirs, "fibre", fibre, 1)
    total = lax.dynamic_slice(mine, (r * piece, 0), (piece, width))
    for bits in range(1, rest):
        part = lax.dynamic_slice(mine, ((r ^ bits) * piece, 0), (piece, width))
        total = total + swap(part, "rest", rest, bits)
    terms = [total] + [swap(total, "fibre", fibre, 2 * bits) for bits in range(1, fibre // 2)]
    while len(terms) > 1:
        terms = [terms[i] + terms[i + 1] for i in range(0, len(terms), 2)]
    total = terms[0]
    out = jnp.zeros((rest, piece, width), jnp.float32)
    for bits in range(rest):
        got = swap(total, "rest", rest, bits) if bits else total
        out = lax.dynamic_update_slice(out, got[None], (r ^ bits, 0, 0))
    out = out.reshape(half, width)
    return in_order(core, out, swap(out, "fibre", fibre, 1), 0)


def lower_inverse(small):
    n = small.shape[0]
    lanes = 128
    full = (8, lanes)
    col = lax.broadcasted_iota(jnp.int32, full, 1)
    row = lax.broadcasted_iota(jnp.int32, full, 0)
    left = [small[8 * i : 8 * i + 8, :] for i in range(n // 8)]
    right = [(col == row + 8 * i).astype(jnp.float32) for i in range(n // 8)]
    done = []
    for p in range(n // 8):
        at = 8 * p
        d = {(a, b): jnp.broadcast_to(left[p][a : a + 1, at + b : at + b + 1], full) for a in range(8) for b in range(a + 1)}
        low, inv_diag = {}, []
        for b in range(8):
            r = lax.rsqrt(d[b, b])
            inv_diag.append(r)
            for a in range(b + 1, 8):
                low[a, b] = d[a, b] * r
            for a in range(b + 1, 8):
                for c in range(b + 1, a + 1):
                    d[a, c] = d[a, c] - low[a, b] * low[c, b]
        inv = {}
        for b in range(8):
            inv[b, b] = inv_diag[b]
            for a in range(b + 1, 8):
                s = low[a, b] * inv[b, b]
                for k in range(b + 1, a):
                    s = s + low[a, k] * inv[k, b]
                inv[a, b] = -s * inv_diag[a]
        lrow = [jnp.broadcast_to(left[p][k : k + 1, :], full) for k in range(8)]
        rrow = [jnp.broadcast_to(right[p][k : k + 1, :], full) for k in range(8)]
        y, v = [], []
        for m in range(8):
            ym, vm = inv[m, 0] * lrow[0], inv[m, 0] * rrow[0]
            for k in range(1, m + 1):
                ym, vm = ym + inv[m, k] * lrow[k], vm + inv[m, k] * rrow[k]
            y.append(ym)
            v.append(vm)
        out = v[0]
        for m in range(1, 8):
            out = jnp.where(row == m, v[m], out)
        done.append(out)
        for i in range(p + 1, n // 8):
            c = [jnp.broadcast_to(left[i][:, at + k : at + k + 1], full) for k in range(8)]
            li, ri = left[i], right[i]
            for m in range(8):
                f = inv[m, 0] * c[0]
                for k in range(1, m + 1):
                    f = f + inv[m, k] * c[k]
                li = li - f * y[m]
                ri = ri - f * v[m]
            left[i], right[i] = li, ri
    return jnp.concatenate(done, 0)


def iterations_kernel(iters, gram_ref, start_ref, factor_ref):
    def times(a, b, dims):
        return lax.dot_general(a, b, (dims, ((), ())), precision=HIGHEST, preferred_element_type=jnp.float32)

    image = times(gram_ref[...], start_ref[...], ((1,), (0,)))
    for step in range(iters):
        small = times(image, image, ((0,), (0,)))
        inverse = lower_inverse(jnp.pad(small, ((0, 0), (0, 128 - small.shape[1]))))[:, : small.shape[1]]
        if step < iters - 1:
            image = times(times(gram_ref[...], image, ((1,), (0,))), inverse, ((1,), (1,)))
        else:
            factor_ref[...] = times(image, inverse, ((1,), (1,)))

def iterations(gram, start, iters=3):
    return pl.pallas_call(
        functools.partial(iterations_kernel, iters),
        out_shape=jax.ShapeDtypeStruct(start.shape, jnp.float32),
        in_specs=[pl.BlockSpec(memory_space=pltpu.VMEM)] * 2,
        out_specs=pl.BlockSpec(memory_space=pltpu.VMEM),
        compiler_params=pltpu.CompilerParams(vmem_limit_bytes=32 * 2**20),
        name="iterations",
    )(gram, start)


def shards(fibre, rest, slab, start_basis):
    rows, cols = slab.shape
    zs = fibre // 2
    f = lax.axis_index("fibre")
    z, core = f // 2, f % 2
    half = cols // 2
    part = half // zs
    unit = part // 8
    chunks = [(0, unit), (unit, 5 * unit), (6 * unit, 2 * unit)]
    order = list(range(zs - 1, -1, -1))
    gram = 0.0
    fibres = []
    for start, width in chunks:
        blocks = []
        for bits in order:
            at = (z ^ bits) * part + start
            mine = lax.dynamic_slice(slab, (0, core * half + at), (rows, width))
            theirs = lax.dynamic_slice(slab, (0, (1 - core) * half + at), (rows, width))
            blocks.append(in_order(core, mine, swap(theirs, "fibre", fibre, 1), 0))
        slab, blocks = lax.optimization_barrier((slab, blocks))
        whole = jnp.zeros((zs, 2 * rows, width), jnp.float32)
        for bits, block in zip(order, blocks):
            if bits:
                block = swap(block, "fibre", fibre, 2 * bits)
            whole = lax.dynamic_update_slice(whole, block[None], (z ^ bits, 0, 0))
        whole = whole.reshape(zs * 2 * rows, width)
        fibres.append(whole)
        gram = gram + jnp.dot(whole, whole.T, precision=HIGH, preferred_element_type=jnp.float32)
    n = gram.shape[0]
    gram = unpack(sum_everywhere(pack(gram), fibre, rest), n)
    basis = iterations(gram, start_basis, ITERS)
    rank = basis.shape[1]
    own = rank // fibre
    rows_of = [lax.dynamic_slice(basis.T, ((z ^ bits) * 2 * own, 0), (2 * own, n)) for bits in range(zs)]
    rows_of = jnp.concatenate(rows_of, 0)
    share = [jnp.dot(rows_of, whole, precision=HIGH, preferred_element_type=jnp.float32) for whole in fibres]
    share = jnp.concatenate(share, 1)
    arrived = jnp.zeros((zs, 2 * own, part), jnp.float32)
    for bits in order:
        block = share[2 * own * bits : 2 * own * (bits + 1)]
        if bits:
            block = swap(block, "fibre", fibre, 2 * bits)
        arrived = lax.dynamic_update_slice(arrived, block[None], (z ^ bits, 0, 0))
    mine = lax.dynamic_slice(arrived, (0, core * own, 0), (zs, own, part))
    theirs = lax.dynamic_slice(arrived, (0, (1 - core) * own, 0), (zs, own, part))
    theirs = theirs.transpose(1, 0, 2).reshape(own, half)
    mine = mine.transpose(1, 0, 2).reshape(own, half)
    return (basis, in_order(core, mine, swap(theirs, "fibre", fibre, 1), 1))


def solution(mesh):
    fibre, rest = mesh.shape["fibre"], mesh.shape["rest"]
    return jax.shard_map(
        lambda slab, start_basis: shards(fibre, rest, slab, start_basis),
        mesh=mesh,
        in_specs=(P("fibre", "rest"), P()),
        out_specs=(P(), P("fibre", "rest")),
        check_vma=False,
    )
```

```python
import functools

import jax
import jax.numpy as jnp
from jax import lax
from jax.experimental import pallas as pl
from jax.experimental.pallas import tpu as pltpu
from jax.sharding import PartitionSpec as P

ITERS = 3
HIGH = lax.Precision.HIGH
HIGHEST = lax.Precision.HIGHEST


def swap(x, axis, size, bits):
    return lax.ppermute(x, axis, [(i, i ^ bits) for i in range(size)])


def in_order(core, mine, other, axis):
    return jnp.where(core == 0, jnp.concatenate([mine, other], axis), jnp.concatenate([other, mine], axis))


def split(x):
    high = x.astype(jnp.bfloat16)
    return high, (x - high.astype(jnp.float32)).astype(jnp.bfloat16)


def layout(n):
    places, at, strip = [], 0, n % 128
    for j in range(n // 128):
        places.append((at, 128 * (j + 1), at + 128 * (j + 1)))
        at += 128 * (j + 1) + strip
    return places, at, at + strip


def pack_kernel(core_ref, whole_ref, gram_ref, mine_ref, theirs_ref, packed):
    n = whole_ref.shape[0]
    places, corner, size = layout(n)
    edge = n // 128 * 128
    high, low = split(whole_ref[...])

    def block(r0, r1, c0, c1):
        def times(a, b):
            return lax.dot_general(a, b, (((1,), (1,)), ((), ())), preferred_element_type=jnp.float32)

        total = times(high[r0:r1], low[c0:c1]) + times(low[r0:r1], high[c0:c1]) + times(high[r0:r1], high[c0:c1])
        return total + gram_ref[r0:r1, c0:c1]

    for start in range(0, edge, 256):
        stop = min(start + 256, edge)
        upper = block(0, stop, start, stop)
        for j in range(start // 128, stop // 128):
            at, rows, _ = places[j]
            packed[at : at + rows, :] = upper[:rows, 128 * j - start : 128 * j - start + 128]
    if n > edge:
        strip = block(edge, n, 0, n)
        for j, (_, _, at) in enumerate(places):
            packed[at : at + n - edge, :] = strip[:, 128 * j : 128 * j + 128]
        packed[corner:size, :] = jnp.pad(strip[:, edge:], ((0, 0), (0, 128 - (n - edge))))
    half = size // 2
    core = core_ref[0]
    mine_ref[...] = packed[pl.ds(pl.multiple_of(core * half, 8), half), :]
    theirs_ref[...] = packed[pl.ds(pl.multiple_of((1 - core) * half, 8), half), :]


def pack(core, whole, gram):
    size = layout(whole.shape[0])[2]
    half = jax.ShapeDtypeStruct((size // 2, 128), jnp.float32)
    return pl.pallas_call(
        pack_kernel,
        out_shape=(half, half),
        in_specs=[pl.BlockSpec(memory_space=pltpu.SMEM)] + [pl.BlockSpec(memory_space=pltpu.VMEM)] * 2,
        out_specs=[pl.BlockSpec(memory_space=pltpu.VMEM)] * 2,
        scratch_shapes=[pltpu.VMEM((size, 128), jnp.float32)],
        compiler_params=pltpu.CompilerParams(vmem_limit_bytes=32 * 2**20),
        name="gram_pack",
    )(core.reshape(1), whole, gram)


def lower_inverse(small):
    n = small.shape[0]
    lanes = 128
    full = (8, lanes)
    col = lax.broadcasted_iota(jnp.int32, full, 1)
    row = lax.broadcasted_iota(jnp.int32, full, 0)
    left = [small[8 * i : 8 * i + 8, :] for i in range(n // 8)]
    right = [(col == row + 8 * i).astype(jnp.float32) for i in range(n // 8)]
    done = []
    for p in range(n // 8):
        at = 8 * p
        d = {(a, b): jnp.broadcast_to(left[p][a : a + 1, at + b : at + b + 1], full) for a in range(8) for b in range(a + 1)}
        low, inv_diag = {}, []
        for b in range(8):
            r = lax.rsqrt(d[b, b])
            inv_diag.append(r)
            for a in range(b + 1, 8):
                low[a, b] = d[a, b] * r
            for a in range(b + 1, 8):
                for c in range(b + 1, a + 1):
                    d[a, c] = d[a, c] - low[a, b] * low[c, b]
        inv = {}
        for b in range(8):
            inv[b, b] = inv_diag[b]
            for a in range(b + 1, 8):
                s = low[a, b] * inv[b, b]
                for k in range(b + 1, a):
                    s = s + low[a, k] * inv[k, b]
                inv[a, b] = -s * inv_diag[a]
        lrow = [jnp.broadcast_to(left[p][k : k + 1, :], full) for k in range(8)]
        rrow = [jnp.broadcast_to(right[p][k : k + 1, :], full) for k in range(8)]
        y, v = [], []
        for m in range(8):
            ym, vm = inv[m, 0] * lrow[0], inv[m, 0] * rrow[0]
            for k in range(1, m + 1):
                ym, vm = ym + inv[m, k] * lrow[k], vm + inv[m, k] * rrow[k]
            y.append(ym)
            v.append(vm)
        out = v[0]
        for m in range(1, 8):
            out = jnp.where(row == m, v[m], out)
        done.append(out)
        for i in range(p + 1, n // 8):
            c = [jnp.broadcast_to(left[i][:, at + k : at + k + 1], full) for k in range(8)]
            li, ri = left[i], right[i]
            for m in range(8):
                f = inv[m, 0] * c[0]
                for k in range(1, m + 1):
                    f = f + inv[m, k] * c[k]
                li = li - f * y[m]
                ri = ri - f * v[m]
            left[i], right[i] = li, ri
    return jnp.concatenate(done, 0)


def iterations_kernel(iters, core_ref, mine_ref, other_ref, start_ref, factor_ref, packed, gram):
    def times(a, b, dims):
        return lax.dot_general(a, b, (dims, ((), ())), precision=HIGHEST, preferred_element_type=jnp.float32)

    n = gram.shape[0]
    places, corner, size = layout(n)
    edge = n // 128 * 128
    half = size // 2
    core = core_ref[0]
    packed[pl.ds(pl.multiple_of(core * half, 8), half), :] = mine_ref[...]
    packed[pl.ds(pl.multiple_of((1 - core) * half, 8), half), :] = other_ref[...]
    for j, (at, rows, strip) in enumerate(places):
        cols = slice(128 * j, 128 * j + 128)
        gram[:rows, cols] = packed[at : at + rows, :]
        for i in range(j):
            gram[cols, 128 * i : 128 * i + 128] = packed[at + 128 * i : at + 128 * i + 128, :].T
        if n > edge:
            gram[edge:, cols] = packed[strip : strip + n - edge, :]
            gram[cols, edge:] = packed[strip : strip + n - edge, :].T
    if n > edge:
        gram[edge:, edge:] = packed[corner:size, : n - edge]

    image = times(gram[...], start_ref[...], ((1,), (0,)))
    for step in range(iters):
        small = times(image, image, ((0,), (0,)))
        inverse = lower_inverse(jnp.pad(small, ((0, 0), (0, 128 - small.shape[1]))))[:, : small.shape[1]]
        if step < iters - 1:
            image = times(times(gram[...], image, ((1,), (0,))), inverse, ((1,), (1,)))
        else:
            factor_ref[...] = times(image, inverse, ((1,), (1,)))


def iterations(core, mine, other, start, iters):
    n = start.shape[0]
    return pl.pallas_call(
        functools.partial(iterations_kernel, iters),
        out_shape=jax.ShapeDtypeStruct(start.shape, jnp.float32),
        in_specs=[pl.BlockSpec(memory_space=pltpu.SMEM)] + [pl.BlockSpec(memory_space=pltpu.VMEM)] * 3,
        out_specs=pl.BlockSpec(memory_space=pltpu.VMEM),
        scratch_shapes=[pltpu.VMEM((layout(n)[2], 128), jnp.float32), pltpu.VMEM((n, n), jnp.float32)],
        compiler_params=pltpu.CompilerParams(vmem_limit_bytes=32 * 2**20),
        name="iterations",
    )(core.reshape(1), mine, other, start)


def sum_everywhere(mine, theirs, fibre, rest):
    r = lax.axis_index("rest")
    half, width = mine.shape
    piece = -(-half // (8 * rest)) * 8
    mine = mine + swap(theirs, "fibre", fibre, 1)
    mine = jnp.pad(mine, ((0, piece * rest - half), (0, 0)))
    total = lax.dynamic_slice(mine, (r * piece, 0), (piece, width))
    for bits in range(1, rest):
        part = lax.dynamic_slice(mine, ((r ^ bits) * piece, 0), (piece, width))
        total = total + swap(part, "rest", rest, bits)
    terms = [total] + [swap(total, "fibre", fibre, 2 * bits) for bits in range(1, fibre // 2)]
    while len(terms) > 1:
        terms = [terms[i] + terms[i + 1] for i in range(0, len(terms), 2)]
    total = terms[0]
    out = jnp.zeros((rest, piece, width), jnp.float32)
    for bits in range(rest):
        got = swap(total, "rest", rest, bits) if bits else total
        out = lax.dynamic_update_slice(out, got[None], (r ^ bits, 0, 0))
    out = out.reshape(rest * piece, width)[:half]
    return out, swap(out, "fibre", fibre, 1)


def shards(fibre, rest, slab, start_basis):
    rows, cols = slab.shape
    zs = fibre // 2
    f = lax.axis_index("fibre")
    z, core = f // 2, f % 2
    half = cols // 2
    part = half // zs
    chunks = [(0, part * 3 // 4), (part * 3 // 4, part // 4)]
    order = list(range(zs - 1, -1, -1))
    fibres = []
    before = [None] * zs
    for start, width in chunks:
        whole = jnp.zeros((zs, 2 * rows, width), jnp.float32)
        for bits in order:
            at = (z ^ bits) * part + start
            mine = lax.dynamic_slice(slab, (0, core * half + at), (rows, width))
            theirs = lax.dynamic_slice(slab, (0, (1 - core) * half + at), (rows, width))
            block = in_order(core, mine, swap(theirs, "fibre", fibre, 1), 0)
            slab, block = lax.optimization_barrier((slab, block))
            if bits:
                if before[bits] is not None:
                    block, before[bits] = lax.optimization_barrier((block, before[bits]))
                block = before[bits] = swap(block, "fibre", fibre, 2 * bits)
            whole = lax.dynamic_update_slice(whole, block[None], (z ^ bits, 0, 0))
        fibres.append(whole.reshape(zs * 2 * rows, width))
    n = zs * 2 * rows
    gram = jnp.dot(fibres[0], fibres[0].T, precision=HIGH, preferred_element_type=jnp.float32)
    mine, other = sum_everywhere(*pack(core, fibres[1], gram), fibre, rest)
    basis = iterations(core, mine, other, start_basis, ITERS)
    rank = basis.shape[1]
    own = rank // fibre
    rows_of = [lax.dynamic_slice(basis.T, ((z ^ bits) * 2 * own, 0), (2 * own, n)) for bits in range(zs)]
    rows_of = jnp.concatenate(rows_of, 0)
    share = [jnp.dot(rows_of, whole, precision=HIGH, preferred_element_type=jnp.float32) for whole in fibres]
    share = jnp.concatenate(share, 1)
    arrived = jnp.zeros((zs, 2 * own, part), jnp.float32)
    for bits in order:
        block = share[2 * own * bits : 2 * own * (bits + 1)]
        if bits:
            block = swap(block, "fibre", fibre, 2 * bits)
        arrived = lax.dynamic_update_slice(arrived, block[None], (z ^ bits, 0, 0))
    mine = lax.dynamic_slice(arrived, (0, core * own, 0), (zs, own, part))
    theirs = lax.dynamic_slice(arrived, (0, (1 - core) * own, 0), (zs, own, part))
    theirs = theirs.transpose(1, 0, 2).reshape(own, half)
    mine = mine.transpose(1, 0, 2).reshape(own, half)
    return (basis, in_order(core, mine, swap(theirs, "fibre", fibre, 1), 1))


def solution(mesh):
    fibre, rest = mesh.shape["fibre"], mesh.shape["rest"]
    return jax.shard_map(
        lambda slab, start_basis: shards(fibre, rest, slab, start_basis),
        mesh=mesh,
        in_specs=(P("fibre", "rest"), P()),
        out_specs=(P(), P("fibre", "rest")),
        check_vma=False,
    )
```

```python
import functools

import jax
import jax.numpy as jnp
from jax import lax
from jax.experimental import pallas as pl
from jax.experimental.pallas import tpu as pltpu
from jax.sharding import PartitionSpec as P

ITERS = 3
HIGH = lax.Precision.HIGH
HIGHEST = lax.Precision.HIGHEST


def swap(x, axis, size, bits):
    return lax.ppermute(x, axis, [(i, i ^ bits) for i in range(size)])


def in_order(core, mine, other, axis):
    return jnp.where(core == 0, jnp.concatenate([mine, other], axis), jnp.concatenate([other, mine], axis))


def prepare_kernel(chunks, place_ref, slab_ref, got_ref, *refs):
    outs, own, sems = refs[:-2], refs[-2], refs[-1]
    zs, rows, part = own.shape
    z, core = place_ref[0], place_ref[1]

    def fetch(bits):
        at = pl.multiple_of(core * (zs * part) + (z ^ bits) * part, 128)
        return pltpu.make_async_copy(slab_ref.at[:, pl.ds(at, part)], own.at[bits], sems.at[bits])

    for bits in reversed(range(zs)):
        fetch(bits).start()
    for bits in reversed(range(zs)):
        fetch(bits).wait()
        for c, (start, width) in enumerate(chunks):
            out = outs[c * zs + bits]
            at = pl.multiple_of((z ^ bits) * part + start, 128)

            @pl.when(core == 0)
            def _():
                out[:rows, :] = own[bits, :, start : start + width]
                out[rows:, :] = got_ref[:, pl.ds(at, width)]

            @pl.when(core == 1)
            def _():
                out[:rows, :] = got_ref[:, pl.ds(at, width)]
                out[rows:, :] = own[bits, :, start : start + width]


def prepare(place, slab, got, zs, chunks):
    rows, half = got.shape
    vmem = pl.BlockSpec(memory_space=pltpu.VMEM)
    outs = [jax.ShapeDtypeStruct((2 * rows, width), jnp.float32) for _, width in chunks for _ in range(zs)]
    outs = pl.pallas_call(
        functools.partial(prepare_kernel, chunks),
        out_shape=outs,
        in_specs=[pl.BlockSpec(memory_space=pltpu.SMEM), pl.BlockSpec(memory_space=pl.ANY), vmem],
        out_specs=[vmem] * len(outs),
        scratch_shapes=[pltpu.VMEM((zs, rows, half // zs), jnp.float32), pltpu.SemaphoreType.DMA((zs,))],
        compiler_params=pltpu.CompilerParams(vmem_limit_bytes=40 * 2**20),
        name="prepare",
    )(place, slab, got)
    return [outs[c * zs : (c + 1) * zs] for c in range(len(chunks))]


def split(x):
    high = x.astype(jnp.bfloat16)
    return high, (x - high.astype(jnp.float32)).astype(jnp.bfloat16)


def layout(n):
    places, at, strip = [], 0, n % 128
    for j in range(n // 128):
        places.append((at, 128 * (j + 1), at + 128 * (j + 1)))
        at += 128 * (j + 1) + strip
    return places, at, at + strip


def pack_kernel(zs, place_ref, gram_ref, *refs):
    blocks, (mine_ref, theirs_ref, whole_ref, packed) = refs[:zs], refs[zs:]
    n = whole_ref.shape[0]
    deep = n // zs
    z, core = place_ref[0], place_ref[1]
    for bits in range(zs):
        whole_ref[pl.ds(pl.multiple_of((z ^ bits) * deep, 8), deep), :] = blocks[bits][...]
    places, corner, size = layout(n)
    edge = n // 128 * 128
    high, low = split(whole_ref[...])

    def block(r0, r1, c0, c1):
        def times(a, b):
            return lax.dot_general(a, b, (((1,), (1,)), ((), ())), preferred_element_type=jnp.float32)

        total = times(high[r0:r1], low[c0:c1]) + times(low[r0:r1], high[c0:c1]) + times(high[r0:r1], high[c0:c1])
        return total + gram_ref[r0:r1, c0:c1]

    for start in range(0, edge, 256):
        stop = min(start + 256, edge)
        upper = block(0, stop, start, stop)
        for j in range(start // 128, stop // 128):
            at, rows, _ = places[j]
            packed[at : at + rows, :] = upper[:rows, 128 * j - start : 128 * j - start + 128]
    if n > edge:
        strip = block(edge, n, 0, n)
        for j, (_, _, at) in enumerate(places):
            packed[at : at + n - edge, :] = strip[:, 128 * j : 128 * j + 128]
        packed[corner:size, :] = jnp.pad(strip[:, edge:], ((0, 0), (0, 128 - (n - edge))))
    half = size // 2
    mine_ref[...] = packed[pl.ds(pl.multiple_of(core * half, 8), half), :]
    theirs_ref[...] = packed[pl.ds(pl.multiple_of((1 - core) * half, 8), half), :]


def pack(place, gram, blocks):
    n = gram.shape[0]
    size = layout(n)[2]
    half = jax.ShapeDtypeStruct((size // 2, 128), jnp.float32)
    vmem = pl.BlockSpec(memory_space=pltpu.VMEM)
    return pl.pallas_call(
        functools.partial(pack_kernel, len(blocks)),
        out_shape=(half, half, jax.ShapeDtypeStruct((n, blocks[0].shape[1]), jnp.float32)),
        in_specs=[pl.BlockSpec(memory_space=pltpu.SMEM)] + [vmem] * (1 + len(blocks)),
        out_specs=[vmem] * 3,
        scratch_shapes=[pltpu.VMEM((size, 128), jnp.float32)],
        compiler_params=pltpu.CompilerParams(vmem_limit_bytes=32 * 2**20),
        name="gram_pack",
    )(place, gram, *blocks)


def lower_inverse(small):
    n = small.shape[0]
    lanes = 128
    full = (8, lanes)
    col = lax.broadcasted_iota(jnp.int32, full, 1)
    row = lax.broadcasted_iota(jnp.int32, full, 0)
    left = [small[8 * i : 8 * i + 8, :] for i in range(n // 8)]
    right = [(col == row + 8 * i).astype(jnp.float32) for i in range(n // 8)]
    done = []
    for p in range(n // 8):
        at = 8 * p
        d = {(a, b): jnp.broadcast_to(left[p][a : a + 1, at + b : at + b + 1], full) for a in range(8) for b in range(a + 1)}
        low, inv_diag = {}, []
        for b in range(8):
            r = lax.rsqrt(d[b, b])
            inv_diag.append(r)
            for a in range(b + 1, 8):
                low[a, b] = d[a, b] * r
            for a in range(b + 1, 8):
                for c in range(b + 1, a + 1):
                    d[a, c] = d[a, c] - low[a, b] * low[c, b]
        inv = {}
        for b in range(8):
            inv[b, b] = inv_diag[b]
            for a in range(b + 1, 8):
                s = low[a, b] * inv[b, b]
                for k in range(b + 1, a):
                    s = s + low[a, k] * inv[k, b]
                inv[a, b] = -s * inv_diag[a]
        lrow = [jnp.broadcast_to(left[p][k : k + 1, :], full) for k in range(8)]
        rrow = [jnp.broadcast_to(right[p][k : k + 1, :], full) for k in range(8)]
        y, v = [], []
        for m in range(8):
            ym, vm = inv[m, 0] * lrow[0], inv[m, 0] * rrow[0]
            for k in range(1, m + 1):
                ym, vm = ym + inv[m, k] * lrow[k], vm + inv[m, k] * rrow[k]
            y.append(ym)
            v.append(vm)
        out = v[0]
        for m in range(1, 8):
            out = jnp.where(row == m, v[m], out)
        done.append(out)
        for i in range(p + 1, n // 8):
            c = [jnp.broadcast_to(left[i][:, at + k : at + k + 1], full) for k in range(8)]
            li, ri = left[i], right[i]
            for m in range(8):
                f = inv[m, 0] * c[0]
                for k in range(1, m + 1):
                    f = f + inv[m, k] * c[k]
                li = li - f * y[m]
                ri = ri - f * v[m]
            left[i], right[i] = li, ri
    return jnp.concatenate(done, 0)


def iterations_kernel(iters, place_ref, mine_ref, other_ref, start_ref, factor_ref, packed, gram):
    def times(a, b, dims):
        return lax.dot_general(a, b, (dims, ((), ())), precision=HIGHEST, preferred_element_type=jnp.float32)

    n = gram.shape[0]
    places, corner, size = layout(n)
    edge = n // 128 * 128
    half = size // 2
    core = place_ref[1]
    packed[pl.ds(pl.multiple_of(core * half, 8), half), :] = mine_ref[...]
    packed[pl.ds(pl.multiple_of((1 - core) * half, 8), half), :] = other_ref[...]
    for j, (at, rows, strip) in enumerate(places):
        cols = slice(128 * j, 128 * j + 128)
        gram[:rows, cols] = packed[at : at + rows, :]
        for i in range(j):
            gram[cols, 128 * i : 128 * i + 128] = packed[at + 128 * i : at + 128 * i + 128, :].T
        if n > edge:
            gram[edge:, cols] = packed[strip : strip + n - edge, :]
            gram[cols, edge:] = packed[strip : strip + n - edge, :].T
    if n > edge:
        gram[edge:, edge:] = packed[corner:size, : n - edge]

    image = times(gram[...], start_ref[...], ((1,), (0,)))
    for step in range(iters):
        small = times(image, image, ((0,), (0,)))
        inverse = lower_inverse(jnp.pad(small, ((0, 0), (0, 128 - small.shape[1]))))[:, : small.shape[1]]
        if step < iters - 1:
            image = times(times(gram[...], image, ((1,), (0,))), inverse, ((1,), (1,)))
        else:
            factor_ref[...] = times(image, inverse, ((1,), (1,)))


def iterations(place, mine, other, start, iters):
    n = start.shape[0]
    return pl.pallas_call(
        functools.partial(iterations_kernel, iters),
        out_shape=jax.ShapeDtypeStruct(start.shape, jnp.float32),
        in_specs=[pl.BlockSpec(memory_space=pltpu.SMEM)] + [pl.BlockSpec(memory_space=pltpu.VMEM)] * 3,
        out_specs=pl.BlockSpec(memory_space=pltpu.VMEM),
        scratch_shapes=[pltpu.VMEM((layout(n)[2], 128), jnp.float32), pltpu.VMEM((n, n), jnp.float32)],
        compiler_params=pltpu.CompilerParams(vmem_limit_bytes=32 * 2**20),
        name="iterations",
    )(place, mine, other, start)


def sum_everywhere(mine, theirs, fibre, rest):
    r = lax.axis_index("rest")
    half, width = mine.shape
    piece = -(-half // (8 * rest)) * 8
    mine = mine + swap(theirs, "fibre", fibre, 1)
    mine = jnp.pad(mine, ((0, piece * rest - half), (0, 0)))
    total = lax.dynamic_slice(mine, (r * piece, 0), (piece, width))
    for bits in range(1, rest):
        part = lax.dynamic_slice(mine, ((r ^ bits) * piece, 0), (piece, width))
        total = total + swap(part, "rest", rest, bits)
    terms = [total] + [swap(total, "fibre", fibre, 2 * bits) for bits in range(1, fibre // 2)]
    while len(terms) > 1:
        terms = [terms[i] + terms[i + 1] for i in range(0, len(terms), 2)]
    total = terms[0]
    out = jnp.zeros((rest, piece, width), jnp.float32)
    for bits in range(rest):
        got = swap(total, "rest", rest, bits) if bits else total
        out = lax.dynamic_update_slice(out, got[None], (r ^ bits, 0, 0))
    out = out.reshape(rest * piece, width)[:half]
    return out, swap(out, "fibre", fibre, 1)


def assemble_kernel(place_ref, *refs):
    blocks, (mine_ref, theirs_ref) = refs[:-2], refs[-2:]
    z, core = place_ref[0], place_ref[1]
    own, part = mine_ref.shape[0], blocks[0].shape[1]
    for bits, block in enumerate(blocks):
        at = pl.multiple_of((z ^ bits) * part, 128)
        first, last = block[:own, :], block[own:, :]
        mine_ref[:, pl.ds(at, part)] = jnp.where(core == 0, first, last)
        theirs_ref[:, pl.ds(at, part)] = jnp.where(core == 0, last, first)


def assemble(place, blocks):
    two_own, part = blocks[0].shape
    vmem = pl.BlockSpec(memory_space=pltpu.VMEM)
    half = jax.ShapeDtypeStruct((two_own // 2, part * len(blocks)), jnp.float32)
    return pl.pallas_call(
        assemble_kernel,
        out_shape=(half, half),
        in_specs=[pl.BlockSpec(memory_space=pltpu.SMEM)] + [vmem] * len(blocks),
        out_specs=[vmem] * 2,
        compiler_params=pltpu.CompilerParams(vmem_limit_bytes=32 * 2**20),
        name="assemble",
    )(place, *blocks)


def shards(fibre, rest, slab, start_basis):
    rows, cols = slab.shape
    zs = fibre // 2
    f = lax.axis_index("fibre")
    z, core = f // 2, f % 2
    place = jnp.stack([z, core])
    half = cols // 2
    part = half // zs
    chunks = [(0, part * 3 // 4), (part * 3 // 4, part // 4)]
    n = zs * 2 * rows
    theirs = lax.dynamic_slice(slab, (0, (1 - core) * half), (rows, half))
    early, late = prepare(place, slab, swap(theirs, "fibre", fibre, 1), zs, chunks)
    arrived = [early[0]] + [swap(early[bits], "fibre", fibre, 2 * bits) for bits in range(1, zs)]
    last = [late[0]]
    for bits in range(1, zs):
        gate = bits if 2 * bits < zs else zs - 1
        block, arrived[gate] = lax.optimization_barrier((late[bits], arrived[gate]))
        last.append(swap(block, "fibre", fibre, 2 * bits))
    whole = jnp.zeros((zs, 2 * rows, chunks[0][1]), jnp.float32)
    for bits in range(zs):
        whole = lax.dynamic_update_slice(whole, arrived[bits][None], (z ^ bits, 0, 0))
    whole = whole.reshape(n, chunks[0][1])
    gram = jnp.dot(whole, whole.T, precision=HIGH, preferred_element_type=jnp.float32)
    mine, theirs, end = pack(place, gram, last)
    mine, other = sum_everywhere(mine, theirs, fibre, rest)
    basis = iterations(place, mine, other, start_basis, ITERS)
    own = basis.shape[1] // fibre
    rows_of = [lax.dynamic_slice(basis.T, ((z ^ bits) * 2 * own, 0), (2 * own, n)) for bits in range(zs)]
    rows_of = jnp.concatenate(rows_of, 0)
    share = [jnp.dot(rows_of, columns, precision=HIGH, preferred_element_type=jnp.float32) for columns in (whole, end)]
    share = jnp.concatenate(share, 1)
    blocks = [share[2 * own * bits : 2 * own * (bits + 1)] for bits in range(zs)]
    blocks = blocks[:1] + [swap(blocks[bits], "fibre", fibre, 2 * bits) for bits in range(1, zs)]
    mine, theirs = assemble(place, blocks)
    return (basis, in_order(core, mine, swap(theirs, "fibre", fibre, 1), 1))


def solution(mesh):
    fibre, rest = mesh.shape["fibre"], mesh.shape["rest"]
    return jax.shard_map(
        lambda slab, start_basis: shards(fibre, rest, slab, start_basis),
        mesh=mesh,
        in_specs=(P("fibre", "rest"), P()),
        out_specs=(P(), P("fibre", "rest")),
        check_vma=False,
    )
```

```python
import functools

import jax
import jax.numpy as jnp
from jax import lax
from jax.experimental import pallas as pl
from jax.experimental.pallas import tpu as pltpu
from jax.sharding import PartitionSpec as P

ITERS = 3
HIGH = lax.Precision.HIGH
HIGHEST = lax.Precision.HIGHEST


def swap(x, axis, size, bits):
    return lax.ppermute(x, axis, [(i, i ^ bits) for i in range(size)])


def in_order(core, mine, other, axis):
    return jnp.where(core == 0, jnp.concatenate([mine, other], axis), jnp.concatenate([other, mine], axis))


def prepare_kernel(pieces, place_ref, slab_ref, got_ref, *refs):
    distances = sorted({bits for bits, _, _ in pieces}, reverse=True)
    outs, (own, sems) = refs[:-2], refs[-2:]
    zs, rows, part = own.shape
    z, core = place_ref[0], place_ref[1]

    def fetch(bits):
        at = pl.multiple_of(core * (zs * part) + (z ^ bits) * part, 128)
        return pltpu.make_async_copy(slab_ref.at[:, pl.ds(at, part)], own.at[bits], sems.at[bits])

    for bits in distances:
        fetch(bits).start()
    for order, bits in enumerate(distances):
        fetch(bits).wait()
        for out, (which, start, width) in zip(outs, pieces):
            if which != bits:
                continue
            columns = slice(start, start + width)
            other = slice(order * part + start, order * part + start + width)

            @pl.when(core == 0)
            def _():
                out[:rows, :] = own[bits, :, columns]
                out[rows:, :] = got_ref[:, other]

            @pl.when(core == 1)
            def _():
                out[:rows, :] = got_ref[:, other]
                out[rows:, :] = own[bits, :, columns]


def prepare(place, slab, got, zs, pieces):
    rows, part = got.shape[0], got.shape[1] // (zs - 1)
    vmem = pl.BlockSpec(memory_space=pltpu.VMEM)
    return pl.pallas_call(
        functools.partial(prepare_kernel, pieces),
        out_shape=[jax.ShapeDtypeStruct((2 * rows, width), jnp.float32) for _, _, width in pieces],
        in_specs=[pl.BlockSpec(memory_space=pltpu.SMEM), pl.BlockSpec(memory_space=pl.ANY), vmem],
        out_specs=[vmem] * len(pieces),
        scratch_shapes=[pltpu.VMEM((zs, rows, part), jnp.float32), pltpu.SemaphoreType.DMA((zs,))],
        compiler_params=pltpu.CompilerParams(vmem_limit_bytes=32 * 2**20),
        cost_estimate=pl.CostEstimate(flops=0, bytes_accessed=100_000_000, transcendentals=0),
        name="prepare",
    )(place, slab, got)


def split(x):
    high = x.astype(jnp.bfloat16)
    return high, (x - high.astype(jnp.float32)).astype(jnp.bfloat16)


def layout(n):
    places, at, strip = [], 0, n % 128
    for j in range(n // 128):
        places.append((at, 128 * (j + 1), at + 128 * (j + 1)))
        at += 128 * (j + 1) + strip
    return places, at, at + strip


def add_gram(starts, width, place_ref, blocks, whole, high_ref, low_ref, packed, base_ref):
    zs = len(blocks)
    n = whole.shape[0]
    deep = n // zs
    z = place_ref[0]
    for bits, (block, start) in enumerate(zip(blocks, starts)):
        if deep % 8 == 0:
            whole[pl.ds(pl.multiple_of((z ^ bits) * deep, 8), deep), :] = block[:, start : start + width]
            continue
        for here in range(zs):

            @pl.when(z == here)
            def _():
                at = (here ^ bits) * deep
                whole[at : at + deep, :] = block[:, start : start + width]

    places, corner, size = layout(n)
    edge = n // 128 * 128
    high_ref[...], low_ref[...] = split(whole[...])

    def product(r0, r1, c0, c1):
        def times(a, b):
            return lax.dot_general(a[r0:r1, :], b[c0:c1, :], (((1,), (1,)), ((), ())), preferred_element_type=jnp.float32)

        return times(high_ref, low_ref) + times(low_ref, high_ref) + times(high_ref, high_ref)

    def put(at, value):
        rows = slice(at, at + value.shape[0])
        packed[rows, :] = value if base_ref is None else value + base_ref[rows, :]

    for start in range(0, edge, 256):
        stop = min(start + 256, edge)
        upper = product(0, stop, start, stop)
        for j in range(start // 128, stop // 128):
            at, rows, _ = places[j]
            put(at, upper[:rows, 128 * j - start : 128 * j - start + 128])
    if n > edge:
        strip = product(edge, n, 0, n)
        for j, (_, _, at) in enumerate(places):
            put(at, strip[:, 128 * j : 128 * j + 128])
        put(corner, jnp.pad(strip[:, edge:], ((0, 0), (0, 128 - (n - edge)))))


def early_kernel(starts, width, place_ref, *refs):
    blocks, (packed, high_ref, low_ref, whole) = refs[: len(starts)], refs[len(starts) :]
    add_gram(starts, width, place_ref, blocks, whole, high_ref, low_ref, packed, None)


def late_kernel(starts, width, place_ref, base_ref, *refs):
    blocks, (mine_ref, theirs_ref, high_ref, low_ref, whole, packed) = refs[: len(starts)], refs[len(starts) :]
    add_gram(starts, width, place_ref, blocks, whole, high_ref, low_ref, packed, base_ref)
    half = mine_ref.shape[0]
    core = place_ref[1]
    mine_ref[...] = packed[pl.ds(pl.multiple_of(core * half, 8), half), :]
    theirs_ref[...] = packed[pl.ds(pl.multiple_of((1 - core) * half, 8), half), :]


def gram_part(place, base, blocks, starts, width):
    n = blocks[0].shape[0] * len(blocks)
    size = layout(n)[2]
    vmem = pl.BlockSpec(memory_space=pltpu.VMEM)
    parts = [jax.ShapeDtypeStruct((n, width), jnp.bfloat16)] * 2
    packed = (size, 128)
    whole = pltpu.VMEM((n, width), jnp.float32)
    if base is None:
        kernel, sums, scratch, first = early_kernel, [jax.ShapeDtypeStruct(packed, jnp.float32)], [whole], []
    else:
        half = jax.ShapeDtypeStruct((size // 2, 128), jnp.float32)
        kernel, sums, scratch, first = late_kernel, [half, half], [whole, pltpu.VMEM(packed, jnp.float32)], [base]
    return pl.pallas_call(
        functools.partial(kernel, starts, width),
        out_shape=[*sums, *parts],
        in_specs=[pl.BlockSpec(memory_space=pltpu.SMEM)] + [vmem] * (len(first) + len(blocks)),
        out_specs=[vmem] * (len(sums) + 2),
        scratch_shapes=scratch,
        compiler_params=pltpu.CompilerParams(vmem_limit_bytes=40 * 2**20),
        cost_estimate=pl.CostEstimate(flops=6 * n * n * width, bytes_accessed=8 * n * width, transcendentals=0),
        name="gram_early" if base is None else "gram_late",
    )(place, *first, *blocks)


def lower_inverse(small):
    n = small.shape[0]
    lanes = 128
    full = (8, lanes)
    col = lax.broadcasted_iota(jnp.int32, full, 1)
    row = lax.broadcasted_iota(jnp.int32, full, 0)
    left = [small[8 * i : 8 * i + 8, :] for i in range(n // 8)]
    right = [(col == row + 8 * i).astype(jnp.float32) for i in range(n // 8)]
    done = []
    for p in range(n // 8):
        at = 8 * p
        d = {(a, b): jnp.broadcast_to(left[p][a : a + 1, at + b : at + b + 1], full) for a in range(8) for b in range(a + 1)}
        low, inv_diag = {}, []
        for b in range(8):
            r = lax.rsqrt(d[b, b])
            inv_diag.append(r)
            for a in range(b + 1, 8):
                low[a, b] = d[a, b] * r
            for a in range(b + 1, 8):
                for c in range(b + 1, a + 1):
                    d[a, c] = d[a, c] - low[a, b] * low[c, b]
        inv = {}
        for b in range(8):
            inv[b, b] = inv_diag[b]
            for a in range(b + 1, 8):
                s = low[a, b] * inv[b, b]
                for k in range(b + 1, a):
                    s = s + low[a, k] * inv[k, b]
                inv[a, b] = -s * inv_diag[a]
        lrow = [jnp.broadcast_to(left[p][k : k + 1, :], full) for k in range(8)]
        rrow = [jnp.broadcast_to(right[p][k : k + 1, :], full) for k in range(8)]
        y, v = [], []
        for m in range(8):
            ym, vm = inv[m, 0] * lrow[0], inv[m, 0] * rrow[0]
            for k in range(1, m + 1):
                ym, vm = ym + inv[m, k] * lrow[k], vm + inv[m, k] * rrow[k]
            y.append(ym)
            v.append(vm)
        out = v[0]
        for m in range(1, 8):
            out = jnp.where(row == m, v[m], out)
        done.append(out)
        for i in range(p + 1, n // 8):
            c = [jnp.broadcast_to(left[i][:, at + k : at + k + 1], full) for k in range(8)]
            li, ri = left[i], right[i]
            for m in range(8):
                f = inv[m, 0] * c[0]
                for k in range(1, m + 1):
                    f = f + inv[m, k] * c[k]
                li = li - f * y[m]
                ri = ri - f * v[m]
            left[i], right[i] = li, ri
    return jnp.concatenate(done, 0)


def iterations_kernel(iters, place_ref, mine_ref, other_ref, start_ref, factor_ref, packed, gram):
    def times(a, b, dims):
        return lax.dot_general(a, b, (dims, ((), ())), precision=HIGHEST, preferred_element_type=jnp.float32)

    n = gram.shape[0]
    places, corner, size = layout(n)
    edge = n // 128 * 128
    half = size // 2
    core = place_ref[1]
    packed[pl.ds(pl.multiple_of(core * half, 8), half), :] = mine_ref[...]
    packed[pl.ds(pl.multiple_of((1 - core) * half, 8), half), :] = other_ref[...]
    for j, (at, rows, strip) in enumerate(places):
        cols = slice(128 * j, 128 * j + 128)
        gram[:rows, cols] = packed[at : at + rows, :]
        for i in range(j):
            gram[cols, 128 * i : 128 * i + 128] = packed[at + 128 * i : at + 128 * i + 128, :].T
        if n > edge:
            gram[edge:, cols] = packed[strip : strip + n - edge, :]
            gram[cols, edge:] = packed[strip : strip + n - edge, :].T
    if n > edge:
        gram[edge:, edge:] = packed[corner:size, : n - edge]

    image = times(gram[...], start_ref[...], ((1,), (0,)))
    for step in range(iters):
        small = times(image, image, ((0,), (0,)))
        inverse = lower_inverse(jnp.pad(small, ((0, 0), (0, 128 - small.shape[1]))))[:, : small.shape[1]]
        if step < iters - 1:
            image = times(times(gram[...], image, ((1,), (0,))), inverse, ((1,), (1,)))
        else:
            factor_ref[...] = times(image, inverse, ((1,), (1,)))


def iterations(place, mine, other, start, iters):
    n = start.shape[0]
    return pl.pallas_call(
        functools.partial(iterations_kernel, iters),
        out_shape=jax.ShapeDtypeStruct(start.shape, jnp.float32),
        in_specs=[pl.BlockSpec(memory_space=pltpu.SMEM)] + [pl.BlockSpec(memory_space=pltpu.VMEM)] * 3,
        out_specs=pl.BlockSpec(memory_space=pltpu.VMEM),
        scratch_shapes=[pltpu.VMEM((layout(n)[2], 128), jnp.float32), pltpu.VMEM((n, n), jnp.float32)],
        compiler_params=pltpu.CompilerParams(vmem_limit_bytes=32 * 2**20),
        name="iterations",
    )(place, mine, other, start)


def sum_everywhere(mine, theirs, fibre, rest):
    r = lax.axis_index("rest")
    half, width = mine.shape
    piece = -(-half // (8 * rest)) * 8
    mine = mine + swap(theirs, "fibre", fibre, 1)
    mine = jnp.pad(mine, ((0, piece * rest - half), (0, 0)))
    total = lax.dynamic_slice(mine, (r * piece, 0), (piece, width))
    for bits in range(1, rest):
        part = lax.dynamic_slice(mine, ((r ^ bits) * piece, 0), (piece, width))
        total = total + swap(part, "rest", rest, bits)
    terms = [total] + [swap(total, "fibre", fibre, 2 * bits) for bits in range(1, fibre // 2)]
    while len(terms) > 1:
        terms = [terms[i] + terms[i + 1] for i in range(0, len(terms), 2)]
    total = terms[0]
    out = jnp.zeros((rest, piece, width), jnp.float32)
    for bits in range(rest):
        got = swap(total, "rest", rest, bits) if bits else total
        out = lax.dynamic_update_slice(out, got[None], (r ^ bits, 0, 0))
    out = out.reshape(rest * piece, width)[:half]
    return out, swap(out, "fibre", fibre, 1)


def core_kernel(place_ref, basis_ref, *refs):
    parts, outs, share = refs[:4], refs[4:-1], refs[-1]
    zs = len(outs)
    two_own = share.shape[0] // zs
    high, low = split(basis_ref[...])

    def times(a, b):
        return lax.dot_general(a, b[...], (((0,), (0,)), ((), ())), preferred_element_type=jnp.float32)

    at = 0
    for first, second in (parts[:2], parts[2:]):
        width = first.shape[1]
        share[:, at : at + width] = times(high, second) + times(low, first) + times(high, first)
        at += width
    for here in range(zs):

        @pl.when(place_ref[0] == here)
        def _():
            for bits, out in enumerate(outs):
                out[...] = share[two_own * (here ^ bits) : two_own * (here ^ bits) + two_own, :]


def core_parts(place, basis, parts, zs):
    rank = basis.shape[1]
    part = parts[0].shape[1] + parts[2].shape[1]
    vmem = pl.BlockSpec(memory_space=pltpu.VMEM)
    return pl.pallas_call(
        core_kernel,
        out_shape=[jax.ShapeDtypeStruct((rank // zs, part), jnp.float32)] * zs,
        in_specs=[pl.BlockSpec(memory_space=pltpu.SMEM)] + [vmem] * 5,
        out_specs=[vmem] * zs,
        scratch_shapes=[pltpu.VMEM((rank, part), jnp.float32)],
        compiler_params=pltpu.CompilerParams(vmem_limit_bytes=32 * 2**20),
        name="core_parts",
    )(place, basis, *parts)


def assemble_kernel(place_ref, *refs):
    blocks, (mine_ref, theirs_ref) = refs[:-2], refs[-2:]
    z, core = place_ref[0], place_ref[1]
    own, part = mine_ref.shape[0], blocks[0].shape[1]
    for bits, block in enumerate(blocks):
        at = pl.multiple_of((z ^ bits) * part, 128)
        first, last = block[:own, :], block[own:, :]
        mine_ref[:, pl.ds(at, part)] = jnp.where(core == 0, first, last)
        theirs_ref[:, pl.ds(at, part)] = jnp.where(core == 0, last, first)


def assemble(place, blocks):
    two_own, part = blocks[0].shape
    vmem = pl.BlockSpec(memory_space=pltpu.VMEM)
    half = jax.ShapeDtypeStruct((two_own // 2, part * len(blocks)), jnp.float32)
    return pl.pallas_call(
        assemble_kernel,
        out_shape=(half, half),
        in_specs=[pl.BlockSpec(memory_space=pltpu.SMEM)] + [vmem] * len(blocks),
        out_specs=[vmem] * 2,
        compiler_params=pltpu.CompilerParams(vmem_limit_bytes=32 * 2**20),
        name="assemble",
    )(place, *blocks)


def shards(fibre, rest, slab, start_basis):
    rows, cols = slab.shape
    zs = fibre // 2
    f = lax.axis_index("fibre")
    z, core = f // 2, f % 2
    place = jnp.stack([z, core])
    half = cols // 2
    part = half // zs
    early = part * 3 // 4

    def cut(slab, whose, bits):
        return lax.dynamic_slice(slab, (0, whose * half + (z ^ bits) * part), (rows, part))

    far = zs - 1
    got = swap(cut(slab, 1 - core, far), "fibre", fibre, 1)
    block = in_order(core, cut(slab, core, far), got, 0)
    slab, block = lax.optimization_barrier((slab, block))
    arrived = {far: swap(block, "fibre", fibre, 2 * far)}
    others = list(range(far - 1, -1, -1))
    theirs = jnp.concatenate([cut(slab, 1 - core, bits) for bits in others], 1)
    got = swap(theirs, "fibre", fibre, 1)
    pieces = []
    for bits in others:
        pieces += [(bits, 0, early), (bits, early, part - early)] if bits > 1 else [(bits, 0, part)]
    late = {}
    for (bits, start, _), block in zip(pieces, prepare(place, slab, got, zs, pieces)):
        if start:
            block, arrived[far] = lax.optimization_barrier((block, arrived[far]))
        into = late if start else arrived
        into[bits] = swap(block, "fibre", fibre, 2 * bits) if bits else block
    first = [arrived[bits] for bits in range(zs)]
    last = [late.get(bits, arrived[bits]) for bits in range(zs)]
    last_from = tuple(0 if bits in late else early for bits in range(zs))
    packed, *parts = gram_part(place, None, first, (0,) * zs, early)
    mine, theirs, *more = gram_part(place, packed, last, last_from, part - early)
    mine, other = sum_everywhere(mine, theirs, fibre, rest)
    basis = iterations(place, mine, other, start_basis, ITERS)
    blocks = core_parts(place, basis, [*parts, *more], zs)
    blocks = [blocks[0]] + [swap(blocks[bits], "fibre", fibre, 2 * bits) for bits in range(1, zs)]
    mine, theirs = assemble(place, blocks)
    return (basis, in_order(core, mine, swap(theirs, "fibre", fibre, 1), 1))


def solution(mesh):
    fibre, rest = mesh.shape["fibre"], mesh.shape["rest"]
    return jax.shard_map(
        lambda slab, start_basis: shards(fibre, rest, slab, start_basis),
        mesh=mesh,
        in_specs=(P("fibre", "rest"), P()),
        out_specs=(P(), P("fibre", "rest")),
        check_vma=False,
    )
```

```python
import functools

import jax
import jax.numpy as jnp
from jax import lax
from jax.experimental import pallas as pl
from jax.experimental.pallas import tpu as pltpu
from jax.sharding import PartitionSpec as P

ITERS = 3
HIGH = lax.Precision.HIGH
HIGHEST = lax.Precision.HIGHEST


def swap(x, axis, size, bits):
    return lax.ppermute(x, axis, [(i, i ^ bits) for i in range(size)])


def in_order(core, mine, other, axis):
    return jnp.where(core == 0, jnp.concatenate([mine, other], axis), jnp.concatenate([other, mine], axis))


def prepare_kernel(cuts, pieces, place_ref, slab_ref, got_ref, *refs):
    outs, (own, sems) = refs[:-2], refs[-2:]
    zs, rows, part = own.shape
    z, core = place_ref[0], place_ref[1]

    def fetch(bits):
        at = pl.multiple_of(core * (zs * part) + (z ^ bits) * part, 128)
        return pltpu.make_async_copy(slab_ref.at[:, pl.ds(at, part)], own.at[bits], sems.at[bits])

    for bits, _, _ in cuts:
        fetch(bits).start()
    begin = 0
    for bits, from_, depth in cuts:
        fetch(bits).wait()
        for out, (which, start, width) in zip(outs, pieces):
            if which != bits:
                continue
            columns = slice(start, start + width)
            other = slice(begin + start - from_, begin + start - from_ + width)

            @pl.when(core == 0)
            def _():
                out[:rows, :] = own[bits, :, columns]
                out[rows:, :] = got_ref[:, other]

            @pl.when(core == 1)
            def _():
                out[:rows, :] = got_ref[:, other]
                out[rows:, :] = own[bits, :, columns]

        begin += depth


def prepare(place, slab, got, part, zs, cuts, pieces):
    rows = got.shape[0]
    vmem = pl.BlockSpec(memory_space=pltpu.VMEM)
    return pl.pallas_call(
        functools.partial(prepare_kernel, cuts, pieces),
        out_shape=[jax.ShapeDtypeStruct((2 * rows, width), jnp.float32) for _, _, width in pieces],
        in_specs=[pl.BlockSpec(memory_space=pltpu.SMEM), pl.BlockSpec(memory_space=pl.ANY), vmem],
        out_specs=[vmem] * len(pieces),
        scratch_shapes=[pltpu.VMEM((zs, rows, part), jnp.float32), pltpu.SemaphoreType.DMA((zs,))],
        compiler_params=pltpu.CompilerParams(vmem_limit_bytes=24 * 2**20),
        cost_estimate=pl.CostEstimate(flops=0, bytes_accessed=100_000_000, transcendentals=0),
        name="prepare",
    )(place, slab, got)


def split(x):
    high = x.astype(jnp.bfloat16)
    return high, (x - high.astype(jnp.float32)).astype(jnp.bfloat16)


def layout(n):
    places, at, strip = [], 0, n % 128
    for j in range(n // 128):
        places.append((at, 128 * (j + 1), at + 128 * (j + 1)))
        at += 128 * (j + 1) + strip
    return places, at, at + strip


def add_gram(starts, width, place_ref, blocks, whole, high_ref, low_ref, packed, base_ref):
    zs = len(blocks)
    n = whole.shape[0]
    deep = n // zs
    z = place_ref[0]
    for bits, (block, start) in enumerate(zip(blocks, starts)):
        if deep % 8 == 0:
            whole[pl.ds(pl.multiple_of((z ^ bits) * deep, 8), deep), :] = block[:, start : start + width]
            continue
        for here in range(zs):

            @pl.when(z == here)
            def _():
                at = (here ^ bits) * deep
                whole[at : at + deep, :] = block[:, start : start + width]

    places, corner, size = layout(n)
    edge = n // 128 * 128
    high_ref[...], low_ref[...] = split(whole[...])

    def product(r0, r1, c0, c1):
        def times(a, b):
            return lax.dot_general(a[r0:r1, :], b[c0:c1, :], (((1,), (1,)), ((), ())), preferred_element_type=jnp.float32)

        return times(high_ref, low_ref) + times(low_ref, high_ref) + times(high_ref, high_ref)

    def put(at, value):
        rows = slice(at, at + value.shape[0])
        packed[rows, :] = value if base_ref is None else value + base_ref[rows, :]

    for start in range(0, edge, 256):
        last = start + 256 >= edge
        stop = min(start + 256, edge)
        upper = product(0, n if last else stop, start, n if last else stop)
        for j in range(start // 128, stop // 128):
            at, rows, _ = places[j]
            put(at, upper[:rows, 128 * j - start : 128 * j - start + 128])
    if n > edge:
        strip = upper[:, edge - start :]
        for j, (_, _, at) in enumerate(places):
            put(at, strip[128 * j : 128 * j + 128].T)
        put(corner, jnp.pad(strip[edge:], ((0, 0), (0, 128 - (n - edge)))))


def early_kernel(starts, width, place_ref, *refs):
    blocks, (packed, high_ref, low_ref, whole) = refs[: len(starts)], refs[len(starts) :]
    add_gram(starts, width, place_ref, blocks, whole, high_ref, low_ref, packed, None)


def late_kernel(starts, width, place_ref, base_ref, *refs):
    blocks, (mine_ref, theirs_ref, high_ref, low_ref, whole, packed) = refs[: len(starts)], refs[len(starts) :]
    add_gram(starts, width, place_ref, blocks, whole, high_ref, low_ref, packed, base_ref)
    half = mine_ref.shape[0]
    core = place_ref[1]
    mine_ref[...] = packed[pl.ds(pl.multiple_of(core * half, 8), half), :]
    theirs_ref[...] = packed[pl.ds(pl.multiple_of((1 - core) * half, 8), half), :]


def gram_part(place, base, blocks, starts, width):
    n = blocks[0].shape[0] * len(blocks)
    size = layout(n)[2]
    vmem = pl.BlockSpec(memory_space=pltpu.VMEM)
    parts = [jax.ShapeDtypeStruct((n, width), jnp.bfloat16)] * 2
    packed = (size, 128)
    whole = pltpu.VMEM((n, width), jnp.float32)
    if base is None:
        kernel, sums, scratch, first = early_kernel, [jax.ShapeDtypeStruct(packed, jnp.float32)], [whole], []
    else:
        half = jax.ShapeDtypeStruct((size // 2, 128), jnp.float32)
        kernel, sums, scratch, first = late_kernel, [half, half], [whole, pltpu.VMEM(packed, jnp.float32)], [base]
    return pl.pallas_call(
        functools.partial(kernel, starts, width),
        out_shape=[*sums, *parts],
        in_specs=[pl.BlockSpec(memory_space=pltpu.SMEM)] + [vmem] * (len(first) + len(blocks)),
        out_specs=[vmem] * (len(sums) + 2),
        scratch_shapes=scratch,
        compiler_params=pltpu.CompilerParams(vmem_limit_bytes=24 * 2**20),
        cost_estimate=pl.CostEstimate(flops=6 * n * n * width, bytes_accessed=8 * n * width, transcendentals=0),
        name="gram_early" if base is None else "gram_late",
    )(place, *first, *blocks)


def lower_inverse(small):
    n = small.shape[0]
    lanes = 128
    full = (8, lanes)
    col = lax.broadcasted_iota(jnp.int32, full, 1)
    row = lax.broadcasted_iota(jnp.int32, full, 0)
    left = [small[8 * i : 8 * i + 8, :] for i in range(n // 8)]
    right = [(col == row + 8 * i).astype(jnp.float32) for i in range(n // 8)]
    done = []
    for p in range(n // 8):
        at = 8 * p
        d = {(a, b): jnp.broadcast_to(left[p][a : a + 1, at + b : at + b + 1], full) for a in range(8) for b in range(a + 1)}
        low, inv_diag = {}, []
        for b in range(8):
            r = lax.rsqrt(d[b, b])
            inv_diag.append(r)
            for a in range(b + 1, 8):
                low[a, b] = d[a, b] * r
            for a in range(b + 1, 8):
                for c in range(b + 1, a + 1):
                    d[a, c] = d[a, c] - low[a, b] * low[c, b]
        inv = {}
        for b in range(8):
            inv[b, b] = inv_diag[b]
            for a in range(b + 1, 8):
                s = low[a, b] * inv[b, b]
                for k in range(b + 1, a):
                    s = s + low[a, k] * inv[k, b]
                inv[a, b] = -s * inv_diag[a]
        lrow = [jnp.broadcast_to(left[p][k : k + 1, :], full) for k in range(8)]
        rrow = [jnp.broadcast_to(right[p][k : k + 1, :], full) for k in range(8)]
        y, v = [], []
        for m in range(8):
            ym, vm = inv[m, 0] * lrow[0], inv[m, 0] * rrow[0]
            for k in range(1, m + 1):
                ym, vm = ym + inv[m, k] * lrow[k], vm + inv[m, k] * rrow[k]
            y.append(ym)
            v.append(vm)
        out = v[0]
        for m in range(1, 8):
            out = jnp.where(row == m, v[m], out)
        done.append(out)
        for i in range(p + 1, n // 8):
            c = [jnp.broadcast_to(left[i][:, at + k : at + k + 1], full) for k in range(8)]
            li, ri = left[i], right[i]
            for m in range(8):
                f = inv[m, 0] * c[0]
                for k in range(1, m + 1):
                    f = f + inv[m, k] * c[k]
                li = li - f * y[m]
                ri = ri - f * v[m]
            left[i], right[i] = li, ri
    return jnp.concatenate(done, 0)


def iterations_kernel(iters, place_ref, mine_ref, other_ref, start_ref, factor_ref, packed, gram, high, low):
    def times(a, b, dims):
        return lax.dot_general(a, b, (dims, ((), ())), precision=HIGHEST, preferred_element_type=jnp.float32)

    n = gram.shape[0]
    places, corner, size = layout(n)
    edge = n // 128 * 128
    half = size // 2
    core = place_ref[1]
    packed[pl.ds(pl.multiple_of(core * half, 8), half), :] = mine_ref[...]
    packed[pl.ds(pl.multiple_of((1 - core) * half, 8), half), :] = other_ref[...]
    for j, (at, rows, strip) in enumerate(places):
        cols = slice(128 * j, 128 * j + 128)
        gram[:rows, cols] = packed[at : at + rows, :]
        for i in range(j):
            gram[cols, 128 * i : 128 * i + 128] = packed[at + 128 * i : at + 128 * i + 128, :].T
        if n > edge:
            gram[edge:, cols] = packed[strip : strip + n - edge, :]
            gram[cols, edge:] = packed[strip : strip + n - edge, :].T
    if n > edge:
        gram[edge:, edge:] = packed[corner:size, : n - edge]

    high[...], low[...] = split(gram[...])

    def apply_gram(x):
        x_high, x_low = split(x)

        def part(a, b):
            return lax.dot_general(a[...], b, (((1,), (0,)), ((), ())), preferred_element_type=jnp.float32)

        return part(high, x_low) + part(low, x_high) + part(high, x_high)

    image = apply_gram(start_ref[...])
    for step in range(iters):
        small = times(image, image, ((0,), (0,)))
        inverse = lower_inverse(jnp.pad(small, ((0, 0), (0, 128 - small.shape[1]))))[:, : small.shape[1]]
        if step < iters - 1:
            image = times(apply_gram(image), inverse, ((1,), (1,)))
        else:
            factor_ref[...] = times(image, inverse, ((1,), (1,)))


def iterations(place, mine, other, start, iters):
    n = start.shape[0]
    return pl.pallas_call(
        functools.partial(iterations_kernel, iters),
        out_shape=jax.ShapeDtypeStruct(start.shape, jnp.float32),
        in_specs=[pl.BlockSpec(memory_space=pltpu.SMEM)] + [pl.BlockSpec(memory_space=pltpu.VMEM)] * 3,
        out_specs=pl.BlockSpec(memory_space=pltpu.VMEM),
        scratch_shapes=[pltpu.VMEM((layout(n)[2], 128), jnp.float32), pltpu.VMEM((n, n), jnp.float32)] + [pltpu.VMEM((n, n), jnp.bfloat16)] * 2,
        compiler_params=pltpu.CompilerParams(vmem_limit_bytes=16 * 2**20),
        name="iterations",
    )(place, mine, other, start)


def sum_everywhere(mine, theirs, fibre, rest):
    r = lax.axis_index("rest")
    half, width = mine.shape
    piece = -(-half // (8 * rest)) * 8
    mine = mine + swap(theirs, "fibre", fibre, 1)
    mine = jnp.pad(mine, ((0, piece * rest - half), (0, 0)))
    total = lax.dynamic_slice(mine, (r * piece, 0), (piece, width))
    for bits in range(1, rest):
        part = lax.dynamic_slice(mine, ((r ^ bits) * piece, 0), (piece, width))
        total = total + swap(part, "rest", rest, bits)
    terms = [total] + [swap(total, "fibre", fibre, 2 * bits) for bits in range(1, fibre // 2)]
    while len(terms) > 1:
        terms = [terms[i] + terms[i + 1] for i in range(0, len(terms), 2)]
    total = terms[0]
    out = jnp.zeros((rest, piece, width), jnp.float32)
    for bits in range(rest):
        got = swap(total, "rest", rest, bits) if bits else total
        out = lax.dynamic_update_slice(out, got[None], (r ^ bits, 0, 0))
    out = out.reshape(rest * piece, width)[:half]
    return out, swap(out, "fibre", fibre, 1)


def core_kernel(place_ref, basis_ref, *refs):
    parts, outs, share = refs[:4], refs[4:-1], refs[-1]
    zs = len(outs)
    two_own = share.shape[0] // zs
    high, low = split(basis_ref[...])

    def times(a, b):
        return lax.dot_general(a, b[...], (((0,), (0,)), ((), ())), preferred_element_type=jnp.float32)

    at = 0
    for first, second in (parts[:2], parts[2:]):
        width = first.shape[1]
        share[:, at : at + width] = times(high, second) + times(low, first) + times(high, first)
        at += width
    for here in range(zs):

        @pl.when(place_ref[0] == here)
        def _():
            for bits, out in enumerate(outs):
                out[...] = share[two_own * (here ^ bits) : two_own * (here ^ bits) + two_own, :]


def core_parts(place, basis, parts, zs):
    rank = basis.shape[1]
    part = parts[0].shape[1] + parts[2].shape[1]
    vmem = pl.BlockSpec(memory_space=pltpu.VMEM)
    return pl.pallas_call(
        core_kernel,
        out_shape=[jax.ShapeDtypeStruct((rank // zs, part), jnp.float32)] * zs,
        in_specs=[pl.BlockSpec(memory_space=pltpu.SMEM)] + [vmem] * 5,
        out_specs=[vmem] * zs,
        scratch_shapes=[pltpu.VMEM((rank, part), jnp.float32)],
        compiler_params=pltpu.CompilerParams(vmem_limit_bytes=16 * 2**20),
        name="core_parts",
    )(place, basis, *parts)


def assemble_kernel(place_ref, *refs):
    blocks, (mine_ref, theirs_ref) = refs[:-2], refs[-2:]
    z, core = place_ref[0], place_ref[1]
    own, part = mine_ref.shape[0], blocks[0].shape[1]
    for bits, block in enumerate(blocks):
        at = pl.multiple_of((z ^ bits) * part, 128)
        first, last = block[:own, :], block[own:, :]
        mine_ref[:, pl.ds(at, part)] = jnp.where(core == 0, first, last)
        theirs_ref[:, pl.ds(at, part)] = jnp.where(core == 0, last, first)


def assemble(place, blocks):
    two_own, part = blocks[0].shape
    vmem = pl.BlockSpec(memory_space=pltpu.VMEM)
    half = jax.ShapeDtypeStruct((two_own // 2, part * len(blocks)), jnp.float32)
    return pl.pallas_call(
        assemble_kernel,
        out_shape=(half, half),
        in_specs=[pl.BlockSpec(memory_space=pltpu.SMEM)] + [vmem] * len(blocks),
        out_specs=[vmem] * 2,
        compiler_params=pltpu.CompilerParams(vmem_limit_bytes=16 * 2**20),
        name="assemble",
    )(place, *blocks)


def shards(fibre, rest, slab, start_basis):
    rows, cols = slab.shape
    zs = fibre // 2
    f = lax.axis_index("fibre")
    z, core = f // 2, f % 2
    place = jnp.stack([z, core])
    half = cols // 2
    part = half // zs
    early = part * 7 // 8

    def cut(slab, whose, bits, start, width):
        return lax.dynamic_slice(slab, (0, whose * half + (z ^ bits) * part + start), (rows, width))

    far = zs - 1
    got = swap(cut(slab, 1 - core, far, 0, part), "fibre", fibre, 1)
    block = in_order(core, cut(slab, core, far, 0, part), got, 0)
    slab, block = lax.optimization_barrier((slab, block))
    arrived = {far: swap(block, "fibre", fibre, 2 * far)}
    cuts = [(bits, 0, part) for bits in range(far - 1, -1, -1)]
    got = swap(jnp.concatenate([cut(slab, 1 - core, *c) for c in cuts], 1), "fibre", fibre, 1)
    pieces = []
    for bits, start, width in cuts:
        split_here = bits > 1
        pieces += [(bits, 0, early), (bits, early, part - early)] if split_here else [(bits, start, width)]
    late = {}
    for (bits, start, _), block in zip(pieces, prepare(place, slab, got, part, zs, cuts, pieces)):
        if start:
            block, arrived[bits] = lax.optimization_barrier((block, arrived[bits]))
        into = late if start else arrived
        into[bits] = swap(block, "fibre", fibre, 2 * bits) if bits else block
    first = [arrived[bits] for bits in range(zs)]
    last = [late.get(bits, arrived[bits]) for bits in range(zs)]
    last_from = tuple(0 if bits in late else early for bits in range(zs))
    packed, *parts = gram_part(place, None, first, (0,) * zs, early)
    mine, theirs, *more = gram_part(place, packed, last, last_from, part - early)
    mine, other = sum_everywhere(mine, theirs, fibre, rest)
    basis = iterations(place, mine, other, start_basis, ITERS)
    blocks = core_parts(place, basis, [*parts, *more], zs)
    blocks = [blocks[0]] + [swap(blocks[bits], "fibre", fibre, 2 * bits) for bits in range(1, zs)]
    mine, theirs = assemble(place, blocks)
    return (basis, in_order(core, mine, swap(theirs, "fibre", fibre, 1), 1))


def solution(mesh):
    fibre, rest = mesh.shape["fibre"], mesh.shape["rest"]
    return jax.shard_map(
        lambda slab, start_basis: shards(fibre, rest, slab, start_basis),
        mesh=mesh,
        in_specs=(P("fibre", "rest"), P()),
        out_specs=(P(), P("fibre", "rest")),
        check_vma=False,
    )
```

```python
import functools

import jax
import jax.numpy as jnp
from jax import lax
from jax.experimental import pallas as pl
from jax.experimental.pallas import tpu as pltpu
from jax.sharding import PartitionSpec as P

ITERS = 3
HIGH = lax.Precision.HIGH
HIGHEST = lax.Precision.HIGHEST


def swap(x, axis, size, bits):
    return lax.ppermute(x, axis, [(i, i ^ bits) for i in range(size)])


def in_order(core, mine, other, axis):
    return jnp.where(core == 0, jnp.concatenate([mine, other], axis), jnp.concatenate([other, mine], axis))


def prepare_kernel(cuts, pieces, place_ref, slab_ref, got_ref, *refs):
    outs, (own, sems) = refs[:-2], refs[-2:]
    zs, rows, part = own.shape
    z, core = place_ref[0], place_ref[1]

    def fetch(bits):
        at = pl.multiple_of(core * (zs * part) + (z ^ bits) * part, 128)
        return pltpu.make_async_copy(slab_ref.at[:, pl.ds(at, part)], own.at[bits], sems.at[bits])

    for bits, _, _ in cuts:
        fetch(bits).start()
    begin = 0
    for bits, from_, depth in cuts:
        fetch(bits).wait()
        for out, (which, start, width) in zip(outs, pieces):
            if which != bits:
                continue
            columns = slice(start, start + width)
            other = slice(begin + start - from_, begin + start - from_ + width)

            @pl.when(core == 0)
            def _():
                out[:rows, :] = own[bits, :, columns]
                out[rows:, :] = got_ref[:, other]

            @pl.when(core == 1)
            def _():
                out[:rows, :] = got_ref[:, other]
                out[rows:, :] = own[bits, :, columns]

        begin += depth


def prepare(place, slab, got, part, zs, cuts, pieces):
    rows = got.shape[0]
    vmem = pl.BlockSpec(memory_space=pltpu.VMEM)
    return pl.pallas_call(
        functools.partial(prepare_kernel, cuts, pieces),
        out_shape=[jax.ShapeDtypeStruct((2 * rows, width), jnp.float32) for _, _, width in pieces],
        in_specs=[pl.BlockSpec(memory_space=pltpu.SMEM), pl.BlockSpec(memory_space=pl.ANY), vmem],
        out_specs=[vmem] * len(pieces),
        scratch_shapes=[pltpu.VMEM((zs, rows, part), jnp.float32), pltpu.SemaphoreType.DMA((zs,))],
        compiler_params=pltpu.CompilerParams(vmem_limit_bytes=24 * 2**20),
        cost_estimate=pl.CostEstimate(flops=0, bytes_accessed=100_000_000, transcendentals=0),
        name="prepare",
    )(place, slab, got)


def split(x):
    high = x.astype(jnp.bfloat16)
    return high, (x - high.astype(jnp.float32)).astype(jnp.bfloat16)


def layout(n):
    places, at, strip = [], 0, n % 128
    for j in range(n // 128):
        places.append((at, 128 * (j + 1), at + 128 * (j + 1)))
        at += 128 * (j + 1) + strip
    return places, at, at + strip


def add_gram(starts, width, place_ref, blocks, whole, high_ref, low_ref, packed, base_ref):
    zs = len(blocks)
    n = whole.shape[0]
    deep = n // zs
    z = place_ref[0]
    for bits, (block, start) in enumerate(zip(blocks, starts)):
        if deep % 8 == 0:
            whole[pl.ds(pl.multiple_of((z ^ bits) * deep, 8), deep), :] = block[:, start : start + width]
            continue
        for here in range(zs):

            @pl.when(z == here)
            def _():
                at = (here ^ bits) * deep
                whole[at : at + deep, :] = block[:, start : start + width]

    places, corner, size = layout(n)
    edge = n // 128 * 128
    high_ref[...], low_ref[...] = split(whole[...])

    def product(r0, r1, c0, c1):
        def times(a, b):
            return lax.dot_general(a[r0:r1, :], b[c0:c1, :], (((1,), (1,)), ((), ())), preferred_element_type=jnp.float32)

        return times(high_ref, low_ref) + times(low_ref, high_ref) + times(high_ref, high_ref)

    def put(at, value):
        rows = slice(at, at + value.shape[0])
        packed[rows, :] = value if base_ref is None else value + base_ref[rows, :]

    for start in range(0, edge, 256):
        last = start + 256 >= edge
        stop = min(start + 256, edge)
        upper = product(0, n if last else stop, start, n if last else stop)
        for j in range(start // 128, stop // 128):
            at, rows, _ = places[j]
            put(at, upper[:rows, 128 * j - start : 128 * j - start + 128])
    if n > edge:
        strip = upper[:, edge - start :]
        for j, (_, _, at) in enumerate(places):
            put(at, strip[128 * j : 128 * j + 128].T)
        put(corner, jnp.pad(strip[edge:], ((0, 0), (0, 128 - (n - edge)))))


def early_kernel(starts, width, place_ref, *refs):
    blocks, (packed, high_ref, low_ref, whole) = refs[: len(starts)], refs[len(starts) :]
    add_gram(starts, width, place_ref, blocks, whole, high_ref, low_ref, packed, None)


def late_kernel(starts, width, place_ref, base_ref, *refs):
    blocks, (mine_ref, theirs_ref, high_ref, low_ref, whole, packed) = refs[: len(starts)], refs[len(starts) :]
    add_gram(starts, width, place_ref, blocks, whole, high_ref, low_ref, packed, base_ref)
    half = mine_ref.shape[0]
    core = place_ref[1]
    mine_ref[...] = packed[pl.ds(pl.multiple_of(core * half, 8), half), :]
    theirs_ref[...] = packed[pl.ds(pl.multiple_of((1 - core) * half, 8), half), :]


def gram_part(place, base, blocks, starts, width):
    n = blocks[0].shape[0] * len(blocks)
    size = layout(n)[2]
    vmem = pl.BlockSpec(memory_space=pltpu.VMEM)
    parts = [jax.ShapeDtypeStruct((n, width), jnp.bfloat16)] * 2
    packed = (size, 128)
    whole = pltpu.VMEM((n, width), jnp.float32)
    if base is None:
        kernel, sums, scratch, first = early_kernel, [jax.ShapeDtypeStruct(packed, jnp.float32)], [whole], []
    else:
        half = jax.ShapeDtypeStruct((size // 2, 128), jnp.float32)
        kernel, sums, scratch, first = late_kernel, [half, half], [whole, pltpu.VMEM(packed, jnp.float32)], [base]
    return pl.pallas_call(
        functools.partial(kernel, starts, width),
        out_shape=[*sums, *parts],
        in_specs=[pl.BlockSpec(memory_space=pltpu.SMEM)] + [vmem] * (len(first) + len(blocks)),
        out_specs=[vmem] * (len(sums) + 2),
        scratch_shapes=scratch,
        compiler_params=pltpu.CompilerParams(vmem_limit_bytes=24 * 2**20),
        cost_estimate=pl.CostEstimate(flops=6 * n * n * width, bytes_accessed=8 * n * width, transcendentals=0),
        name="gram_early" if base is None else "gram_late",
    )(place, *first, *blocks)


def lower_inverse(small):
    n = small.shape[0]
    lanes = 128
    full = (8, lanes)
    col = lax.broadcasted_iota(jnp.int32, full, 1)
    row = lax.broadcasted_iota(jnp.int32, full, 0)
    left = [small[8 * i : 8 * i + 8, :] for i in range(n // 8)]
    right = [(col == row + 8 * i).astype(jnp.float32) for i in range(n // 8)]
    done = []
    for p in range(n // 8):
        at = 8 * p
        d = {(a, b): jnp.broadcast_to(left[p][a : a + 1, at + b : at + b + 1], full) for a in range(8) for b in range(a + 1)}
        low, inv_diag = {}, []
        for b in range(8):
            r = lax.rsqrt(d[b, b])
            inv_diag.append(r)
            for a in range(b + 1, 8):
                low[a, b] = d[a, b] * r
            for a in range(b + 1, 8):
                for c in range(b + 1, a + 1):
                    d[a, c] = d[a, c] - low[a, b] * low[c, b]
        inv = {}
        for b in range(8):
            inv[b, b] = inv_diag[b]
            for a in range(b + 1, 8):
                s = low[a, b] * inv[b, b]
                for k in range(b + 1, a):
                    s = s + low[a, k] * inv[k, b]
                inv[a, b] = -s * inv_diag[a]
        lrow = [jnp.broadcast_to(left[p][k : k + 1, :], full) for k in range(8)]
        rrow = [jnp.broadcast_to(right[p][k : k + 1, :], full) for k in range(8)]
        y, v = [], []
        for m in range(8):
            ym, vm = inv[m, 0] * lrow[0], inv[m, 0] * rrow[0]
            for k in range(1, m + 1):
                ym, vm = ym + inv[m, k] * lrow[k], vm + inv[m, k] * rrow[k]
            y.append(ym)
            v.append(vm)
        out = v[0]
        for m in range(1, 8):
            out = jnp.where(row == m, v[m], out)
        done.append(out)
        for i in range(p + 1, n // 8):
            c = [jnp.broadcast_to(left[i][:, at + k : at + k + 1], full) for k in range(8)]
            li, ri = left[i], right[i]
            for m in range(8):
                f = inv[m, 0] * c[0]
                for k in range(1, m + 1):
                    f = f + inv[m, k] * c[k]
                li = li - f * y[m]
                ri = ri - f * v[m]
            left[i], right[i] = li, ri
    return jnp.concatenate(done, 0)


def iterations_kernel(iters, place_ref, mine_ref, other_ref, start_ref, factor_ref, copy_ref, packed, gram, high, low):
    def times(a, b, dims):
        return lax.dot_general(a, b, (dims, ((), ())), precision=HIGHEST, preferred_element_type=jnp.float32)

    n = gram.shape[0]
    places, corner, size = layout(n)
    edge = n // 128 * 128
    half = size // 2
    core = place_ref[1]
    packed[pl.ds(pl.multiple_of(core * half, 8), half), :] = mine_ref[...]
    packed[pl.ds(pl.multiple_of((1 - core) * half, 8), half), :] = other_ref[...]
    for j, (at, rows, strip) in enumerate(places):
        cols = slice(128 * j, 128 * j + 128)
        gram[:rows, cols] = packed[at : at + rows, :]
        for i in range(j):
            gram[cols, 128 * i : 128 * i + 128] = packed[at + 128 * i : at + 128 * i + 128, :].T
        if n > edge:
            gram[edge:, cols] = packed[strip : strip + n - edge, :]
            gram[cols, edge:] = packed[strip : strip + n - edge, :].T
    if n > edge:
        gram[edge:, edge:] = packed[corner:size, : n - edge]

    high[...], low[...] = split(gram[...])

    def apply_gram(x, over=0):
        x_high, x_low = split(x)

        def part(a, b):
            return lax.dot_general(a[...], b, (((1,), (over,)), ((), ())), preferred_element_type=jnp.float32)

        return part(high, x_low) + part(low, x_high) + part(high, x_high)

    image = apply_gram(start_ref[...], 1)
    for step in range(iters):
        small = times(image, image, ((0,), (0,)))
        inverse = lower_inverse(jnp.pad(small, ((0, 0), (0, 128 - small.shape[1]))))[:, : small.shape[1]]
        if step < iters - 1:
            image = times(apply_gram(image), inverse, ((1,), (1,)))
        else:
            factor_ref[...] = times(inverse, image, ((1,), (1,)))
            copy_ref[...] = factor_ref[...]


def iterations(place, mine, other, start, iters):
    n = start.shape[1]
    return pl.pallas_call(
        functools.partial(iterations_kernel, iters),
        out_shape=[jax.ShapeDtypeStruct(start.shape, jnp.float32)] * 2,
        in_specs=[pl.BlockSpec(memory_space=pltpu.SMEM)] + [pl.BlockSpec(memory_space=pltpu.VMEM)] * 3,
        out_specs=[pl.BlockSpec(memory_space=pltpu.VMEM)] * 2,
        scratch_shapes=[pltpu.VMEM((layout(n)[2], 128), jnp.float32), pltpu.VMEM((n, n), jnp.float32)] + [pltpu.VMEM((n, n), jnp.bfloat16)] * 2,
        compiler_params=pltpu.CompilerParams(vmem_limit_bytes=16 * 2**20),
        name="iterations",
    )(place, mine, other, start)


def farthest_first(size):
    return [size - 1, *range(1, size - 1)]


def mirrored(bits, rest):
    side = int(rest**0.5)
    return bits % side * side + bits // side if side * side == rest else bits


def swap_rest(x, fibre, rest, bits):
    other = mirrored(bits, rest)
    pairs = [(f * rest + r, f * rest + (r ^ (other if f % 2 else bits))) for f in range(fibre) for r in range(rest)]
    return lax.ppermute(x, ("fibre", "rest"), pairs)


def sum_everywhere(core, mine, theirs, fibre, rest):
    r = lax.axis_index("rest")
    half, width = mine.shape
    piece = -(-half // (8 * rest)) * 8
    mine = mine + swap(theirs, "fibre", fibre, 1)
    mine = jnp.pad(mine, ((0, piece * rest - half), (0, 0)))
    peers = {bits: r ^ jnp.where(core == 0, bits, mirrored(bits, rest)) for bits in farthest_first(rest)}
    total = lax.dynamic_slice(mine, (r * piece, 0), (piece, width))
    for bits, peer in peers.items():
        part = lax.dynamic_slice(mine, (peer * piece, 0), (piece, width))
        total = total + swap_rest(part, fibre, rest, bits)
    terms = {bits: swap(total, "fibre", fibre, 2 * bits) for bits in farthest_first(fibre // 2)}
    terms = [terms.get(bits, total) for bits in range(fibre // 2)]
    while len(terms) > 1:
        last = len(terms) - 1
        terms = [terms[i] + terms[last - i] for i in range(1, len(terms) // 2)] + [terms[last] + terms[0]]
    total = terms[0]
    out = lax.dynamic_update_slice(jnp.zeros((rest, piece, width), jnp.float32), total[None], (r, 0, 0))
    for bits, peer in peers.items():
        out = lax.dynamic_update_slice(out, swap_rest(total, fibre, rest, bits)[None], (peer, 0, 0))
    out = out.reshape(rest * piece, width)[:half]
    return out, swap(out, "fibre", fibre, 1)


def core_kernel(place_ref, basis_ref, *refs):
    parts, outs, share = refs[:4], refs[4:-1], refs[-1]
    zs = len(outs)
    two_own = share.shape[0] // zs
    high, low = split(basis_ref[...])

    def times(a, b):
        return lax.dot_general(a, b[...], (((1,), (0,)), ((), ())), preferred_element_type=jnp.float32)

    at = 0
    for first, second in (parts[:2], parts[2:]):
        width = first.shape[1]
        share[:, at : at + width] = times(high, second) + times(low, first) + times(high, first)
        at += width
    for here in range(zs):

        @pl.when(place_ref[0] == here)
        def _():
            for bits, out in enumerate(outs):
                out[...] = share[two_own * (here ^ bits) : two_own * (here ^ bits) + two_own, :]


def core_parts(place, basis, parts, zs):
    rank = basis.shape[0]
    part = parts[0].shape[1] + parts[2].shape[1]
    vmem = pl.BlockSpec(memory_space=pltpu.VMEM)
    return pl.pallas_call(
        core_kernel,
        out_shape=[jax.ShapeDtypeStruct((rank // zs, part), jnp.float32)] * zs,
        in_specs=[pl.BlockSpec(memory_space=pltpu.SMEM)] + [vmem] * 5,
        out_specs=[vmem] * zs,
        scratch_shapes=[pltpu.VMEM((rank, part), jnp.float32)],
        compiler_params=pltpu.CompilerParams(vmem_limit_bytes=16 * 2**20),
        name="core_parts",
    )(place, basis, *parts)


def assemble_kernel(distances, place_ref, *refs):
    blocks, (mine_ref, theirs_ref) = refs[:-2], refs[-2:]
    z, core = place_ref[0], place_ref[1]
    own, part = mine_ref.shape[0], blocks[0].shape[1]
    for bits, block in zip(distances, blocks):
        at = pl.multiple_of((z ^ bits) * part, 128)
        first, last = block[:own, :], block[own:, :]
        mine_ref[:, pl.ds(at, part)] = jnp.where(core == 0, first, last)
        theirs_ref[:, pl.ds(at, part)] = jnp.where(core == 0, last, first)


def assemble(place, moved):
    blocks = list(moved.values())
    two_own, part = blocks[0].shape
    vmem = pl.BlockSpec(memory_space=pltpu.VMEM)
    half = jax.ShapeDtypeStruct((two_own // 2, part * len(blocks)), jnp.float32)
    return pl.pallas_call(
        functools.partial(assemble_kernel, tuple(moved)),
        out_shape=(half, half),
        in_specs=[pl.BlockSpec(memory_space=pltpu.SMEM)] + [vmem] * len(blocks),
        out_specs=[vmem] * 2,
        compiler_params=pltpu.CompilerParams(vmem_limit_bytes=16 * 2**20),
        name="assemble",
    )(place, *blocks)


def shards(fibre, rest, slab, start_basis):
    rows, cols = slab.shape
    zs = fibre // 2
    f = lax.axis_index("fibre")
    z, core = f // 2, f % 2
    place = jnp.stack([z, core])
    half = cols // 2
    part = half // zs
    early = part * 3 // 4

    def cut(slab, whose, bits, start, width):
        return lax.dynamic_slice(slab, (0, whose * half + (z ^ bits) * part + start), (rows, width))

    far = zs - 1
    theirs, mine = cut(slab, 1 - core, far, 0, part), cut(slab, core, far, 0, part)
    slab, theirs, mine = lax.optimization_barrier((slab, theirs, mine))
    cuts = [(bits, 0, part) for bits in range(far - 1, -1, -1)]
    others = jnp.concatenate([cut(slab, 1 - core, *c) for c in cuts], 1)
    block = in_order(core, mine, swap(theirs, "fibre", fibre, 1), 0)
    others, block = lax.optimization_barrier((others, block))
    arrived = {far: swap(block, "fibre", fibre, 2 * far)}
    got = swap(others, "fibre", fibre, 1)
    pieces = []
    for bits, start, width in cuts:
        split_here = bits > 1
        pieces += [(bits, 0, early), (bits, early, part - early)] if split_here else [(bits, start, width)]
    late = {}
    for (bits, start, _), block in zip(pieces, prepare(place, slab, got, part, zs, cuts, pieces)):
        if start:
            block, arrived[far] = lax.optimization_barrier((block, arrived[far]))
        into = late if start else arrived
        into[bits] = swap(block, "fibre", fibre, 2 * bits) if bits else block
    first = [arrived[bits] for bits in range(zs)]
    last = [late.get(bits, arrived[bits]) for bits in range(zs)]
    last_from = tuple(0 if bits in late else early for bits in range(zs))
    packed, *parts = gram_part(place, None, first, (0,) * zs, early)
    mine, theirs, *more = gram_part(place, packed, last, last_from, part - early)
    mine, other = sum_everywhere(core, mine, theirs, fibre, rest)
    factor, basis = iterations(place, mine, other, start_basis.T, ITERS)
    blocks = core_parts(place, basis, [*parts, *more], zs)
    moved = {bits: swap(blocks[bits], "fibre", fibre, 2 * bits) for bits in farthest_first(zs)}
    moved[0] = blocks[0]
    mine, theirs = assemble(place, moved)
    return (factor.T, in_order(core, mine, swap(theirs, "fibre", fibre, 1), 1))


def solution(mesh):
    fibre, rest = mesh.shape["fibre"], mesh.shape["rest"]
    return jax.shard_map(
        lambda slab, start_basis: shards(fibre, rest, slab, start_basis),
        mesh=mesh,
        in_specs=(P("fibre", "rest"), P()),
        out_specs=(P(), P("fibre", "rest")),
        check_vma=False,
    )
```

```python
import functools

import jax
import jax.numpy as jnp
from jax import lax
from jax.experimental import pallas as pl
from jax.experimental.pallas import tpu as pltpu
from jax.sharding import PartitionSpec as P

ITERS = 3
HIGH = lax.Precision.HIGH
HIGHEST = lax.Precision.HIGHEST


def swap(x, axis, size, bits):
    return lax.ppermute(x, axis, [(i, i ^ bits) for i in range(size)])


def in_order(core, mine, other, axis):
    return jnp.where(core == 0, jnp.concatenate([mine, other], axis), jnp.concatenate([other, mine], axis))


def prepare_kernel(cuts, pieces, place_ref, slab_ref, got_ref, *refs):
    outs, (own, sems) = refs[:-2], refs[-2:]
    zs, rows, part = own.shape
    z, core = place_ref[0], place_ref[1]

    def fetch(bits):
        at = pl.multiple_of(core * (zs * part) + (z ^ bits) * part, 128)
        return pltpu.make_async_copy(slab_ref.at[:, pl.ds(at, part)], own.at[bits], sems.at[bits])

    for bits, _, _ in cuts:
        fetch(bits).start()
    begin = 0
    for bits, from_, depth in cuts:
        fetch(bits).wait()
        for out, (which, start, width) in zip(outs, pieces):
            if which != bits:
                continue
            columns = slice(start, start + width)
            other = slice(begin + start - from_, begin + start - from_ + width)

            @pl.when(core == 0)
            def _():
                out[:rows, :] = own[bits, :, columns]
                out[rows:, :] = got_ref[:, other]

            @pl.when(core == 1)
            def _():
                out[:rows, :] = got_ref[:, other]
                out[rows:, :] = own[bits, :, columns]

        begin += depth


def prepare(place, slab, got, part, zs, cuts, pieces):
    rows = got.shape[0]
    vmem = pl.BlockSpec(memory_space=pltpu.VMEM)
    return pl.pallas_call(
        functools.partial(prepare_kernel, cuts, pieces),
        out_shape=[jax.ShapeDtypeStruct((2 * rows, width), jnp.float32) for _, _, width in pieces],
        in_specs=[pl.BlockSpec(memory_space=pltpu.SMEM), pl.BlockSpec(memory_space=pltpu.HBM), vmem],
        out_specs=[vmem] * len(pieces),
        scratch_shapes=[pltpu.VMEM((zs, rows, part), jnp.float32), pltpu.SemaphoreType.DMA((zs,))],
        compiler_params=pltpu.CompilerParams(vmem_limit_bytes=24 * 2**20),
        cost_estimate=pl.CostEstimate(flops=0, bytes_accessed=100_000_000, transcendentals=0),
        name="prepare",
    )(place, slab, got)


def split(x):
    high = x.astype(jnp.bfloat16)
    return high, (x - high.astype(jnp.float32)).astype(jnp.bfloat16)


def layout(n):
    places, at, strip = [], 0, n % 128
    for j in range(n // 128):
        places.append((at, 128 * (j + 1), at + 128 * (j + 1)))
        at += 128 * (j + 1) + strip
    return places, at, at + strip


def add_gram(starts, width, place_ref, blocks, whole, parts, packed, base_ref):
    high_out, low_out, high_ref, low_ref, sems = parts
    zs = len(blocks)
    n = whole.shape[0]
    deep = n // zs
    z = place_ref[0]
    for bits, (block, start) in enumerate(zip(blocks, starts)):
        if deep % 8 == 0:
            whole[pl.ds(pl.multiple_of((z ^ bits) * deep, 8), deep), :] = block[:, start : start + width]
            continue
        for here in range(zs):

            @pl.when(z == here)
            def _():
                at = (here ^ bits) * deep
                whole[at : at + deep, :] = block[:, start : start + width]

    places, corner, size = layout(n)
    edge = n // 128 * 128
    high_ref[...], low_ref[...] = split(whole[...])
    saves = [
        pltpu.make_async_copy(high_ref, high_out, sems.at[0]),
        pltpu.make_async_copy(low_ref, low_out, sems.at[1]),
    ]
    for save in saves:
        save.start()

    def product(r0, r1, c0, c1):
        def times(a, b):
            return lax.dot_general(a[r0:r1, :], b[c0:c1, :], (((1,), (1,)), ((), ())), preferred_element_type=jnp.float32)

        return times(high_ref, low_ref) + times(low_ref, high_ref) + times(high_ref, high_ref)

    def put(at, value):
        rows = slice(at, at + value.shape[0])
        packed[rows, :] = value if base_ref is None else value + base_ref[rows, :]

    for start in range(0, edge, 256):
        last = start + 256 >= edge
        stop = min(start + 256, edge)
        upper = product(0, n if last else stop, start, n if last else stop)
        for j in range(start // 128, stop // 128):
            at, rows, _ = places[j]
            put(at, upper[:rows, 128 * j - start : 128 * j - start + 128])
    if n > edge:
        strip = upper[:, edge - start :]
        for j, (_, _, at) in enumerate(places):
            put(at, strip[128 * j : 128 * j + 128].T)
        put(corner, jnp.pad(strip[edge:], ((0, 0), (0, 128 - (n - edge)))))
    for save in saves:
        save.wait()


def early_kernel(starts, width, place_ref, *refs):
    blocks, (packed, *parts, whole) = refs[: len(starts)], refs[len(starts) :]
    add_gram(starts, width, place_ref, blocks, whole, parts, packed, None)


def late_kernel(starts, width, place_ref, base_ref, *refs):
    blocks, (mine_ref, theirs_ref, *parts, whole, packed) = refs[: len(starts)], refs[len(starts) :]
    add_gram(starts, width, place_ref, blocks, whole, parts, packed, base_ref)
    half = mine_ref.shape[0]
    core = place_ref[1]
    mine_ref[...] = packed[pl.ds(pl.multiple_of(core * half, 8), half), :]
    theirs_ref[...] = packed[pl.ds(pl.multiple_of((1 - core) * half, 8), half), :]


def gram_part(place, base, blocks, starts, width):
    n = blocks[0].shape[0] * len(blocks)
    size = layout(n)[2]
    vmem = pl.BlockSpec(memory_space=pltpu.VMEM)
    parts = [jax.ShapeDtypeStruct((n, width), jnp.bfloat16)] * 2
    scratch = [pltpu.VMEM((n, width), jnp.bfloat16)] * 2
    scratch += [pltpu.SemaphoreType.DMA((2,)), pltpu.VMEM((n, width), jnp.float32)]
    if base is None:
        kernel, sums, first = early_kernel, [jax.ShapeDtypeStruct((size, 128), jnp.float32)], []
    else:
        half = jax.ShapeDtypeStruct((size // 2, 128), jnp.float32)
        kernel, sums, first = late_kernel, [half, half], [base]
        scratch.append(pltpu.VMEM((size, 128), jnp.float32))
    return pl.pallas_call(
        functools.partial(kernel, starts, width),
        out_shape=[*sums, *parts],
        in_specs=[pl.BlockSpec(memory_space=pltpu.SMEM)] + [vmem] * (len(first) + len(blocks)),
        out_specs=[vmem] * len(sums) + [pl.BlockSpec(memory_space=pltpu.HBM)] * 2,
        scratch_shapes=scratch,
        compiler_params=pltpu.CompilerParams(vmem_limit_bytes=24 * 2**20),
        cost_estimate=pl.CostEstimate(flops=6 * n * n * width, bytes_accessed=8 * n * width, transcendentals=0),
        name="gram_early" if base is None else "gram_late",
    )(place, *first, *blocks)


def lower_inverse(small):
    n = small.shape[0]
    lanes = 128
    full = (8, lanes)
    col = lax.broadcasted_iota(jnp.int32, full, 1)
    row = lax.broadcasted_iota(jnp.int32, full, 0)
    left = [small[8 * i : 8 * i + 8, :] for i in range(n // 8)]
    right = [(col == row + 8 * i).astype(jnp.float32) for i in range(n // 8)]
    done = []
    for p in range(n // 8):
        at = 8 * p
        d = {(a, b): jnp.broadcast_to(left[p][a : a + 1, at + b : at + b + 1], full) for a in range(8) for b in range(a + 1)}
        lrow = [jnp.broadcast_to(left[p][k : k + 1, :], full) for k in range(8)]
        rrow = [jnp.broadcast_to(right[p][k : k + 1, :], full) for k in range(8)]
        low, scale, y, v = {}, [], [], []
        for b in range(8):
            scale.append(lax.rsqrt(d[b, b]))
            y.append(lrow[b] * scale[b])
            v.append(rrow[b] * scale[b])
            for a in range(b + 1, 8):
                low[a, b] = d[a, b] * scale[b]
            for a in range(b + 1, 8):
                for c in range(b + 1, a + 1):
                    d[a, c] = d[a, c] - low[a, b] * low[c, b]
                lrow[a] = lrow[a] - low[a, b] * y[b]
                rrow[a] = rrow[a] - low[a, b] * v[b]
        out = v[0]
        for m in range(1, 8):
            out = jnp.where(row == m, v[m], out)
        done.append(out)
        for i in range(p + 1, n // 8):
            c = [jnp.broadcast_to(left[i][:, at + k : at + k + 1], full) for k in range(8)]
            li, ri = left[i], right[i]
            for m in range(8):
                f = c[m] * scale[m]
                li = li - f * y[m]
                ri = ri - f * v[m]
                for k in range(m + 1, 8):
                    c[k] = c[k] - low[k, m] * f
            left[i], right[i] = li, ri
    return jnp.concatenate(done, 0)


def iterations_kernel(iters, zs, place_ref, mine_ref, other_ref, start_ref, *refs):
    kept, (factor_ref, *outs) = refs[:4], refs[4 : 5 + zs]
    packed, gram, high, low, columns_high, columns_low, share, sems = refs[5 + zs :]
    early = kept[0].shape[1]
    fetches = [
        pltpu.make_async_copy(kept[0], columns_high.at[:, :early], sems.at[0]),
        pltpu.make_async_copy(kept[1], columns_low.at[:, :early], sems.at[1]),
        pltpu.make_async_copy(kept[2], columns_high.at[:, early:], sems.at[2]),
        pltpu.make_async_copy(kept[3], columns_low.at[:, early:], sems.at[3]),
    ]
    for fetch in fetches:
        fetch.start()

    def times(a, b, dims):
        return lax.dot_general(a, b, (dims, ((), ())), precision=HIGHEST, preferred_element_type=jnp.float32)

    n = gram.shape[0]
    places, corner, size = layout(n)
    edge = n // 128 * 128
    half = size // 2
    core = place_ref[1]
    packed[pl.ds(pl.multiple_of(core * half, 8), half), :] = mine_ref[...]
    packed[pl.ds(pl.multiple_of((1 - core) * half, 8), half), :] = other_ref[...]
    for j, (at, rows, strip) in enumerate(places):
        cols = slice(128 * j, 128 * j + 128)
        gram[:rows, cols] = packed[at : at + rows, :]
        for i in range(j):
            gram[cols, 128 * i : 128 * i + 128] = packed[at + 128 * i : at + 128 * i + 128, :].T
        if n > edge:
            gram[edge:, cols] = packed[strip : strip + n - edge, :]
            gram[cols, edge:] = packed[strip : strip + n - edge, :].T
    if n > edge:
        gram[edge:, edge:] = packed[corner:size, : n - edge]

    high[...], low[...] = split(gram[...])

    def apply_gram(x, over=0):
        x_high, x_low = split(x)

        def part(a, b):
            return lax.dot_general(a[...], b, (((1,), (over,)), ((), ())), preferred_element_type=jnp.float32)

        return part(high, x_low) + part(low, x_high) + part(high, x_high)

    image = apply_gram(start_ref[...], 1)
    for step in range(iters):
        small = times(image, image, ((0,), (0,)))
        inverse = lower_inverse(jnp.pad(small, ((0, 0), (0, 128 - small.shape[1]))))[:, : small.shape[1]]
        if step < iters - 1:
            image = times(apply_gram(image), inverse, ((1,), (1,)))
        else:
            basis = times(inverse, image, ((1,), (1,)))

    factor_ref[...] = basis
    basis_high, basis_low = split(basis)
    for fetch in fetches:
        fetch.wait()

    def on_columns(a, b):
        return lax.dot_general(a, b[...], (((1,), (0,)), ((), ())), preferred_element_type=jnp.float32)

    share[...] = on_columns(basis_high, columns_low) + on_columns(basis_low, columns_high) + on_columns(basis_high, columns_high)
    two_own = share.shape[0] // zs
    for here in range(zs):

        @pl.when(place_ref[0] == here)
        def _():
            for bits, out in enumerate(outs):
                out[...] = share[two_own * (here ^ bits) : two_own * (here ^ bits) + two_own, :]


def iterations(place, mine, other, start, parts, iters, zs):
    rank, n = start.shape
    part = parts[0].shape[1] + parts[2].shape[1]
    vmem, hbm = pl.BlockSpec(memory_space=pltpu.VMEM), pl.BlockSpec(memory_space=pltpu.HBM)
    return pl.pallas_call(
        functools.partial(iterations_kernel, iters, zs),
        out_shape=[jax.ShapeDtypeStruct(start.shape, jnp.float32)]
        + [jax.ShapeDtypeStruct((rank // zs, part), jnp.float32)] * zs,
        in_specs=[pl.BlockSpec(memory_space=pltpu.SMEM)] + [vmem] * 3 + [hbm] * 4,
        out_specs=[vmem] * (1 + zs),
        scratch_shapes=[pltpu.VMEM((layout(n)[2], 128), jnp.float32), pltpu.VMEM((n, n), jnp.float32)]
        + [pltpu.VMEM((n, n), jnp.bfloat16)] * 2
        + [pltpu.VMEM((n, part), jnp.bfloat16)] * 2
        + [pltpu.VMEM((rank, part), jnp.float32), pltpu.SemaphoreType.DMA((4,))],
        compiler_params=pltpu.CompilerParams(vmem_limit_bytes=24 * 2**20),
        name="iterations",
    )(place, mine, other, start, *parts)


def farthest_first(size):
    return [size - 1, *range(1, size - 1)]


def mirrored(bits, rest):
    side = int(rest**0.5)
    return bits % side * side + bits // side if side * side == rest else bits


def swap_rest(x, fibre, rest, bits):
    other = mirrored(bits, rest)
    pairs = [(f * rest + r, f * rest + (r ^ (other if f % 2 else bits))) for f in range(fibre) for r in range(rest)]
    return lax.ppermute(x, ("fibre", "rest"), pairs)


def sum_everywhere(core, mine, theirs, fibre, rest):
    r = lax.axis_index("rest")
    half, width = mine.shape
    piece = -(-half // (8 * rest)) * 8
    mine = mine + swap(theirs, "fibre", fibre, 1)
    mine = jnp.pad(mine, ((0, piece * rest - half), (0, 0)))
    peers = {bits: r ^ jnp.where(core == 0, bits, mirrored(bits, rest)) for bits in farthest_first(rest)}
    total = lax.dynamic_slice(mine, (r * piece, 0), (piece, width))
    for bits, peer in peers.items():
        part = lax.dynamic_slice(mine, (peer * piece, 0), (piece, width))
        total = total + swap_rest(part, fibre, rest, bits)
    terms = {bits: swap(total, "fibre", fibre, 2 * bits) for bits in farthest_first(fibre // 2)}
    terms = [terms.get(bits, total) for bits in range(fibre // 2)]
    while len(terms) > 1:
        last = len(terms) - 1
        terms = [terms[i] + terms[last - i] for i in range(1, len(terms) // 2)] + [terms[last] + terms[0]]
    total = terms[0]
    out = lax.dynamic_update_slice(jnp.zeros((rest, piece, width), jnp.float32), total[None], (r, 0, 0))
    for bits, peer in peers.items():
        out = lax.dynamic_update_slice(out, swap_rest(total, fibre, rest, bits)[None], (peer, 0, 0))
    out = out.reshape(rest * piece, width)[:half]
    return out, swap(out, "fibre", fibre, 1)


def assemble_kernel(distances, place_ref, *refs):
    blocks, (mine_ref, theirs_ref) = refs[:-2], refs[-2:]
    z, core = place_ref[0], place_ref[1]
    own, part = mine_ref.shape[0], blocks[0].shape[1]
    for bits, block in zip(distances, blocks):
        at = pl.multiple_of((z ^ bits) * part, 128)
        first, last = block[:own, :], block[own:, :]
        mine_ref[:, pl.ds(at, part)] = jnp.where(core == 0, first, last)
        theirs_ref[:, pl.ds(at, part)] = jnp.where(core == 0, last, first)


def assemble(place, moved):
    blocks = list(moved.values())
    two_own, part = blocks[0].shape
    vmem = pl.BlockSpec(memory_space=pltpu.VMEM)
    half = jax.ShapeDtypeStruct((two_own // 2, part * len(blocks)), jnp.float32)
    return pl.pallas_call(
        functools.partial(assemble_kernel, tuple(moved)),
        out_shape=(half, half),
        in_specs=[pl.BlockSpec(memory_space=pltpu.SMEM)] + [vmem] * len(blocks),
        out_specs=[vmem] * 2,
        compiler_params=pltpu.CompilerParams(vmem_limit_bytes=16 * 2**20),
        name="assemble",
    )(place, *blocks)


def shards(fibre, rest, slab, start_basis):
    rows, cols = slab.shape
    zs = fibre // 2
    f = lax.axis_index("fibre")
    z, core = f // 2, f % 2
    place = jnp.stack([z, core])
    half = cols // 2
    part = half // zs
    early = part * 3 // 4

    def cut(slab, whose, bits, start, width):
        return lax.dynamic_slice(slab, (0, whose * half + (z ^ bits) * part + start), (rows, width))

    far = zs - 1
    theirs, mine = cut(slab, 1 - core, far, 0, part), cut(slab, core, far, 0, part)
    slab, theirs, mine = lax.optimization_barrier((slab, theirs, mine))
    cuts = [(bits, 0, part) for bits in range(far - 1, -1, -1)]
    others = jnp.concatenate([cut(slab, 1 - core, *c) for c in cuts], 1)
    block = in_order(core, mine, swap(theirs, "fibre", fibre, 1), 0)
    others, block = lax.optimization_barrier((others, block))
    arrived = {far: swap(block, "fibre", fibre, 2 * far)}
    got = swap(others, "fibre", fibre, 1)
    pieces = []
    for bits, start, width in cuts:
        split_here = bits > 1
        pieces += [(bits, 0, early), (bits, early, part - early)] if split_here else [(bits, start, width)]
    late = {}
    for (bits, start, _), block in zip(pieces, prepare(place, slab, got, part, zs, cuts, pieces)):
        if start:
            block, arrived[far] = lax.optimization_barrier((block, arrived[far]))
        into = late if start else arrived
        into[bits] = swap(block, "fibre", fibre, 2 * bits) if bits else block
    first = [arrived[bits] for bits in range(zs)]
    last = [late.get(bits, arrived[bits]) for bits in range(zs)]
    last_from = tuple(0 if bits in late else early for bits in range(zs))
    packed, *parts = gram_part(place, None, first, (0,) * zs, early)
    mine, theirs, *more = gram_part(place, packed, last, last_from, part - early)
    mine, other = sum_everywhere(core, mine, theirs, fibre, rest)
    factor, *blocks = iterations(place, mine, other, start_basis.T, [*parts, *more], ITERS, zs)
    moved = {bits: swap(blocks[bits], "fibre", fibre, 2 * bits) for bits in farthest_first(zs)}
    moved[0] = blocks[0]
    mine, theirs = assemble(place, moved)
    return (factor.T, in_order(core, mine, swap(theirs, "fibre", fibre, 1), 1))


def solution(mesh):
    fibre, rest = mesh.shape["fibre"], mesh.shape["rest"]
    return jax.shard_map(
        lambda slab, start_basis: shards(fibre, rest, slab, start_basis),
        mesh=mesh,
        in_specs=(P("fibre", "rest"), P()),
        out_specs=(P(), P("fibre", "rest")),
        check_vma=False,
    )
```

```python
import functools

import jax
import jax.numpy as jnp
from jax import lax
from jax.experimental import pallas as pl
from jax.experimental.pallas import tpu as pltpu
from jax.sharding import PartitionSpec as P

ITERS = 3
HIGH = lax.Precision.HIGH
HIGHEST = lax.Precision.HIGHEST


def swap(x, axis, size, bits):
    return lax.ppermute(x, axis, [(i, i ^ bits) for i in range(size)])


def in_order(core, mine, other, axis):
    return jnp.where(core == 0, jnp.concatenate([mine, other], axis), jnp.concatenate([other, mine], axis))


def prepare_kernel(cuts, pieces, place_ref, slab_ref, got_ref, *refs):
    outs, (own, sems) = refs[:-2], refs[-2:]
    zs, rows, part = own.shape
    z, core = place_ref[0], place_ref[1]

    def fetch(bits):
        at = pl.multiple_of(core * (zs * part) + (z ^ bits) * part, 128)
        return pltpu.make_async_copy(slab_ref.at[:, pl.ds(at, part)], own.at[bits], sems.at[bits])

    for bits, _, _ in cuts:
        fetch(bits).start()
    begin = 0
    for bits, from_, depth in cuts:
        fetch(bits).wait()
        for out, (which, start, width) in zip(outs, pieces):
            if which != bits:
                continue
            columns = slice(start, start + width)
            other = slice(begin + start - from_, begin + start - from_ + width)

            @pl.when(core == 0)
            def _():
                out[:rows, :] = own[bits, :, columns]
                out[rows:, :] = got_ref[:, other]

            @pl.when(core == 1)
            def _():
                out[:rows, :] = got_ref[:, other]
                out[rows:, :] = own[bits, :, columns]

        begin += depth


def prepare(place, slab, got, part, zs, cuts, pieces):
    rows = got.shape[0]
    vmem = pl.BlockSpec(memory_space=pltpu.VMEM)
    return pl.pallas_call(
        functools.partial(prepare_kernel, cuts, pieces),
        out_shape=[jax.ShapeDtypeStruct((2 * rows, width), jnp.float32) for _, _, width in pieces],
        in_specs=[pl.BlockSpec(memory_space=pltpu.SMEM), pl.BlockSpec(memory_space=pltpu.HBM), vmem],
        out_specs=[vmem] * len(pieces),
        scratch_shapes=[pltpu.VMEM((zs, rows, part), jnp.float32), pltpu.SemaphoreType.DMA((zs,))],
        compiler_params=pltpu.CompilerParams(vmem_limit_bytes=24 * 2**20),
        cost_estimate=pl.CostEstimate(flops=0, bytes_accessed=100_000_000, transcendentals=0),
        name="prepare",
    )(place, slab, got)


def split(x):
    high = x.astype(jnp.bfloat16)
    return high, (x - high.astype(jnp.float32)).astype(jnp.bfloat16)


def layout(n):
    places, at, strip = [], 0, n % 128
    for j in range(n // 128):
        places.append((at, 128 * (j + 1), at + 128 * (j + 1)))
        at += 128 * (j + 1) + strip
    return places, at, at + strip


def add_gram(starts, place_ref, blocks, whole, parts, packed, base):
    high_out, low_out, high_ref, low_ref, sems, *staged = parts
    zs = len(blocks)
    n, width = whole.shape
    deep = n // zs
    z = place_ref[0]

    def fetch(bits):
        source = blocks[bits].at[:, pl.ds(starts[bits], width)]
        target = staged[0].at[bits] if staged else whole.at[pl.ds(pl.multiple_of((z ^ bits) * deep, 8), deep)]
        return pltpu.make_async_copy(source, target, sems.at[2 + bits])

    fetches = [fetch(bits) for bits in range(zs)]
    if base is not None:
        fetches.append(pltpu.make_async_copy(base[0], base[1], sems.at[2 + zs]))
    for copy in fetches:
        copy.start()
    for copy in fetches:
        copy.wait()
    for here in range(zs if staged else 0):

        @pl.when(z == here)
        def _():
            for bits in range(zs):
                whole[(here ^ bits) * deep : (here ^ bits) * deep + deep, :] = staged[0][bits]

    places, corner, size = layout(n)
    edge = n // 128 * 128
    high_ref[...], low_ref[...] = split(whole[...])
    saves = [
        pltpu.make_async_copy(high_ref, high_out, sems.at[0]),
        pltpu.make_async_copy(low_ref, low_out, sems.at[1]),
    ]
    for save in saves:
        save.start()

    def product(r0, r1, c0, c1):
        def times(a, b):
            return lax.dot_general(a[r0:r1, :], b[c0:c1, :], (((1,), (1,)), ((), ())), preferred_element_type=jnp.float32)

        return times(high_ref, low_ref) + times(low_ref, high_ref) + times(high_ref, high_ref)

    def put(at, value):
        rows = slice(at, at + value.shape[0])
        packed[rows, :] = value if base is None else value + base[1][rows, :]

    for start in range(0, edge, 256):
        last = start + 256 >= edge
        stop = min(start + 256, edge)
        upper = product(0, n if last else stop, start, n if last else stop)
        for j in range(start // 128, stop // 128):
            at, rows, _ = places[j]
            put(at, upper[:rows, 128 * j - start : 128 * j - start + 128])
    if n > edge:
        strip = upper[:, edge - start :]
        for j, (_, _, at) in enumerate(places):
            put(at, strip[128 * j : 128 * j + 128].T)
        put(corner, jnp.pad(strip[edge:], ((0, 0), (0, 128 - (n - edge)))))
    for save in saves:
        save.wait()


def early_kernel(starts, place_ref, *refs):
    blocks, (packed, high_out, low_out, whole, *parts) = refs[: len(starts)], refs[len(starts) :]
    add_gram(starts, place_ref, blocks, whole, [high_out, low_out, *parts], packed, None)


def late_kernel(starts, place_ref, base_ref, *refs):
    blocks, (mine_ref, theirs_ref, high_out, low_out) = refs[: len(starts)], refs[len(starts) : len(starts) + 4]
    packed, base, whole, *parts = refs[len(starts) + 4 :]
    add_gram(starts, place_ref, blocks, whole, [high_out, low_out, *parts], packed, (base_ref, base))
    half = mine_ref.shape[0]
    core = place_ref[1]
    mine_ref[...] = packed[pl.ds(pl.multiple_of(core * half, 8), half), :]
    theirs_ref[...] = packed[pl.ds(pl.multiple_of((1 - core) * half, 8), half), :]


def gram_part(place, base, blocks, starts, width):
    zs, deep = len(blocks), blocks[0].shape[0]
    n = zs * deep
    size = layout(n)[2]
    vmem, hbm = pl.BlockSpec(memory_space=pltpu.VMEM), pl.BlockSpec(memory_space=pltpu.HBM)
    parts = [jax.ShapeDtypeStruct((n, width), jnp.bfloat16)] * 2
    scratch = [pltpu.VMEM((n, width), jnp.float32)] + [pltpu.VMEM((n, width), jnp.bfloat16)] * 2
    scratch += [pltpu.SemaphoreType.DMA((3 + zs,))]
    scratch += [pltpu.VMEM((zs, deep, width), jnp.float32)] if deep % 8 else []
    if base is None:
        kernel, sums, first = early_kernel, [jax.ShapeDtypeStruct((size, 128), jnp.float32)], []
    else:
        half = jax.ShapeDtypeStruct((size // 2, 128), jnp.float32)
        kernel, sums, first = late_kernel, [half, half], [base]
        scratch = [pltpu.VMEM((size, 128), jnp.float32)] * 2 + scratch
    return pl.pallas_call(
        functools.partial(kernel, starts),
        out_shape=[*sums, *parts],
        in_specs=[pl.BlockSpec(memory_space=pltpu.SMEM)] + [hbm] * (len(first) + len(blocks)),
        out_specs=[vmem] * len(sums) + [hbm] * 2,
        scratch_shapes=scratch,
        compiler_params=pltpu.CompilerParams(vmem_limit_bytes=48 * 2**20),
        cost_estimate=pl.CostEstimate(flops=6 * n * n * width, bytes_accessed=8 * n * width, transcendentals=0),
        name="gram_early" if base is None else "gram_late",
    )(place, *first, *blocks)


def lower_inverse(small):
    n = small.shape[0]
    lanes = 128
    full = (8, lanes)
    col = lax.broadcasted_iota(jnp.int32, full, 1)
    row = lax.broadcasted_iota(jnp.int32, full, 0)
    left = [small[8 * i : 8 * i + 8, :] for i in range(n // 8)]
    right = [(col == row + 8 * i).astype(jnp.float32) for i in range(n // 8)]
    done = []
    for p in range(n // 8):
        at = 8 * p
        d = {(a, b): jnp.broadcast_to(left[p][a : a + 1, at + b : at + b + 1], full) for a in range(8) for b in range(a + 1)}
        lrow = [jnp.broadcast_to(left[p][k : k + 1, :], full) for k in range(8)]
        rrow = [jnp.broadcast_to(right[p][k : k + 1, :], full) for k in range(8)]
        low, scale, y, v = {}, [], [], []
        for b in range(8):
            scale.append(lax.rsqrt(d[b, b]))
            y.append(lrow[b] * scale[b])
            v.append(rrow[b] * scale[b])
            for a in range(b + 1, 8):
                low[a, b] = d[a, b] * scale[b]
            for a in range(b + 1, 8):
                for c in range(b + 1, a + 1):
                    d[a, c] = d[a, c] - low[a, b] * low[c, b]
                lrow[a] = lrow[a] - low[a, b] * y[b]
                rrow[a] = rrow[a] - low[a, b] * v[b]
        out = v[0]
        for m in range(1, 8):
            out = jnp.where(row == m, v[m], out)
        done.append(out)
        for i in range(p + 1, n // 8):
            c = [jnp.broadcast_to(left[i][:, at + k : at + k + 1], full) for k in range(8)]
            li, ri = left[i], right[i]
            for m in range(8):
                f = c[m] * scale[m]
                li = li - f * y[m]
                ri = ri - f * v[m]
                for k in range(m + 1, 8):
                    c[k] = c[k] - low[k, m] * f
            left[i], right[i] = li, ri
    return jnp.concatenate(done, 0)


def iterations_kernel(iters, zs, place_ref, mine_ref, other_ref, start_ref, *refs):
    kept, (factor_ref, *outs) = refs[:4], refs[4 : 5 + zs]
    packed, gram, high, low, columns_high, columns_low, share, sems = refs[5 + zs :]
    early = kept[0].shape[1]
    fetches = [
        pltpu.make_async_copy(kept[0], columns_high.at[:, :early], sems.at[0]),
        pltpu.make_async_copy(kept[1], columns_low.at[:, :early], sems.at[1]),
        pltpu.make_async_copy(kept[2], columns_high.at[:, early:], sems.at[2]),
        pltpu.make_async_copy(kept[3], columns_low.at[:, early:], sems.at[3]),
    ]
    for fetch in fetches:
        fetch.start()

    def times(a, b, dims):
        return lax.dot_general(a, b, (dims, ((), ())), precision=HIGHEST, preferred_element_type=jnp.float32)

    n = gram.shape[0]
    places, corner, size = layout(n)
    edge = n // 128 * 128
    half = size // 2
    core = place_ref[1]
    packed[pl.ds(pl.multiple_of(core * half, 8), half), :] = mine_ref[...]
    packed[pl.ds(pl.multiple_of((1 - core) * half, 8), half), :] = other_ref[...]
    for j, (at, rows, strip) in enumerate(places):
        cols = slice(128 * j, 128 * j + 128)
        gram[:rows, cols] = packed[at : at + rows, :]
        for i in range(j):
            gram[cols, 128 * i : 128 * i + 128] = packed[at + 128 * i : at + 128 * i + 128, :].T
        if n > edge:
            gram[edge:, cols] = packed[strip : strip + n - edge, :]
            gram[cols, edge:] = packed[strip : strip + n - edge, :].T
    if n > edge:
        gram[edge:, edge:] = packed[corner:size, : n - edge]

    high[...], low[...] = split(gram[...])

    def apply_gram(x, over=0):
        x_high, x_low = split(x)

        def part(a, b):
            return lax.dot_general(a[...], b, (((1,), (over,)), ((), ())), preferred_element_type=jnp.float32)

        return part(high, x_low) + part(low, x_high) + part(high, x_high)

    image = apply_gram(start_ref[...], 1)
    for step in range(iters):
        small = times(image, image, ((0,), (0,)))
        inverse = lower_inverse(jnp.pad(small, ((0, 0), (0, 128 - small.shape[1]))))[:, : small.shape[1]]
        if step < iters - 1:
            image = times(apply_gram(image), inverse, ((1,), (1,)))
        else:
            basis = times(inverse, image, ((1,), (1,)))

    factor_ref[...] = basis
    basis_high, basis_low = split(basis)
    for fetch in fetches:
        fetch.wait()

    def on_columns(a, b):
        return lax.dot_general(a, b[...], (((1,), (0,)), ((), ())), preferred_element_type=jnp.float32)

    share[...] = on_columns(basis_high, columns_low) + on_columns(basis_low, columns_high) + on_columns(basis_high, columns_high)
    two_own = share.shape[0] // zs
    for here in range(zs):

        @pl.when(place_ref[0] == here)
        def _():
            for bits, out in enumerate(outs):
                out[...] = share[two_own * (here ^ bits) : two_own * (here ^ bits) + two_own, :]


def iterations(place, mine, other, start, parts, iters, zs):
    rank, n = start.shape
    part = parts[0].shape[1] + parts[2].shape[1]
    vmem, hbm = pl.BlockSpec(memory_space=pltpu.VMEM), pl.BlockSpec(memory_space=pltpu.HBM)
    return pl.pallas_call(
        functools.partial(iterations_kernel, iters, zs),
        out_shape=[jax.ShapeDtypeStruct(start.shape, jnp.float32)]
        + [jax.ShapeDtypeStruct((rank // zs, part), jnp.float32)] * zs,
        in_specs=[pl.BlockSpec(memory_space=pltpu.SMEM)] + [vmem] * 3 + [hbm] * 4,
        out_specs=[vmem] * (1 + zs),
        scratch_shapes=[pltpu.VMEM((layout(n)[2], 128), jnp.float32), pltpu.VMEM((n, n), jnp.float32)]
        + [pltpu.VMEM((n, n), jnp.bfloat16)] * 2
        + [pltpu.VMEM((n, part), jnp.bfloat16)] * 2
        + [pltpu.VMEM((rank, part), jnp.float32), pltpu.SemaphoreType.DMA((4,))],
        compiler_params=pltpu.CompilerParams(vmem_limit_bytes=50 * 2**20),
        name="iterations",
    )(place, mine, other, start, *parts)


def farthest_first(size):
    return [size - 1, *range(1, size - 1)]


def mirrored(bits, rest):
    side = int(rest**0.5)
    return bits % side * side + bits // side if side * side == rest else bits


def swap_rest(x, fibre, rest, bits):
    other = mirrored(bits, rest)
    pairs = [(f * rest + r, f * rest + (r ^ (other if f % 2 else bits))) for f in range(fibre) for r in range(rest)]
    return lax.ppermute(x, ("fibre", "rest"), pairs)


def sum_everywhere(core, mine, theirs, fibre, rest):
    r = lax.axis_index("rest")
    half, width = mine.shape
    piece = -(-half // (8 * rest)) * 8
    mine = mine + swap(theirs, "fibre", fibre, 1)
    mine = jnp.pad(mine, ((0, piece * rest - half), (0, 0)))
    peers = {bits: r ^ jnp.where(core == 0, bits, mirrored(bits, rest)) for bits in farthest_first(rest)}
    total = lax.dynamic_slice(mine, (r * piece, 0), (piece, width))
    for bits, peer in peers.items():
        part = lax.dynamic_slice(mine, (peer * piece, 0), (piece, width))
        total = total + swap_rest(part, fibre, rest, bits)
    terms = {bits: swap(total, "fibre", fibre, 2 * bits) for bits in farthest_first(fibre // 2)}
    terms = [terms.get(bits, total) for bits in range(fibre // 2)]
    while len(terms) > 1:
        last = len(terms) - 1
        terms = [terms[i] + terms[last - i] for i in range(1, len(terms) // 2)] + [terms[last] + terms[0]]
    total = terms[0]
    out = lax.dynamic_update_slice(jnp.zeros((rest, piece, width), jnp.float32), total[None], (r, 0, 0))
    for bits, peer in peers.items():
        out = lax.dynamic_update_slice(out, swap_rest(total, fibre, rest, bits)[None], (peer, 0, 0))
    out = out.reshape(rest * piece, width)[:half]
    return out, swap(out, "fibre", fibre, 1)


def assemble_kernel(distances, place_ref, *refs):
    blocks, (mine_ref, theirs_ref) = refs[:-2], refs[-2:]
    z, core = place_ref[0], place_ref[1]
    own, part = mine_ref.shape[0], blocks[0].shape[1]
    for bits, block in zip(distances, blocks):
        at = pl.multiple_of((z ^ bits) * part, 128)
        first, last = block[:own, :], block[own:, :]
        mine_ref[:, pl.ds(at, part)] = jnp.where(core == 0, first, last)
        theirs_ref[:, pl.ds(at, part)] = jnp.where(core == 0, last, first)


def assemble(place, moved):
    blocks = list(moved.values())
    two_own, part = blocks[0].shape
    vmem = pl.BlockSpec(memory_space=pltpu.VMEM)
    half = jax.ShapeDtypeStruct((two_own // 2, part * len(blocks)), jnp.float32)
    return pl.pallas_call(
        functools.partial(assemble_kernel, tuple(moved)),
        out_shape=(half, half),
        in_specs=[pl.BlockSpec(memory_space=pltpu.SMEM)] + [vmem] * len(blocks),
        out_specs=[vmem] * 2,
        compiler_params=pltpu.CompilerParams(vmem_limit_bytes=16 * 2**20),
        name="assemble",
    )(place, *blocks)


def shards(fibre, rest, slab, start_basis):
    rows, cols = slab.shape
    zs = fibre // 2
    f = lax.axis_index("fibre")
    z, core = f // 2, f % 2
    place = jnp.stack([z, core])
    half = cols // 2
    part = half // zs
    early = part * 3 // 4

    def cut(slab, whose, bits, start, width):
        return lax.dynamic_slice(slab, (0, whose * half + (z ^ bits) * part + start), (rows, width))

    far = zs - 1
    theirs, mine = cut(slab, 1 - core, far, 0, part), cut(slab, core, far, 0, part)
    slab, theirs, mine = lax.optimization_barrier((slab, theirs, mine))
    cuts = [(bits, 0, part) for bits in range(far - 1, -1, -1)]
    others = jnp.concatenate([cut(slab, 1 - core, *c) for c in cuts], 1)
    block = in_order(core, mine, swap(theirs, "fibre", fibre, 1), 0)
    others, block = lax.optimization_barrier((others, block))
    arrived = {far: swap(block, "fibre", fibre, 2 * far)}
    got = swap(others, "fibre", fibre, 1)
    pieces = []
    for bits, start, width in cuts:
        split_here = bits > 1
        pieces += [(bits, 0, early), (bits, early, part - early)] if split_here else [(bits, start, width)]
    late = {}
    for (bits, start, _), block in zip(pieces, prepare(place, slab, got, part, zs, cuts, pieces)):
        if start:
            block, arrived[far] = lax.optimization_barrier((block, arrived[far]))
        into = late if start else arrived
        into[bits] = swap(block, "fibre", fibre, 2 * bits) if bits else block
    first = [arrived[bits] for bits in range(zs)]
    last = [late.get(bits, arrived[bits]) for bits in range(zs)]
    last_from = tuple(0 if bits in late else early for bits in range(zs))
    packed, *parts = gram_part(place, None, first, (0,) * zs, early)
    mine, theirs, *more = gram_part(place, packed, last, last_from, part - early)
    mine, other = sum_everywhere(core, mine, theirs, fibre, rest)
    factor, *blocks = iterations(place, mine, other, start_basis.T, [*parts, *more], ITERS, zs)
    moved = {bits: swap(blocks[bits], "fibre", fibre, 2 * bits) for bits in farthest_first(zs)}
    moved[0] = blocks[0]
    mine, theirs = assemble(place, moved)
    return (factor.T, in_order(core, mine, swap(theirs, "fibre", fibre, 1), 1))


def solution(mesh):
    fibre, rest = mesh.shape["fibre"], mesh.shape["rest"]
    return jax.shard_map(
        lambda slab, start_basis: shards(fibre, rest, slab, start_basis),
        mesh=mesh,
        in_specs=(P("fibre", "rest"), P()),
        out_specs=(P(), P("fibre", "rest")),
        check_vma=False,
    )
```

```python
import functools

import jax
import jax.numpy as jnp
from jax import lax
from jax.experimental import pallas as pl
from jax.experimental.pallas import tpu as pltpu
from jax.sharding import PartitionSpec as P

ITERS = 3
HIGH = lax.Precision.HIGH
HIGHEST = lax.Precision.HIGHEST


def swap(x, axis, size, bits):
    return lax.ppermute(x, axis, [(i, i ^ bits) for i in range(size)])


def in_order(core, mine, other, axis):
    return jnp.where(core == 0, jnp.concatenate([mine, other], axis), jnp.concatenate([other, mine], axis))


def prepare_kernel(cuts, pieces, place_ref, slab_ref, got_ref, *refs):
    outs, (own, sems) = refs[:-2], refs[-2:]
    zs, rows, part = own.shape
    z, core = place_ref[0], place_ref[1]

    def fetch(bits):
        at = pl.multiple_of(core * (zs * part) + (z ^ bits) * part, 128)
        return pltpu.make_async_copy(slab_ref.at[:, pl.ds(at, part)], own.at[bits], sems.at[bits])

    for bits, _, _ in cuts:
        fetch(bits).start()
    begin = 0
    for bits, from_, depth in cuts:
        fetch(bits).wait()
        for out, (which, start, width) in zip(outs, pieces):
            if which != bits:
                continue
            columns = slice(start, start + width)
            other = slice(begin + start - from_, begin + start - from_ + width)

            @pl.when(core == 0)
            def _():
                out[:rows, :] = own[bits, :, columns]
                out[rows:, :] = got_ref[:, other]

            @pl.when(core == 1)
            def _():
                out[:rows, :] = got_ref[:, other]
                out[rows:, :] = own[bits, :, columns]

        begin += depth


def prepare(place, slab, got, part, zs, cuts, pieces):
    rows = got.shape[0]
    vmem = pl.BlockSpec(memory_space=pltpu.VMEM)
    return pl.pallas_call(
        functools.partial(prepare_kernel, cuts, pieces),
        out_shape=[jax.ShapeDtypeStruct((2 * rows, width), jnp.float32) for _, _, width in pieces],
        in_specs=[pl.BlockSpec(memory_space=pltpu.SMEM), pl.BlockSpec(memory_space=pltpu.HBM), vmem],
        out_specs=[vmem] * len(pieces),
        scratch_shapes=[pltpu.VMEM((zs, rows, part), jnp.float32), pltpu.SemaphoreType.DMA((zs,))],
        compiler_params=pltpu.CompilerParams(vmem_limit_bytes=50 * 2**20),
        cost_estimate=pl.CostEstimate(flops=0, bytes_accessed=100_000_000, transcendentals=0),
        name="prepare",
    )(place, slab, got)


def split(x):
    high = x.astype(jnp.bfloat16)
    return high, (x - high.astype(jnp.float32)).astype(jnp.bfloat16)


def layout(n):
    blocks, strip = n // 128, n % 128
    above, strips, at = [], [], 0
    for j in range(blocks):
        above.append(at)
        strips.append(at + 128 * j)
        at += 128 * j + strip
    folded = [at + 128 * k for k in range((blocks + 1) // 2)]
    diagonals = at + 128 * len(folded)
    corner = diagonals + 8
    if blocks % 2 and strip <= 64:
        return above, strips, folded, diagonals, folded[-1] + 128 - strip, -(-corner // 64) * 64
    return above, strips, folded, diagonals, corner, -(-(corner + strip) // 64) * 64


def square(op):
    return op(lax.broadcasted_iota(jnp.int32, (128, 128), 0), lax.broadcasted_iota(jnp.int32, (128, 128), 1))


def add_gram(starts, place_ref, blocks, whole, parts, packed, base):
    high_out, low_out, high_ref, low_ref, sems, *staged = parts
    zs = len(blocks)
    n, width = whole.shape
    deep = n // zs
    z = place_ref[0]

    def fetch(bits):
        source = blocks[bits].at[:, pl.ds(starts[bits], width)]
        target = staged[0].at[bits] if staged else whole.at[pl.ds(pl.multiple_of((z ^ bits) * deep, 8), deep)]
        return pltpu.make_async_copy(source, target, sems.at[2 + bits])

    fetches = [fetch(bits) for bits in range(zs)]
    for copy in fetches:
        copy.start()
    if base is not None:
        base_copy = pltpu.make_async_copy(base[0], base[1], sems.at[2 + zs])
        base_copy.start()
    for copy in fetches:
        copy.wait()
    for here in range(zs if staged else 0):

        @pl.when(z == here)
        def _():
            for bits in range(zs):
                whole[(here ^ bits) * deep : (here ^ bits) * deep + deep, :] = staged[0][bits]

    above, strips, folded, diagonals, corner, size = layout(n)
    edge = n // 128 * 128
    high_ref[...], low_ref[...] = split(whole[...])
    saves = [
        pltpu.make_async_copy(high_ref, high_out, sems.at[0]),
        pltpu.make_async_copy(low_ref, low_out, sems.at[1]),
    ]
    for save in saves:
        save.start()

    def product(r0, r1, c0, c1):
        def times(a, b):
            return lax.dot_general(a[r0:r1, :], b[c0:c1, :], (((1,), (1,)), ((), ())), preferred_element_type=jnp.float32)

        return times(high_ref, low_ref) + times(low_ref, high_ref) + times(high_ref, high_ref)

    def put(at, value):
        rows = slice(at, at + value.shape[0])
        packed[rows, :] = value if base is None else value + base[1][rows, :]

    if base is not None:
        base_copy.wait()
    squares = []
    for start in range(0, edge, 256):
        last = start + 256 >= edge
        stop = min(start + 256, edge)
        upper = product(0, n if last else stop, start, n if last else stop)
        for j in range(start // 128, stop // 128):
            columns = slice(128 * j - start, 128 * j - start + 128)
            if j:
                put(above[j], upper[: 128 * j, columns])
            squares.append(upper[128 * j : 128 * j + 128, columns])
    rest = jnp.zeros((0, 128), jnp.float32)
    if n > edge:
        strip = upper[:, edge - start :]
        for j, at in enumerate(strips):
            put(at, strip[128 * j : 128 * j + 128].T)
        rest = jnp.pad(strip[edge:], ((0, 0), (0, 128 - (n - edge))))
    diagonal_rows = jnp.zeros((8, 128), jnp.float32)
    row = lax.broadcasted_iota(jnp.int32, (8, 128), 0)
    for k, at in enumerate(folded):
        value = squares[2 * k]
        if 2 * k + 1 < len(squares):
            other = squares[2 * k + 1]
            value = jnp.where(square(jnp.less_equal), value, other)
            diagonal = jnp.sum(jnp.where(square(jnp.equal), other, 0.0), axis=0, keepdims=True)
            diagonal_rows = jnp.where(row == k, diagonal, diagonal_rows)
        elif corner < diagonals:
            value = jnp.where(square(jnp.less_equal), value, jnp.pad(rest, ((128 - (n - edge), 0), (0, 0))))
        put(at, value)
    put(diagonals, diagonal_rows)
    if n > edge and corner > diagonals:
        put(corner, rest)
    filled = diagonals + 8 if corner < diagonals else corner + n - edge
    if filled < size:
        packed[filled:size, :] = jnp.zeros((size - filled, 128), jnp.float32)
    for save in saves:
        save.wait()


def early_kernel(starts, place_ref, *refs):
    blocks, (packed, high_out, low_out, whole, *parts) = refs[: len(starts)], refs[len(starts) :]
    add_gram(starts, place_ref, blocks, whole, [high_out, low_out, *parts], packed, None)


def late_kernel(starts, place_ref, base_ref, *refs):
    blocks, (mine_ref, theirs_ref, high_out, low_out) = refs[: len(starts)], refs[len(starts) : len(starts) + 4]
    packed, base, whole, *parts = refs[len(starts) + 4 :]
    add_gram(starts, place_ref, blocks, whole, [high_out, low_out, *parts], packed, (base_ref, base))
    half = mine_ref.shape[0]
    core = place_ref[1]
    mine_ref[...] = packed[pl.ds(pl.multiple_of(core * half, 8), half), :]
    theirs_ref[...] = packed[pl.ds(pl.multiple_of((1 - core) * half, 8), half), :]


def gram_part(place, base, blocks, starts, width):
    zs, deep = len(blocks), blocks[0].shape[0]
    n = zs * deep
    size = layout(n)[-1]
    vmem, hbm = pl.BlockSpec(memory_space=pltpu.VMEM), pl.BlockSpec(memory_space=pltpu.HBM)
    parts = [jax.ShapeDtypeStruct((n, width), jnp.bfloat16)] * 2
    scratch = [pltpu.VMEM((n, width), jnp.float32)] + [pltpu.VMEM((n, width), jnp.bfloat16)] * 2
    scratch += [pltpu.SemaphoreType.DMA((3 + zs,))]
    scratch += [pltpu.VMEM((zs, deep, width), jnp.float32)] if deep % 8 else []
    if base is None:
        kernel, sums, first = early_kernel, [jax.ShapeDtypeStruct((size, 128), jnp.float32)], []
    else:
        half = jax.ShapeDtypeStruct((size // 2, 128), jnp.float32)
        kernel, sums, first = late_kernel, [half, half], [base]
        scratch = [pltpu.VMEM((size, 128), jnp.float32)] * 2 + scratch
    return pl.pallas_call(
        functools.partial(kernel, starts),
        out_shape=[*sums, *parts],
        in_specs=[pl.BlockSpec(memory_space=pltpu.SMEM)] + [hbm] * (len(first) + len(blocks)),
        out_specs=[vmem] * len(sums) + [hbm] * 2,
        scratch_shapes=scratch,
        compiler_params=pltpu.CompilerParams(vmem_limit_bytes=48 * 2**20),
        cost_estimate=pl.CostEstimate(flops=6 * n * n * width, bytes_accessed=8 * n * width, transcendentals=0),
        name="gram_early" if base is None else "gram_late",
    )(place, *first, *blocks)


def lower_inverse(small):
    n = small.shape[0]
    lanes = 128
    full = (8, lanes)
    col = lax.broadcasted_iota(jnp.int32, full, 1)
    row = lax.broadcasted_iota(jnp.int32, full, 0)
    left = [small[8 * i : 8 * i + 8, :] for i in range(n // 8)]
    right = [(col == row + 8 * i).astype(jnp.float32) for i in range(n // 8)]
    done = []
    for p in range(n // 8):
        at = 8 * p
        d = {(a, b): jnp.broadcast_to(left[p][a : a + 1, at + b : at + b + 1], full) for a in range(8) for b in range(a + 1)}
        lrow = [jnp.broadcast_to(left[p][k : k + 1, :], full) for k in range(8)]
        rrow = [jnp.broadcast_to(right[p][k : k + 1, :], full) for k in range(8)]
        low, scale, y, v = {}, [], [], []
        for b in range(8):
            scale.append(lax.rsqrt(d[b, b]))
            y.append(lrow[b] * scale[b])
            v.append(rrow[b] * scale[b])
            for a in range(b + 1, 8):
                low[a, b] = d[a, b] * scale[b]
            for a in range(b + 1, 8):
                for c in range(b + 1, a + 1):
                    d[a, c] = d[a, c] - low[a, b] * low[c, b]
                lrow[a] = lrow[a] - low[a, b] * y[b]
                rrow[a] = rrow[a] - low[a, b] * v[b]
        out = v[0]
        for m in range(1, 8):
            out = jnp.where(row == m, v[m], out)
        done.append(out)
        for i in range(p + 1, n // 8):
            c = [jnp.broadcast_to(left[i][:, at + k : at + k + 1], full) for k in range(8)]
            li, ri = left[i], right[i]
            for m in range(8):
                f = c[m] * scale[m]
                li = li - f * y[m]
                ri = ri - f * v[m]
                for k in range(m + 1, 8):
                    c[k] = c[k] - low[k, m] * f
            left[i], right[i] = li, ri
    return jnp.concatenate(done, 0)


def iterations_kernel(iters, zs, place_ref, mine_ref, other_ref, start_ref, *refs):
    kept, (factor_ref, *outs) = refs[:4], refs[4 : 5 + zs]
    packed, gram, high, low, columns_high, columns_low, share, sems = refs[5 + zs :]
    early = kept[0].shape[1]
    fetches = [
        pltpu.make_async_copy(kept[0], columns_high.at[:, :early], sems.at[0]),
        pltpu.make_async_copy(kept[1], columns_low.at[:, :early], sems.at[1]),
        pltpu.make_async_copy(kept[2], columns_high.at[:, early:], sems.at[2]),
        pltpu.make_async_copy(kept[3], columns_low.at[:, early:], sems.at[3]),
    ]
    for fetch in fetches:
        fetch.start()

    def times(a, b, dims):
        return lax.dot_general(a, b, (dims, ((), ())), precision=HIGHEST, preferred_element_type=jnp.float32)

    n = gram.shape[0]
    above, strips, folded, diagonals, corner, size = layout(n)
    edge = n // 128 * 128
    half = size // 2
    core = place_ref[1]
    packed[pl.ds(pl.multiple_of(core * half, 8), half), :] = mine_ref[...]
    packed[pl.ds(pl.multiple_of((1 - core) * half, 8), half), :] = other_ref[...]
    for j, (at, strip) in enumerate(zip(above, strips)):
        cols = slice(128 * j, 128 * j + 128)
        if j:
            gram[: 128 * j, cols] = packed[at : at + 128 * j, :]
        for i in range(j):
            gram[cols, 128 * i : 128 * i + 128] = packed[at + 128 * i : at + 128 * i + 128, :].T
        fold = packed[folded[j // 2] : folded[j // 2] + 128, :]
        if j % 2 == 0:
            gram[cols, cols] = jnp.where(square(jnp.less_equal), fold, fold.T)
        else:
            diagonal = packed[diagonals : diagonals + 8, :][j // 2 : j // 2 + 1, :]
            fold = jnp.where(square(jnp.greater), fold, fold.T)
            gram[cols, cols] = jnp.where(square(jnp.equal), diagonal, fold)
        if n > edge:
            gram[edge:, cols] = packed[strip : strip + n - edge, :]
            gram[cols, edge:] = packed[strip : strip + n - edge, :].T
    if n > edge:
        gram[edge:, edge:] = packed[corner : corner + n - edge, : n - edge]

    high[...], low[...] = split(gram[...])

    def apply_gram(x, over=0):
        x_high, x_low = split(x)

        def part(a, b):
            return lax.dot_general(a[...], b, (((1,), (over,)), ((), ())), preferred_element_type=jnp.float32)

        return part(high, x_low) + part(low, x_high) + part(high, x_high)

    image = apply_gram(start_ref[...], 1)
    for step in range(iters):
        small = times(image, image, ((0,), (0,)))
        inverse = lower_inverse(jnp.pad(small, ((0, 0), (0, 128 - small.shape[1]))))[:, : small.shape[1]]
        if step < iters - 1:
            image = times(apply_gram(image), inverse, ((1,), (1,)))
        else:
            basis = times(inverse, image, ((1,), (1,)))

    factor_ref[...] = basis
    basis_high, basis_low = split(basis)
    for fetch in fetches:
        fetch.wait()

    def on_columns(a, b):
        return lax.dot_general(a, b[...], (((1,), (0,)), ((), ())), preferred_element_type=jnp.float32)

    share[...] = on_columns(basis_high, columns_low) + on_columns(basis_low, columns_high) + on_columns(basis_high, columns_high)
    two_own = share.shape[0] // zs
    for here in range(zs):

        @pl.when(place_ref[0] == here)
        def _():
            for bits, out in enumerate(outs):
                out[...] = share[two_own * (here ^ bits) : two_own * (here ^ bits) + two_own, :]


def iterations(place, mine, other, start, parts, iters, zs):
    rank, n = start.shape
    part = parts[0].shape[1] + parts[2].shape[1]
    vmem, hbm = pl.BlockSpec(memory_space=pltpu.VMEM), pl.BlockSpec(memory_space=pltpu.HBM)
    return pl.pallas_call(
        functools.partial(iterations_kernel, iters, zs),
        out_shape=[jax.ShapeDtypeStruct(start.shape, jnp.float32)]
        + [jax.ShapeDtypeStruct((rank // zs, part), jnp.float32)] * zs,
        in_specs=[pl.BlockSpec(memory_space=pltpu.SMEM)] + [vmem] * 3 + [hbm] * 4,
        out_specs=[vmem] * (1 + zs),
        scratch_shapes=[pltpu.VMEM((layout(n)[-1], 128), jnp.float32), pltpu.VMEM((n, n), jnp.float32)]
        + [pltpu.VMEM((n, n), jnp.bfloat16)] * 2
        + [pltpu.VMEM((n, part), jnp.bfloat16)] * 2
        + [pltpu.VMEM((rank, part), jnp.float32), pltpu.SemaphoreType.DMA((4,))],
        compiler_params=pltpu.CompilerParams(vmem_limit_bytes=50 * 2**20),
        name="iterations",
    )(place, mine, other, start, *parts)


def farthest_first(size):
    return [size - 1, *range(1, size - 1)]


def mirrored(bits, rest):
    side = int(rest**0.5)
    return bits % side * side + bits // side if side * side == rest else bits


def swap_rest(x, fibre, rest, bits):
    other = mirrored(bits, rest)
    pairs = [(f * rest + r, f * rest + (r ^ (other if f % 2 else bits))) for f in range(fibre) for r in range(rest)]
    return lax.ppermute(x, ("fibre", "rest"), pairs)


def sum_everywhere(core, mine, theirs, fibre, rest):
    r = lax.axis_index("rest")
    half, width = mine.shape
    piece = -(-half // (8 * rest)) * 8
    mine = mine + swap(theirs, "fibre", fibre, 1)
    mine = jnp.pad(mine, ((0, piece * rest - half), (0, 0)))
    peers = {bits: r ^ jnp.where(core == 0, bits, mirrored(bits, rest)) for bits in farthest_first(rest)}
    total = lax.dynamic_slice(mine, (r * piece, 0), (piece, width))
    for bits, peer in peers.items():
        part = lax.dynamic_slice(mine, (peer * piece, 0), (piece, width))
        total = total + swap_rest(part, fibre, rest, bits)
    terms = {bits: swap(total, "fibre", fibre, 2 * bits) for bits in farthest_first(fibre // 2)}
    terms = [terms.get(bits, total) for bits in range(fibre // 2)]
    while len(terms) > 1:
        last = len(terms) - 1
        terms = [terms[i] + terms[last - i] for i in range(1, len(terms) // 2)] + [terms[last] + terms[0]]
    total = terms[0]
    out = lax.dynamic_update_slice(jnp.zeros((rest, piece, width), jnp.float32), total[None], (r, 0, 0))
    for bits, peer in peers.items():
        out = lax.dynamic_update_slice(out, swap_rest(total, fibre, rest, bits)[None], (peer, 0, 0))
    out = out.reshape(rest * piece, width)[:half]
    return out, swap(out, "fibre", fibre, 1)


def assemble_kernel(distances, place_ref, *refs):
    blocks, (mine_ref, theirs_ref) = refs[:-2], refs[-2:]
    z, core = place_ref[0], place_ref[1]
    own, part = mine_ref.shape[0], blocks[0].shape[1]
    for bits, block in zip(distances, blocks):
        at = pl.multiple_of((z ^ bits) * part, 128)
        first, last = block[:own, :], block[own:, :]
        mine_ref[:, pl.ds(at, part)] = jnp.where(core == 0, first, last)
        theirs_ref[:, pl.ds(at, part)] = jnp.where(core == 0, last, first)


def assemble(place, moved):
    blocks = list(moved.values())
    two_own, part = blocks[0].shape
    vmem = pl.BlockSpec(memory_space=pltpu.VMEM)
    half = jax.ShapeDtypeStruct((two_own // 2, part * len(blocks)), jnp.float32)
    return pl.pallas_call(
        functools.partial(assemble_kernel, tuple(moved)),
        out_shape=(half, half),
        in_specs=[pl.BlockSpec(memory_space=pltpu.SMEM)] + [vmem] * len(blocks),
        out_specs=[vmem] * 2,
        compiler_params=pltpu.CompilerParams(vmem_limit_bytes=16 * 2**20),
        name="assemble",
    )(place, *blocks)


def shards(fibre, rest, slab, start_basis):
    rows, cols = slab.shape
    zs = fibre // 2
    f = lax.axis_index("fibre")
    z, core = f // 2, f % 2
    place = jnp.stack([z, core])
    half = cols // 2
    part = half // zs
    early = part * 3 // 4

    def cut(slab, whose, bits, start, width):
        return lax.dynamic_slice(slab, (0, whose * half + (z ^ bits) * part + start), (rows, width))

    far = zs - 1
    theirs, mine = cut(slab, 1 - core, far, 0, part), cut(slab, core, far, 0, part)
    slab, theirs, mine = lax.optimization_barrier((slab, theirs, mine))
    cuts = [(bits, 0, part) for bits in range(far - 1, -1, -1)]
    others = jnp.concatenate([cut(slab, 1 - core, *c) for c in cuts], 1)
    block = in_order(core, mine, swap(theirs, "fibre", fibre, 1), 0)
    others, block = lax.optimization_barrier((others, block))
    arrived = {far: swap(block, "fibre", fibre, 2 * far)}
    got = swap(others, "fibre", fibre, 1)
    pieces = []
    for bits, start, width in cuts:
        split_here = bits > 1
        pieces += [(bits, 0, early), (bits, early, part - early)] if split_here else [(bits, start, width)]
    late = {}
    for (bits, start, _), block in zip(pieces, prepare(place, slab, got, part, zs, cuts, pieces)):
        if start:
            block, arrived[far] = lax.optimization_barrier((block, arrived[far]))
        into = late if start else arrived
        into[bits] = swap(block, "fibre", fibre, 2 * bits) if bits else block
    first = [arrived[bits] for bits in range(zs)]
    last = [late.get(bits, arrived[bits]) for bits in range(zs)]
    last_from = tuple(0 if bits in late else early for bits in range(zs))
    packed, *parts = gram_part(place, None, first, (0,) * zs, early)
    mine, theirs, *more = gram_part(place, packed, last, last_from, part - early)
    mine, other = sum_everywhere(core, mine, theirs, fibre, rest)
    factor, *blocks = iterations(place, mine, other, start_basis.T, [*parts, *more], ITERS, zs)
    moved = {bits: swap(blocks[bits], "fibre", fibre, 2 * bits) for bits in farthest_first(zs)}
    moved[0] = blocks[0]
    mine, theirs = assemble(place, moved)
    return (factor.T, in_order(core, mine, swap(theirs, "fibre", fibre, 1), 1))


def solution(mesh):
    fibre, rest = mesh.shape["fibre"], mesh.shape["rest"]
    return jax.shard_map(
        lambda slab, start_basis: shards(fibre, rest, slab, start_basis),
        mesh=mesh,
        in_specs=(P("fibre", "rest"), P()),
        out_specs=(P(), P("fibre", "rest")),
        check_vma=False,
    )
```

```python
import functools

import jax
import jax.numpy as jnp
from jax import lax
from jax.experimental import pallas as pl
from jax.experimental.pallas import tpu as pltpu
from jax.sharding import PartitionSpec as P

ITERS = 3


def swap(x, axis, size, bits):
    return lax.ppermute(x, axis, [(i, i ^ bits) for i in range(size)])


def in_order(core, mine, other, axis):
    return jnp.where(core == 0, jnp.concatenate([mine, other], axis), jnp.concatenate([other, mine], axis))


def prepare_kernel(cuts, pieces, place_ref, slab_ref, got_ref, *refs):
    outs, (own, sems) = refs[:-2], refs[-2:]
    zs, rows, part = own.shape
    z, core = place_ref[0], place_ref[1]

    def fetch(bits):
        at = pl.multiple_of(core * (zs * part) + (z ^ bits) * part, 128)
        return pltpu.make_async_copy(slab_ref.at[:, pl.ds(at, part)], own.at[bits], sems.at[bits])

    for bits, _, _ in cuts:
        fetch(bits).start()
    begin = 0
    for bits, from_, depth in cuts:
        fetch(bits).wait()
        for out, (which, start, width) in zip(outs, pieces):
            if which != bits:
                continue
            columns = slice(start, start + width)
            other = slice(begin + start - from_, begin + start - from_ + width)

            @pl.when(core == 0)
            def _():
                out[:rows, :] = own[bits, :, columns]
                out[rows:, :] = got_ref[:, other]

            @pl.when(core == 1)
            def _():
                out[:rows, :] = got_ref[:, other]
                out[rows:, :] = own[bits, :, columns]

        begin += depth


def prepare(place, slab, got, part, zs, cuts, pieces):
    rows = got.shape[0]
    vmem = pl.BlockSpec(memory_space=pltpu.VMEM)
    return pl.pallas_call(
        functools.partial(prepare_kernel, cuts, pieces),
        out_shape=[jax.ShapeDtypeStruct((2 * rows, width), jnp.float32) for _, _, width in pieces],
        in_specs=[pl.BlockSpec(memory_space=pltpu.SMEM), pl.BlockSpec(memory_space=pltpu.HBM), vmem],
        out_specs=[vmem] * len(pieces),
        scratch_shapes=[pltpu.VMEM((zs, rows, part), jnp.float32), pltpu.SemaphoreType.DMA((zs,))],
        compiler_params=pltpu.CompilerParams(vmem_limit_bytes=50 * 2**20),
        cost_estimate=pl.CostEstimate(flops=0, bytes_accessed=100_000_000, transcendentals=0),
        name="prepare",
    )(place, slab, got)


def split(x):
    high = x.astype(jnp.bfloat16)
    return high, (x - high.astype(jnp.float32)).astype(jnp.bfloat16)


def split3(x):
    high = x.astype(jnp.bfloat16)
    rest = x - high.astype(jnp.float32)
    middle = rest.astype(jnp.bfloat16)
    return high, middle, (rest - middle.astype(jnp.float32)).astype(jnp.bfloat16)


def contract(a, b, over_a, over_b):
    return lax.dot_general(a, b, (((over_a,), (over_b,)), ((), ())), preferred_element_type=jnp.float32)


def side_by_side(*parts):
    return jnp.concatenate(parts, 1)


def quarters(x):
    return (x[:128, :128] + x[128:, 128:]) + (x[:128, 128:] + x[128:, :128])


def layout(n):
    blocks, strip = n // 128, n % 128
    above, strips, at = [], [], 0
    for j in range(blocks):
        above.append(at)
        strips.append(at + 128 * j)
        at += 128 * j + strip
    folded = [at + 128 * k for k in range((blocks + 1) // 2)]
    diagonals = at + 128 * len(folded)
    corner = diagonals + 8
    if blocks % 2 and strip <= 64:
        return above, strips, folded, diagonals, folded[-1] + 128 - strip, -(-corner // 64) * 64
    return above, strips, folded, diagonals, corner, -(-(corner + strip) // 64) * 64


def square(op):
    return op(lax.broadcasted_iota(jnp.int32, (128, 128), 0), lax.broadcasted_iota(jnp.int32, (128, 128), 1))


def add_gram(starts, place_ref, blocks, whole, parts, packed, base):
    high_out, low_out, high_ref, low_ref, sems, *staged = parts
    zs = len(blocks)
    n, width = whole.shape
    deep = n // zs
    z = place_ref[0]

    def fetch(bits):
        source = blocks[bits].at[:, pl.ds(starts[bits], width)]
        target = staged[0].at[bits] if staged else whole.at[pl.ds(pl.multiple_of((z ^ bits) * deep, 8), deep)]
        return pltpu.make_async_copy(source, target, sems.at[2 + bits])

    fetches = [fetch(bits) for bits in range(zs)]
    for copy in fetches:
        copy.start()
    if base is not None:
        base_copy = pltpu.make_async_copy(base[0], base[1], sems.at[2 + zs])
        base_copy.start()
    for copy in fetches:
        copy.wait()
    for here in range(zs if staged else 0):

        @pl.when(z == here)
        def _():
            for bits in range(zs):
                whole[(here ^ bits) * deep : (here ^ bits) * deep + deep, :] = staged[0][bits]

    above, strips, folded, diagonals, corner, size = layout(n)
    edge = n // 128 * 128
    high_ref[...], low_ref[...] = split(whole[...])
    saves = [
        pltpu.make_async_copy(high_ref, high_out, sems.at[0]),
        pltpu.make_async_copy(low_ref, low_out, sems.at[1]),
    ]
    for save in saves:
        save.start()

    def product(r0, r1, c0, c1):
        def times(a, b):
            return lax.dot_general(a[r0:r1, :], b[c0:c1, :], (((1,), (1,)), ((), ())), preferred_element_type=jnp.float32)

        return times(high_ref, low_ref) + times(low_ref, high_ref) + times(high_ref, high_ref)

    def put(at, value):
        rows = slice(at, at + value.shape[0])
        packed[rows, :] = value if base is None else value + base[1][rows, :]

    if base is not None:
        base_copy.wait()
    squares = []
    for start in range(0, edge, 256):
        last = start + 256 >= edge
        stop = min(start + 256, edge)
        upper = product(0, n if last else stop, start, n if last else stop)
        for j in range(start // 128, stop // 128):
            columns = slice(128 * j - start, 128 * j - start + 128)
            if j:
                put(above[j], upper[: 128 * j, columns])
            squares.append(upper[128 * j : 128 * j + 128, columns])
    rest = jnp.zeros((0, 128), jnp.float32)
    if n > edge:
        strip = upper[:, edge - start :]
        for j, at in enumerate(strips):
            put(at, strip[128 * j : 128 * j + 128].T)
        rest = jnp.pad(strip[edge:], ((0, 0), (0, 128 - (n - edge))))
    diagonal_rows = jnp.zeros((8, 128), jnp.float32)
    row = lax.broadcasted_iota(jnp.int32, (8, 128), 0)
    for k, at in enumerate(folded):
        value = squares[2 * k]
        if 2 * k + 1 < len(squares):
            other = squares[2 * k + 1]
            value = jnp.where(square(jnp.less_equal), value, other)
            diagonal = jnp.sum(jnp.where(square(jnp.equal), other, 0.0), axis=0, keepdims=True)
            diagonal_rows = jnp.where(row == k, diagonal, diagonal_rows)
        elif corner < diagonals:
            value = jnp.where(square(jnp.less_equal), value, jnp.pad(rest, ((128 - (n - edge), 0), (0, 0))))
        put(at, value)
    put(diagonals, diagonal_rows)
    if n > edge and corner > diagonals:
        put(corner, rest)
    filled = diagonals + 8 if corner < diagonals else corner + n - edge
    if filled < size:
        packed[filled:size, :] = jnp.zeros((size - filled, 128), jnp.float32)
    for save in saves:
        save.wait()


def early_kernel(starts, place_ref, *refs):
    blocks, (packed, high_out, low_out, whole, *parts) = refs[: len(starts)], refs[len(starts) :]
    add_gram(starts, place_ref, blocks, whole, [high_out, low_out, *parts], packed, None)


def late_kernel(starts, place_ref, base_ref, *refs):
    blocks, (mine_ref, theirs_ref, high_out, low_out) = refs[: len(starts)], refs[len(starts) : len(starts) + 4]
    packed, base, whole, *parts = refs[len(starts) + 4 :]
    add_gram(starts, place_ref, blocks, whole, [high_out, low_out, *parts], packed, (base_ref, base))
    half = mine_ref.shape[0]
    core = place_ref[1]
    mine_ref[...] = packed[pl.ds(pl.multiple_of(core * half, 8), half), :]
    theirs_ref[...] = packed[pl.ds(pl.multiple_of((1 - core) * half, 8), half), :]


def gram_part(place, base, blocks, starts, width):
    zs, deep = len(blocks), blocks[0].shape[0]
    n = zs * deep
    size = layout(n)[-1]
    vmem, hbm = pl.BlockSpec(memory_space=pltpu.VMEM), pl.BlockSpec(memory_space=pltpu.HBM)
    parts = [jax.ShapeDtypeStruct((n, width), jnp.bfloat16)] * 2
    scratch = [pltpu.VMEM((n, width), jnp.float32)] + [pltpu.VMEM((n, width), jnp.bfloat16)] * 2
    scratch += [pltpu.SemaphoreType.DMA((3 + zs,))]
    scratch += [pltpu.VMEM((zs, deep, width), jnp.float32)] if deep % 8 else []
    if base is None:
        kernel, sums, first = early_kernel, [jax.ShapeDtypeStruct((size, 128), jnp.float32)], []
    else:
        half = jax.ShapeDtypeStruct((size // 2, 128), jnp.float32)
        kernel, sums, first = late_kernel, [half, half], [base]
        scratch = [pltpu.VMEM((size, 128), jnp.float32)] * 2 + scratch
    return pl.pallas_call(
        functools.partial(kernel, starts),
        out_shape=[*sums, *parts],
        in_specs=[pl.BlockSpec(memory_space=pltpu.SMEM)] + [hbm] * (len(first) + len(blocks)),
        out_specs=[vmem] * len(sums) + [hbm] * 2,
        scratch_shapes=scratch,
        compiler_params=pltpu.CompilerParams(vmem_limit_bytes=48 * 2**20),
        cost_estimate=pl.CostEstimate(flops=6 * n * n * width, bytes_accessed=8 * n * width, transcendentals=0),
        name="gram_early" if base is None else "gram_late",
    )(place, *first, *blocks)


def lower_inverse(small):
    n = small.shape[0]
    lanes = 128
    full = (8, lanes)
    col = lax.broadcasted_iota(jnp.int32, full, 1)
    row = lax.broadcasted_iota(jnp.int32, full, 0)
    left = [small[8 * i : 8 * i + 8, :] for i in range(n // 8)]
    right = [(col == row + 8 * i).astype(jnp.float32) for i in range(n // 8)]
    done = []
    for p in range(n // 8):
        at = 8 * p
        d = {(a, b): jnp.broadcast_to(left[p][a : a + 1, at + b : at + b + 1], full) for a in range(8) for b in range(a + 1)}
        lrow = [jnp.broadcast_to(left[p][k : k + 1, :], full) for k in range(8)]
        rrow = [jnp.broadcast_to(right[p][k : k + 1, :], full) for k in range(8)]
        low, scale, y, v = {}, [], [], []
        for b in range(8):
            scale.append(lax.rsqrt(d[b, b]))
            y.append(lrow[b] * scale[b])
            v.append(rrow[b] * scale[b])
            for a in range(b + 1, 8):
                low[a, b] = d[a, b] * scale[b]
            for a in range(b + 1, 8):
                for c in range(b + 1, a + 1):
                    d[a, c] = d[a, c] - low[a, b] * low[c, b]
                lrow[a] = lrow[a] - low[a, b] * y[b]
                rrow[a] = rrow[a] - low[a, b] * v[b]
        out = v[0]
        for m in range(1, 8):
            out = jnp.where(row == m, v[m], out)
        done.append(out)
        for i in range(p + 1, n // 8):
            c = [jnp.broadcast_to(left[i][:, at + k : at + k + 1], full) for k in range(8)]
            li, ri = left[i], right[i]
            for m in range(8):
                f = c[m] * scale[m]
                li = li - f * y[m]
                ri = ri - f * v[m]
                for k in range(m + 1, 8):
                    c[k] = c[k] - low[k, m] * f
            left[i], right[i] = li, ri
    return jnp.concatenate(done, 0)


def iterations_kernel(iters, zs, place_ref, mine_ref, other_ref, start_ref, *refs):
    kept, (factor_ref, *outs) = refs[:4], refs[4 : 5 + zs]
    packed, gram, high, low, columns_high, columns_low, share, sems = refs[5 + zs :]
    early = kept[0].shape[1]
    fetches = [
        pltpu.make_async_copy(kept[0], columns_high.at[:, :early], sems.at[0]),
        pltpu.make_async_copy(kept[1], columns_low.at[:, :early], sems.at[1]),
        pltpu.make_async_copy(kept[2], columns_high.at[:, early:], sems.at[2]),
        pltpu.make_async_copy(kept[3], columns_low.at[:, early:], sems.at[3]),
    ]
    for fetch in fetches:
        fetch.start()

    n = gram.shape[0]
    above, strips, folded, diagonals, corner, size = layout(n)
    edge = n // 128 * 128
    half = size // 2
    core = place_ref[1]
    packed[pl.ds(pl.multiple_of(core * half, 8), half), :] = mine_ref[...]
    packed[pl.ds(pl.multiple_of((1 - core) * half, 8), half), :] = other_ref[...]
    for j, (at, strip) in enumerate(zip(above, strips)):
        cols = slice(128 * j, 128 * j + 128)
        if j:
            gram[: 128 * j, cols] = packed[at : at + 128 * j, :]
        for i in range(j):
            gram[cols, 128 * i : 128 * i + 128] = packed[at + 128 * i : at + 128 * i + 128, :].T
        fold = packed[folded[j // 2] : folded[j // 2] + 128, :]
        if j % 2 == 0:
            gram[cols, cols] = jnp.where(square(jnp.less_equal), fold, fold.T)
        else:
            diagonal = packed[diagonals : diagonals + 8, :][j // 2 : j // 2 + 1, :]
            fold = jnp.where(square(jnp.greater), fold, fold.T)
            gram[cols, cols] = jnp.where(square(jnp.equal), diagonal, fold)
        if n > edge:
            gram[edge:, cols] = packed[strip : strip + n - edge, :]
            gram[cols, edge:] = packed[strip : strip + n - edge, :].T
    if n > edge:
        gram[edge:, edge:] = packed[corner : corner + n - edge, : n - edge]

    high[...], low[...] = split(gram[...])

    rank = start_ref.shape[0]
    x_high, x_low = split(jnp.pad(start_ref[...], ((0, 128 - rank), (0, 0))))
    both = contract(high[...], jnp.concatenate([x_high, x_low], 0), 1, 1)
    image = both[:, :128] + both[:, 128:] + contract(low[...], x_high, 1, 1)
    for step in range(iters):
        parts = split3(image)
        first = side_by_side(parts[0], parts[1])
        cross = contract(parts[0], parts[2], 0, 0)
        small = quarters(contract(first, first, 0, 0)) + (cross + cross.T)
        inverse = jnp.pad(lower_inverse(small[:rank]), ((0, 128 - rank), (0, 0)))
        inv = split3(inverse)
        if step < iters - 1:
            both = contract(high[...], first, 1, 0)
            image = both[:, :128] + both[:, 128:] + contract(low[...], parts[0], 1, 0)
            parts = split3(image)
            twice = [side_by_side(inv[0], inv[0]), side_by_side(inv[1], inv[1])]
            both = contract(side_by_side(parts[0], parts[1]), jnp.concatenate(twice, 0), 1, 1)
            last = contract(side_by_side(parts[0], parts[2]), side_by_side(inv[2], inv[0]), 1, 1)
            image = both[:, :128] + both[:, 128:] + last
        else:
            basis = contract(side_by_side(inv[0], inv[2]), side_by_side(parts[2], parts[0]), 1, 1)
            basis += contract(side_by_side(inv[0], inv[1]), side_by_side(parts[1], parts[1]), 1, 1)
            basis += contract(side_by_side(inv[0], inv[1]), side_by_side(parts[0], parts[0]), 1, 1)

    basis = basis[:rank]
    factor_ref[...] = basis
    basis_high, basis_low = split(basis)
    for fetch in fetches:
        fetch.wait()
    both = contract(jnp.concatenate([basis_high, basis_low], 0), columns_high[...], 1, 0)
    share[...] = both[:rank] + both[rank:] + contract(basis_high, columns_low[...], 1, 0)
    two_own = share.shape[0] // zs
    for here in range(zs):

        @pl.when(place_ref[0] == here)
        def _():
            for bits, out in enumerate(outs):
                out[...] = share[two_own * (here ^ bits) : two_own * (here ^ bits) + two_own, :]


def iterations(place, mine, other, start, parts, iters, zs):
    rank, n = start.shape
    part = parts[0].shape[1] + parts[2].shape[1]
    vmem, hbm = pl.BlockSpec(memory_space=pltpu.VMEM), pl.BlockSpec(memory_space=pltpu.HBM)
    return pl.pallas_call(
        functools.partial(iterations_kernel, iters, zs),
        out_shape=[jax.ShapeDtypeStruct(start.shape, jnp.float32)]
        + [jax.ShapeDtypeStruct((rank // zs, part), jnp.float32)] * zs,
        in_specs=[pl.BlockSpec(memory_space=pltpu.SMEM)] + [vmem] * 3 + [hbm] * 4,
        out_specs=[vmem] * (1 + zs),
        scratch_shapes=[pltpu.VMEM((layout(n)[-1], 128), jnp.float32), pltpu.VMEM((n, n), jnp.float32)]
        + [pltpu.VMEM((n, n), jnp.bfloat16)] * 2
        + [pltpu.VMEM((n, part), jnp.bfloat16)] * 2
        + [pltpu.VMEM((rank, part), jnp.float32), pltpu.SemaphoreType.DMA((4,))],
        compiler_params=pltpu.CompilerParams(vmem_limit_bytes=50 * 2**20),
        name="iterations",
    )(place, mine, other, start, *parts)


def farthest_first(size):
    return [size - 1, *range(1, size - 1)]


def mirrored(bits, rest):
    side = int(rest**0.5)
    return bits % side * side + bits // side if side * side == rest else bits


def swap_rest(x, fibre, rest, bits):
    other = mirrored(bits, rest)
    pairs = [(f * rest + r, f * rest + (r ^ (other if f % 2 else bits))) for f in range(fibre) for r in range(rest)]
    return lax.ppermute(x, ("fibre", "rest"), pairs)


def sum_everywhere(core, mine, theirs, fibre, rest):
    r = lax.axis_index("rest")
    half, width = mine.shape
    piece = -(-half // (8 * rest)) * 8
    mine = mine + swap(theirs, "fibre", fibre, 1)
    mine = jnp.pad(mine, ((0, piece * rest - half), (0, 0)))
    peers = {bits: r ^ jnp.where(core == 0, bits, mirrored(bits, rest)) for bits in farthest_first(rest)}
    total = lax.dynamic_slice(mine, (r * piece, 0), (piece, width))
    for bits, peer in peers.items():
        part = lax.dynamic_slice(mine, (peer * piece, 0), (piece, width))
        total = total + swap_rest(part, fibre, rest, bits)
    terms = {bits: swap(total, "fibre", fibre, 2 * bits) for bits in farthest_first(fibre // 2)}
    terms = [terms.get(bits, total) for bits in range(fibre // 2)]
    while len(terms) > 1:
        last = len(terms) - 1
        terms = [terms[i] + terms[last - i] for i in range(1, len(terms) // 2)] + [terms[last] + terms[0]]
    total = terms[0]
    out = lax.dynamic_update_slice(jnp.zeros((rest, piece, width), jnp.float32), total[None], (r, 0, 0))
    for bits, peer in peers.items():
        out = lax.dynamic_update_slice(out, swap_rest(total, fibre, rest, bits)[None], (peer, 0, 0))
    out = out.reshape(rest * piece, width)[:half]
    return out, swap(out, "fibre", fibre, 1)


def assemble_kernel(distances, place_ref, *refs):
    blocks, (mine_ref, theirs_ref) = refs[:-2], refs[-2:]
    z, core = place_ref[0], place_ref[1]
    own, part = mine_ref.shape[0], blocks[0].shape[1]
    for bits, block in zip(distances, blocks):
        at = pl.multiple_of((z ^ bits) * part, 128)
        first, last = block[:own, :], block[own:, :]
        mine_ref[:, pl.ds(at, part)] = jnp.where(core == 0, first, last)
        theirs_ref[:, pl.ds(at, part)] = jnp.where(core == 0, last, first)


def assemble(place, moved):
    blocks = list(moved.values())
    two_own, part = blocks[0].shape
    vmem = pl.BlockSpec(memory_space=pltpu.VMEM)
    half = jax.ShapeDtypeStruct((two_own // 2, part * len(blocks)), jnp.float32)
    return pl.pallas_call(
        functools.partial(assemble_kernel, tuple(moved)),
        out_shape=(half, half),
        in_specs=[pl.BlockSpec(memory_space=pltpu.SMEM)] + [vmem] * len(blocks),
        out_specs=[vmem] * 2,
        compiler_params=pltpu.CompilerParams(vmem_limit_bytes=16 * 2**20),
        name="assemble",
    )(place, *blocks)


def shards(fibre, rest, slab, start_basis):
    rows, cols = slab.shape
    zs = fibre // 2
    f = lax.axis_index("fibre")
    z, core = f // 2, f % 2
    place = jnp.stack([z, core])
    half = cols // 2
    part = half // zs
    early = part * 3 // 4

    def cut(slab, whose, bits, start, width):
        return lax.dynamic_slice(slab, (0, whose * half + (z ^ bits) * part + start), (rows, width))

    far = zs - 1
    theirs, mine = cut(slab, 1 - core, far, 0, part), cut(slab, core, far, 0, part)
    slab, theirs, mine = lax.optimization_barrier((slab, theirs, mine))
    cuts = [(bits, 0, part) for bits in range(far - 1, -1, -1)]
    others = jnp.concatenate([cut(slab, 1 - core, *c) for c in cuts], 1)
    block = in_order(core, mine, swap(theirs, "fibre", fibre, 1), 0)
    others, block = lax.optimization_barrier((others, block))
    arrived = {far: swap(block, "fibre", fibre, 2 * far)}
    got = swap(others, "fibre", fibre, 1)
    pieces = []
    for bits, start, width in cuts:
        split_here = bits > 1
        pieces += [(bits, 0, early), (bits, early, part - early)] if split_here else [(bits, start, width)]
    late = {}
    for (bits, start, _), block in zip(pieces, prepare(place, slab, got, part, zs, cuts, pieces)):
        if start:
            block, arrived[far] = lax.optimization_barrier((block, arrived[far]))
        into = late if start else arrived
        into[bits] = swap(block, "fibre", fibre, 2 * bits) if bits else block
    first = [arrived[bits] for bits in range(zs)]
    last = [late.get(bits, arrived[bits]) for bits in range(zs)]
    last_from = tuple(0 if bits in late else early for bits in range(zs))
    packed, *parts = gram_part(place, None, first, (0,) * zs, early)
    mine, theirs, *more = gram_part(place, packed, last, last_from, part - early)
    mine, other = sum_everywhere(core, mine, theirs, fibre, rest)
    factor, *blocks = iterations(place, mine, other, start_basis.T, [*parts, *more], ITERS, zs)
    moved = {bits: swap(blocks[bits], "fibre", fibre, 2 * bits) for bits in farthest_first(zs)}
    moved[0] = blocks[0]
    mine, theirs = assemble(place, moved)
    return (factor.T, in_order(core, mine, swap(theirs, "fibre", fibre, 1), 1))


def solution(mesh):
    fibre, rest = mesh.shape["fibre"], mesh.shape["rest"]
    return jax.shard_map(
        lambda slab, start_basis: shards(fibre, rest, slab, start_basis),
        mesh=mesh,
        in_specs=(P("fibre", "rest"), P()),
        out_specs=(P(), P("fibre", "rest")),
        check_vma=False,
    )
```

```python
import functools

import jax
import jax.numpy as jnp
from jax import lax
from jax.experimental import pallas as pl
from jax.experimental.pallas import tpu as pltpu
from jax.sharding import PartitionSpec as P

ITERS = 3


def swap(x, axis, size, bits):
    return lax.ppermute(x, axis, [(i, i ^ bits) for i in range(size)])


def in_order(core, mine, other, axis):
    return jnp.where(core == 0, jnp.concatenate([mine, other], axis), jnp.concatenate([other, mine], axis))


def prepare_kernel(cuts, pieces, place_ref, slab_ref, got_ref, *refs):
    outs, (own, sems) = refs[:-2], refs[-2:]
    zs, rows, part = own.shape
    z, core = place_ref[0], place_ref[1]

    def fetch(bits):
        at = pl.multiple_of(core * (zs * part) + (z ^ bits) * part, 128)
        return pltpu.make_async_copy(slab_ref.at[:, pl.ds(at, part)], own.at[bits], sems.at[bits])

    for bits, _, _ in cuts:
        fetch(bits).start()
    begin = 0
    for bits, from_, depth in cuts:
        fetch(bits).wait()
        for out, (which, start, width) in zip(outs, pieces):
            if which != bits:
                continue
            columns = slice(start, start + width)
            other = slice(begin + start - from_, begin + start - from_ + width)

            @pl.when(core == 0)
            def _():
                out[:rows, :] = own[bits, :, columns]
                out[rows:, :] = got_ref[:, other]

            @pl.when(core == 1)
            def _():
                out[:rows, :] = got_ref[:, other]
                out[rows:, :] = own[bits, :, columns]

        begin += depth


def prepare(place, slab, got, part, zs, cuts, pieces):
    rows = got.shape[0]
    vmem = pl.BlockSpec(memory_space=pltpu.VMEM)
    return pl.pallas_call(
        functools.partial(prepare_kernel, cuts, pieces),
        out_shape=[jax.ShapeDtypeStruct((2 * rows, width), jnp.float32) for _, _, width in pieces],
        in_specs=[pl.BlockSpec(memory_space=pltpu.SMEM), pl.BlockSpec(memory_space=pltpu.HBM), vmem],
        out_specs=[vmem] * len(pieces),
        scratch_shapes=[pltpu.VMEM((zs, rows, part), jnp.float32), pltpu.SemaphoreType.DMA((zs,))],
        compiler_params=pltpu.CompilerParams(vmem_limit_bytes=50 * 2**20),
        cost_estimate=pl.CostEstimate(flops=0, bytes_accessed=100_000_000, transcendentals=0),
        name="prepare",
    )(place, slab, got)


def split(x):
    high = x.astype(jnp.bfloat16)
    return high, (x - high.astype(jnp.float32)).astype(jnp.bfloat16)


def split3(x):
    high = x.astype(jnp.bfloat16)
    rest = x - high.astype(jnp.float32)
    middle = rest.astype(jnp.bfloat16)
    return high, middle, (rest - middle.astype(jnp.float32)).astype(jnp.bfloat16)


def contract(a, b, over_a, over_b):
    return lax.dot_general(a, b, (((over_a,), (over_b,)), ((), ())), preferred_element_type=jnp.float32)


def side_by_side(*parts):
    return jnp.concatenate(parts, 1)


def quarters(x):
    return (x[:128, :128] + x[128:, 128:]) + (x[:128, 128:] + x[128:, :128])


def layout(n):
    blocks, strip = n // 128, n % 128
    above, strips, at = [], [], 0
    for j in range(blocks):
        above.append(at)
        strips.append(at + 128 * j)
        at += 128 * j + strip
    folded = [at + 128 * k for k in range((blocks + 1) // 2)]
    diagonals = at + 128 * len(folded)
    corner = diagonals + 8
    if blocks % 2 and strip <= 64:
        return above, strips, folded, diagonals, folded[-1] + 128 - strip, -(-corner // 64) * 64
    return above, strips, folded, diagonals, corner, -(-(corner + strip) // 64) * 64


def square(op):
    return op(lax.broadcasted_iota(jnp.int32, (128, 128), 0), lax.broadcasted_iota(jnp.int32, (128, 128), 1))


def add_gram(starts, place_ref, blocks, whole, parts, packed, base):
    high_out, low_out, high_ref, low_ref, sems, *staged = parts
    zs = len(blocks)
    n, width = whole.shape
    deep = n // zs
    z = place_ref[0]

    def fetch(bits):
        source = blocks[bits].at[:, pl.ds(starts[bits], width)]
        target = staged[0].at[bits] if staged else whole.at[pl.ds(pl.multiple_of((z ^ bits) * deep, 8), deep)]
        return pltpu.make_async_copy(source, target, sems.at[2 + bits])

    fetches = [fetch(bits) for bits in range(zs)]
    for copy in fetches:
        copy.start()
    if base is not None:
        base_copy = pltpu.make_async_copy(base[0], base[1], sems.at[2 + zs])
        base_copy.start()
    for copy in fetches:
        copy.wait()
    for here in range(zs if staged else 0):

        @pl.when(z == here)
        def _():
            for bits in range(zs):
                whole[(here ^ bits) * deep : (here ^ bits) * deep + deep, :] = staged[0][bits]

    above, strips, folded, diagonals, corner, size = layout(n)
    edge = n // 128 * 128
    high_ref[...], low_ref[...] = split(whole[...])
    saves = [
        pltpu.make_async_copy(high_ref, high_out, sems.at[0]),
        pltpu.make_async_copy(low_ref, low_out, sems.at[1]),
    ]
    for save in saves:
        save.start()

    def product(r0, r1, c0, c1):
        def times(a, b):
            return lax.dot_general(a[r0:r1, :], b[c0:c1, :], (((1,), (1,)), ((), ())), preferred_element_type=jnp.float32)

        return times(high_ref, low_ref) + times(low_ref, high_ref) + times(high_ref, high_ref)

    def put(at, value):
        rows = slice(at, at + value.shape[0])
        packed[rows, :] = value if base is None else value + base[1][rows, :]

    if base is not None:
        base_copy.wait()
    squares = []
    for start in range(0, edge, 256):
        last = start + 256 >= edge
        stop = min(start + 256, edge)
        upper = product(0, n if last else stop, start, n if last else stop)
        for j in range(start // 128, stop // 128):
            columns = slice(128 * j - start, 128 * j - start + 128)
            if j:
                put(above[j], upper[: 128 * j, columns])
            squares.append(upper[128 * j : 128 * j + 128, columns])
    rest = jnp.zeros((0, 128), jnp.float32)
    if n > edge:
        strip = upper[:, edge - start :]
        for j, at in enumerate(strips):
            put(at, strip[128 * j : 128 * j + 128].T)
        rest = jnp.pad(strip[edge:], ((0, 0), (0, 128 - (n - edge))))
    diagonal_rows = jnp.zeros((8, 128), jnp.float32)
    row = lax.broadcasted_iota(jnp.int32, (8, 128), 0)
    for k, at in enumerate(folded):
        value = squares[2 * k]
        if 2 * k + 1 < len(squares):
            other = squares[2 * k + 1]
            value = jnp.where(square(jnp.less_equal), value, other)
            diagonal = jnp.sum(jnp.where(square(jnp.equal), other, 0.0), axis=0, keepdims=True)
            diagonal_rows = jnp.where(row == k, diagonal, diagonal_rows)
        elif corner < diagonals:
            value = jnp.where(square(jnp.less_equal), value, jnp.pad(rest, ((128 - (n - edge), 0), (0, 0))))
        put(at, value)
    put(diagonals, diagonal_rows)
    if n > edge and corner > diagonals:
        put(corner, rest)
    filled = diagonals + 8 if corner < diagonals else corner + n - edge
    if filled < size:
        packed[filled:size, :] = jnp.zeros((size - filled, 128), jnp.float32)
    for save in saves:
        save.wait()


def early_kernel(starts, place_ref, *refs):
    blocks, (packed, high_out, low_out, whole, *parts) = refs[: len(starts)], refs[len(starts) :]
    add_gram(starts, place_ref, blocks, whole, [high_out, low_out, *parts], packed, None)


def late_kernel(starts, place_ref, base_ref, *refs):
    blocks, (mine_ref, theirs_ref, high_out, low_out) = refs[: len(starts)], refs[len(starts) : len(starts) + 4]
    packed, base, whole, *parts = refs[len(starts) + 4 :]
    add_gram(starts, place_ref, blocks, whole, [high_out, low_out, *parts], packed, (base_ref, base))
    half = mine_ref.shape[0]
    core = place_ref[1]
    mine_ref[...] = packed[pl.ds(pl.multiple_of(core * half, 8), half), :]
    theirs_ref[...] = packed[pl.ds(pl.multiple_of((1 - core) * half, 8), half), :]


def gram_part(place, base, blocks, starts, width):
    zs, deep = len(blocks), blocks[0].shape[0]
    n = zs * deep
    size = layout(n)[-1]
    vmem, hbm = pl.BlockSpec(memory_space=pltpu.VMEM), pl.BlockSpec(memory_space=pltpu.HBM)
    parts = [jax.ShapeDtypeStruct((n, width), jnp.bfloat16)] * 2
    scratch = [pltpu.VMEM((n, width), jnp.float32)] + [pltpu.VMEM((n, width), jnp.bfloat16)] * 2
    scratch += [pltpu.SemaphoreType.DMA((3 + zs,))]
    scratch += [pltpu.VMEM((zs, deep, width), jnp.float32)] if deep % 8 else []
    if base is None:
        kernel, sums, first = early_kernel, [jax.ShapeDtypeStruct((size, 128), jnp.float32)], []
    else:
        half = jax.ShapeDtypeStruct((size // 2, 128), jnp.float32)
        kernel, sums, first = late_kernel, [half, half], [base]
        scratch = [pltpu.VMEM((size, 128), jnp.float32)] * 2 + scratch
    return pl.pallas_call(
        functools.partial(kernel, starts),
        out_shape=[*sums, *parts],
        in_specs=[pl.BlockSpec(memory_space=pltpu.SMEM)] + [hbm] * (len(first) + len(blocks)),
        out_specs=[vmem] * len(sums) + [hbm] * 2,
        scratch_shapes=scratch,
        compiler_params=pltpu.CompilerParams(vmem_limit_bytes=48 * 2**20),
        cost_estimate=pl.CostEstimate(flops=6 * n * n * width, bytes_accessed=8 * n * width, transcendentals=0),
        name="gram_early" if base is None else "gram_late",
    )(place, *first, *blocks)


def lower_inverse(small):
    n = small.shape[0]
    lanes = 128
    full = (8, lanes)
    col = lax.broadcasted_iota(jnp.int32, full, 1)
    row = lax.broadcasted_iota(jnp.int32, full, 0)
    left = [small[8 * i : 8 * i + 8, :] for i in range(n // 8)]
    right = [(col == row + 8 * i).astype(jnp.float32) for i in range(n // 8)]
    done = []
    for p in range(n // 8):
        at = 8 * p
        d = {(a, b): jnp.broadcast_to(left[p][a : a + 1, at + b : at + b + 1], full) for a in range(8) for b in range(a + 1)}
        lrow = [jnp.broadcast_to(left[p][k : k + 1, :], full) for k in range(8)]
        rrow = [jnp.broadcast_to(right[p][k : k + 1, :], full) for k in range(8)]
        low, scale, y, v = {}, [], [], []
        for b in range(8):
            scale.append(lax.rsqrt(d[b, b]))
            y.append(lrow[b] * scale[b])
            v.append(rrow[b] * scale[b])
            for a in range(b + 1, 8):
                low[a, b] = d[a, b] * scale[b]
            for a in range(b + 1, 8):
                for c in range(b + 1, a + 1):
                    d[a, c] = d[a, c] - low[a, b] * low[c, b]
                lrow[a] = lrow[a] - low[a, b] * y[b]
                rrow[a] = rrow[a] - low[a, b] * v[b]
        out = v[0]
        for m in range(1, 8):
            out = jnp.where(row == m, v[m], out)
        done.append(out)
        for i in range(p + 1, n // 8):
            c = [jnp.broadcast_to(left[i][:, at + k : at + k + 1], full) for k in range(8)]
            li, ri = left[i], right[i]
            for m in range(8):
                f = c[m] * scale[m]
                li = li - f * y[m]
                ri = ri - f * v[m]
                for k in range(m + 1, 8):
                    c[k] = c[k] - low[k, m] * f
            left[i], right[i] = li, ri
    return jnp.concatenate(done, 0)


def iterations_kernel(iters, zs, place_ref, mine_ref, other_ref, start_ref, *refs):
    kept, (factor_ref, *outs) = refs[:4], refs[4 : 5 + 2 * zs]
    packed, gram, high, low, columns_high, columns_low, share, sems = refs[5 + 2 * zs :]
    early = kept[0].shape[1]
    fetches = [
        pltpu.make_async_copy(kept[0], columns_high.at[:, :early], sems.at[0]),
        pltpu.make_async_copy(kept[1], columns_low.at[:, :early], sems.at[1]),
        pltpu.make_async_copy(kept[2], columns_high.at[:, early:], sems.at[2]),
        pltpu.make_async_copy(kept[3], columns_low.at[:, early:], sems.at[3]),
    ]
    for fetch in fetches:
        fetch.start()

    n = gram.shape[0]
    above, strips, folded, diagonals, corner, size = layout(n)
    edge = n // 128 * 128
    half = size // 2
    core = place_ref[1]
    packed[pl.ds(pl.multiple_of(core * half, 8), half), :] = mine_ref[...]
    packed[pl.ds(pl.multiple_of((1 - core) * half, 8), half), :] = other_ref[...]
    for j, (at, strip) in enumerate(zip(above, strips)):
        cols = slice(128 * j, 128 * j + 128)
        if j:
            gram[: 128 * j, cols] = packed[at : at + 128 * j, :]
        for i in range(j):
            gram[cols, 128 * i : 128 * i + 128] = packed[at + 128 * i : at + 128 * i + 128, :].T
        fold = packed[folded[j // 2] : folded[j // 2] + 128, :]
        if j % 2 == 0:
            gram[cols, cols] = jnp.where(square(jnp.less_equal), fold, fold.T)
        else:
            diagonal = packed[diagonals : diagonals + 8, :][j // 2 : j // 2 + 1, :]
            fold = jnp.where(square(jnp.greater), fold, fold.T)
            gram[cols, cols] = jnp.where(square(jnp.equal), diagonal, fold)
        if n > edge:
            gram[edge:, cols] = packed[strip : strip + n - edge, :]
            gram[cols, edge:] = packed[strip : strip + n - edge, :].T
    if n > edge:
        gram[edge:, edge:] = packed[corner : corner + n - edge, : n - edge]

    high[...], low[...] = split(gram[...])

    rank = start_ref.shape[0]
    x_high, x_low = split(jnp.pad(start_ref[...], ((0, 128 - rank), (0, 0))))
    both = contract(high[...], jnp.concatenate([x_high, x_low], 0), 1, 1)
    image = both[:, :128] + both[:, 128:] + contract(low[...], x_high, 1, 1)
    for step in range(iters):
        parts = split3(image)
        first = side_by_side(parts[0], parts[1])
        cross = contract(parts[0], parts[2], 0, 0)
        small = quarters(contract(first, first, 0, 0)) + (cross + cross.T)
        inverse = jnp.pad(lower_inverse(small[:rank]), ((0, 128 - rank), (0, 0)))
        inv = split3(inverse)
        if step < iters - 1:
            both = contract(high[...], first, 1, 0)
            image = both[:, :128] + both[:, 128:] + contract(low[...], parts[0], 1, 0)
            parts = split3(image)
            twice = [side_by_side(inv[0], inv[0]), side_by_side(inv[1], inv[1])]
            both = contract(side_by_side(parts[0], parts[1]), jnp.concatenate(twice, 0), 1, 1)
            last = contract(side_by_side(parts[0], parts[2]), side_by_side(inv[2], inv[0]), 1, 1)
            image = both[:, :128] + both[:, 128:] + last
        else:
            basis = contract(side_by_side(inv[0], inv[2]), side_by_side(parts[2], parts[0]), 1, 1)
            basis += contract(side_by_side(inv[0], inv[1]), side_by_side(parts[1], parts[1]), 1, 1)
            basis += contract(side_by_side(inv[0], inv[1]), side_by_side(parts[0], parts[0]), 1, 1)

    basis = basis[:rank]
    factor_ref[...] = basis
    basis_high, basis_low = split(basis)
    for fetch in fetches:
        fetch.wait()
    both = contract(jnp.concatenate([basis_high, basis_low], 0), columns_high[...], 1, 0)
    share[...] = both[:rank] + both[rank:] + contract(basis_high, columns_low[...], 1, 0)
    own, wide = outs[0].shape[0] // 2, outs[0].shape[1]
    for here in range(2 * zs):

        @pl.when(2 * place_ref[0] + place_ref[1] == here)
        def _():
            for bits, out in enumerate(outs):
                rows = slice(own * (here ^ bits), own * (here ^ bits) + own)
                out[:own, :] = share[rows, :wide]
                out[own:, :] = share[rows, wide:]


def iterations(place, mine, other, start, parts, iters, zs):
    rank, n = start.shape
    part = parts[0].shape[1] + parts[2].shape[1]
    vmem, hbm = pl.BlockSpec(memory_space=pltpu.VMEM), pl.BlockSpec(memory_space=pltpu.HBM)
    return pl.pallas_call(
        functools.partial(iterations_kernel, iters, zs),
        out_shape=[jax.ShapeDtypeStruct(start.shape, jnp.float32)]
        + [jax.ShapeDtypeStruct((rank // zs, part // 2), jnp.float32)] * (2 * zs),
        in_specs=[pl.BlockSpec(memory_space=pltpu.SMEM)] + [vmem] * 3 + [hbm] * 4,
        out_specs=[vmem] * (1 + 2 * zs),
        scratch_shapes=[pltpu.VMEM((layout(n)[-1], 128), jnp.float32), pltpu.VMEM((n, n), jnp.float32)]
        + [pltpu.VMEM((n, n), jnp.bfloat16)] * 2
        + [pltpu.VMEM((n, part), jnp.bfloat16)] * 2
        + [pltpu.VMEM((rank, part), jnp.float32), pltpu.SemaphoreType.DMA((4,))],
        compiler_params=pltpu.CompilerParams(vmem_limit_bytes=50 * 2**20),
        name="iterations",
    )(place, mine, other, start, *parts)


def farthest_first(size):
    return [size - 1, *range(1, size - 1)]


def mirrored(bits, rest):
    side = int(rest**0.5)
    return bits % side * side + bits // side if side * side == rest else bits


def swap_rest(x, fibre, rest, bits):
    other = mirrored(bits, rest)
    pairs = [(f * rest + r, f * rest + (r ^ (other if f % 2 else bits))) for f in range(fibre) for r in range(rest)]
    return lax.ppermute(x, ("fibre", "rest"), pairs)


def sum_everywhere(core, mine, theirs, fibre, rest):
    r = lax.axis_index("rest")
    half, width = mine.shape
    piece = -(-half // (8 * rest)) * 8
    mine = mine + swap(theirs, "fibre", fibre, 1)
    mine = jnp.pad(mine, ((0, piece * rest - half), (0, 0)))
    peers = {bits: r ^ jnp.where(core == 0, bits, mirrored(bits, rest)) for bits in farthest_first(rest)}
    total = lax.dynamic_slice(mine, (r * piece, 0), (piece, width))
    for bits, peer in peers.items():
        part = lax.dynamic_slice(mine, (peer * piece, 0), (piece, width))
        total = total + swap_rest(part, fibre, rest, bits)
    terms = {bits: swap(total, "fibre", fibre, 2 * bits) for bits in farthest_first(fibre // 2)}
    terms = [terms.get(bits, total) for bits in range(fibre // 2)]
    while len(terms) > 1:
        last = len(terms) - 1
        terms = [terms[i] + terms[last - i] for i in range(1, len(terms) // 2)] + [terms[last] + terms[0]]
    total = terms[0]
    out = lax.dynamic_update_slice(jnp.zeros((rest, piece, width), jnp.float32), total[None], (r, 0, 0))
    for bits, peer in peers.items():
        out = lax.dynamic_update_slice(out, swap_rest(total, fibre, rest, bits)[None], (peer, 0, 0))
    out = out.reshape(rest * piece, width)[:half]
    return out, swap(out, "fibre", fibre, 1)


def assemble_kernel(distances, place_ref, *refs):
    blocks, out_ref = refs[:-1], refs[-1]
    f = 2 * place_ref[0] + place_ref[1]
    own, wide = out_ref.shape[0], blocks[0].shape[1]
    half = out_ref.shape[1] // 2
    for bits, block in zip(distances, blocks):
        source = f ^ bits
        at = pl.multiple_of((source % 2) * half + (source // 2) * (2 * wide), 128)
        out_ref[:, pl.ds(at, wide)] = block[:own, :]
        out_ref[:, pl.ds(at + wide, wide)] = block[own:, :]


def assemble(place, moved, cols):
    blocks = list(moved.values())
    vmem = pl.BlockSpec(memory_space=pltpu.VMEM)
    return pl.pallas_call(
        functools.partial(assemble_kernel, tuple(moved)),
        out_shape=jax.ShapeDtypeStruct((blocks[0].shape[0] // 2, cols), jnp.float32),
        in_specs=[pl.BlockSpec(memory_space=pltpu.SMEM)] + [vmem] * len(blocks),
        out_specs=vmem,
        compiler_params=pltpu.CompilerParams(vmem_limit_bytes=24 * 2**20),
        name="assemble",
    )(place, *blocks)


def shards(fibre, rest, slab, start_basis):
    rows, cols = slab.shape
    zs = fibre // 2
    f = lax.axis_index("fibre")
    z, core = f // 2, f % 2
    place = jnp.stack([z, core])
    half = cols // 2
    part = half // zs
    early = part * 3 // 4

    def cut(slab, whose, bits, start, width):
        return lax.dynamic_slice(slab, (0, whose * half + (z ^ bits) * part + start), (rows, width))

    far = zs - 1
    theirs, mine = cut(slab, 1 - core, far, 0, part), cut(slab, core, far, 0, part)
    slab, theirs, mine = lax.optimization_barrier((slab, theirs, mine))
    cuts = [(bits, 0, part) for bits in range(far - 1, -1, -1)]
    others = jnp.concatenate([cut(slab, 1 - core, *c) for c in cuts], 1)
    block = in_order(core, mine, swap(theirs, "fibre", fibre, 1), 0)
    others, block = lax.optimization_barrier((others, block))
    arrived = {far: swap(block, "fibre", fibre, 2 * far)}
    got = swap(others, "fibre", fibre, 1)
    pieces = []
    for bits, start, width in cuts:
        split_here = bits > 1
        pieces += [(bits, 0, early), (bits, early, part - early)] if split_here else [(bits, start, width)]
    late = {}
    for (bits, start, _), block in zip(pieces, prepare(place, slab, got, part, zs, cuts, pieces)):
        if start:
            block, arrived[far] = lax.optimization_barrier((block, arrived[far]))
        into = late if start else arrived
        into[bits] = swap(block, "fibre", fibre, 2 * bits) if bits else block
    first = [arrived[bits] for bits in range(zs)]
    last = [late.get(bits, arrived[bits]) for bits in range(zs)]
    last_from = tuple(0 if bits in late else early for bits in range(zs))
    packed, *parts = gram_part(place, None, first, (0,) * zs, early)
    mine, theirs, *more = gram_part(place, packed, last, last_from, part - early)
    mine, other = sum_everywhere(core, mine, theirs, fibre, rest)
    factor, *blocks = iterations(place, mine, other, start_basis.T, [*parts, *more], ITERS, zs)
    order = [2 * bits + d for bits in farthest_first(zs) for d in range(2)]
    order.insert(2, 1)
    moved = {bits: swap(blocks[bits], "fibre", fibre, bits) for bits in order}
    moved[0] = blocks[0]
    return (factor.T, assemble(place, moved, cols))


def solution(mesh):
    fibre, rest = mesh.shape["fibre"], mesh.shape["rest"]
    return jax.shard_map(
        lambda slab, start_basis: shards(fibre, rest, slab, start_basis),
        mesh=mesh,
        in_specs=(P("fibre", "rest"), P()),
        out_specs=(P(), P("fibre", "rest")),
        check_vma=False,
    )
```

```python
import functools

import jax
import jax.numpy as jnp
from jax import lax
from jax.experimental import pallas as pl
from jax.experimental.pallas import tpu as pltpu
from jax.sharding import PartitionSpec as P

ITERS = 3


def swap(x, axis, size, bits):
    return lax.ppermute(x, axis, [(i, i ^ bits) for i in range(size)])


def in_order(core, mine, other, axis):
    return jnp.where(core == 0, jnp.concatenate([mine, other], axis), jnp.concatenate([other, mine], axis))


def prepare_kernel(cuts, pieces, place_ref, slab_ref, got_ref, *refs):
    outs, (own, sems) = refs[:-2], refs[-2:]
    zs, rows, part = own.shape
    z, core = place_ref[0], place_ref[1]

    def fetch(bits):
        at = pl.multiple_of(core * (zs * part) + (z ^ bits) * part, 128)
        return pltpu.make_async_copy(slab_ref.at[:, pl.ds(at, part)], own.at[bits], sems.at[bits])

    for bits, _, _ in cuts:
        fetch(bits).start()
    begin = 0
    for bits, from_, depth in cuts:
        fetch(bits).wait()
        for out, (which, start, width) in zip(outs, pieces):
            if which != bits:
                continue
            columns = slice(start, start + width)
            other = slice(begin + start - from_, begin + start - from_ + width)

            @pl.when(core == 0)
            def _():
                out[:rows, :] = own[bits, :, columns]
                out[rows:, :] = got_ref[:, other]

            @pl.when(core == 1)
            def _():
                out[:rows, :] = got_ref[:, other]
                out[rows:, :] = own[bits, :, columns]

        begin += depth


def prepare(place, slab, got, part, zs, cuts, pieces):
    rows = got.shape[0]
    vmem = pl.BlockSpec(memory_space=pltpu.VMEM)
    return pl.pallas_call(
        functools.partial(prepare_kernel, cuts, pieces),
        out_shape=[jax.ShapeDtypeStruct((2 * rows, width), jnp.float32) for _, _, width in pieces],
        in_specs=[pl.BlockSpec(memory_space=pltpu.SMEM), pl.BlockSpec(memory_space=pltpu.HBM), vmem],
        out_specs=[vmem] * len(pieces),
        scratch_shapes=[pltpu.VMEM((zs, rows, part), jnp.float32), pltpu.SemaphoreType.DMA((zs,))],
        compiler_params=pltpu.CompilerParams(vmem_limit_bytes=50 * 2**20),
        cost_estimate=pl.CostEstimate(flops=0, bytes_accessed=100_000_000, transcendentals=0),
        name="prepare",
    )(place, slab, got)


def split(x):
    high = x.astype(jnp.bfloat16)
    return high, (x - high.astype(jnp.float32)).astype(jnp.bfloat16)


def split3(x):
    high = x.astype(jnp.bfloat16)
    rest = x - high.astype(jnp.float32)
    middle = rest.astype(jnp.bfloat16)
    return high, middle, (rest - middle.astype(jnp.float32)).astype(jnp.bfloat16)


def contract(a, b, over_a, over_b):
    return lax.dot_general(a, b, (((over_a,), (over_b,)), ((), ())), preferred_element_type=jnp.float32)


def side_by_side(*parts):
    return jnp.concatenate(parts, 1)


def quarters(x):
    return (x[:128, :128] + x[128:, 128:]) + (x[:128, 128:] + x[128:, :128])


def layout(n):
    blocks, strip = n // 128, n % 128
    above, strips, at = [], [], 0
    for j in range(blocks):
        above.append(at)
        strips.append(at + 128 * j)
        at += 128 * j + strip
    folded = [at + 128 * k for k in range((blocks + 1) // 2)]
    diagonals = at + 128 * len(folded)
    corner = diagonals + 8
    if blocks % 2 and strip <= 64:
        return above, strips, folded, diagonals, folded[-1] + 128 - strip, -(-corner // 64) * 64
    return above, strips, folded, diagonals, corner, -(-(corner + strip) // 64) * 64


def square(op):
    return op(lax.broadcasted_iota(jnp.int32, (128, 128), 0), lax.broadcasted_iota(jnp.int32, (128, 128), 1))


def add_gram(starts, place_ref, blocks, whole, parts, packed, base):
    high_out, low_out, high_ref, low_ref, sems, *staged = parts
    zs = len(blocks)
    n, width = whole.shape
    deep = n // zs
    z = place_ref[0]

    def fetch(bits):
        source = blocks[bits].at[:, pl.ds(starts[bits], width)]
        target = staged[0].at[bits] if staged else whole.at[pl.ds(pl.multiple_of((z ^ bits) * deep, 8), deep)]
        return pltpu.make_async_copy(source, target, sems.at[2 + bits])

    fetches = [fetch(bits) for bits in range(zs)]
    for copy in fetches:
        copy.start()
    if base is not None:
        base_copy = pltpu.make_async_copy(base[0], base[1], sems.at[2 + zs])
        base_copy.start()
    for copy in fetches:
        copy.wait()
    for here in range(zs if staged else 0):

        @pl.when(z == here)
        def _():
            for bits in range(zs):
                whole[(here ^ bits) * deep : (here ^ bits) * deep + deep, :] = staged[0][bits]

    above, strips, folded, diagonals, corner, size = layout(n)
    edge = n // 128 * 128
    high_ref[...], low_ref[...] = split(whole[...])
    saves = [
        pltpu.make_async_copy(high_ref, high_out, sems.at[0]),
        pltpu.make_async_copy(low_ref, low_out, sems.at[1]),
    ]
    for save in saves:
        save.start()

    def product(r0, r1, c0, c1):
        def times(a, b):
            return lax.dot_general(a[r0:r1, :], b[c0:c1, :], (((1,), (1,)), ((), ())), preferred_element_type=jnp.float32)

        return times(high_ref, low_ref) + times(low_ref, high_ref) + times(high_ref, high_ref)

    def put(at, value):
        rows = slice(at, at + value.shape[0])
        packed[rows, :] = value if base is None else value + base[1][rows, :]

    if base is not None:
        base_copy.wait()
    squares = []
    for start in range(0, edge, 256):
        last = start + 256 >= edge
        stop = min(start + 256, edge)
        upper = product(0, n if last else stop, start, n if last else stop)
        for j in range(start // 128, stop // 128):
            columns = slice(128 * j - start, 128 * j - start + 128)
            if j:
                put(above[j], upper[: 128 * j, columns])
            squares.append(upper[128 * j : 128 * j + 128, columns])
    rest = jnp.zeros((0, 128), jnp.float32)
    if n > edge:
        strip = upper[:, edge - start :]
        for j, at in enumerate(strips):
            put(at, strip[128 * j : 128 * j + 128].T)
        rest = jnp.pad(strip[edge:], ((0, 0), (0, 128 - (n - edge))))
    diagonal_rows = jnp.zeros((8, 128), jnp.float32)
    row = lax.broadcasted_iota(jnp.int32, (8, 128), 0)
    for k, at in enumerate(folded):
        value = squares[2 * k]
        if 2 * k + 1 < len(squares):
            other = squares[2 * k + 1]
            value = jnp.where(square(jnp.less_equal), value, other)
            diagonal = jnp.sum(jnp.where(square(jnp.equal), other, 0.0), axis=0, keepdims=True)
            diagonal_rows = jnp.where(row == k, diagonal, diagonal_rows)
        elif corner < diagonals:
            value = jnp.where(square(jnp.less_equal), value, jnp.pad(rest, ((128 - (n - edge), 0), (0, 0))))
        put(at, value)
    put(diagonals, diagonal_rows)
    if n > edge and corner > diagonals:
        put(corner, rest)
    filled = diagonals + 8 if corner < diagonals else corner + n - edge
    if filled < size:
        packed[filled:size, :] = jnp.zeros((size - filled, 128), jnp.float32)
    for save in saves:
        save.wait()


def early_kernel(starts, place_ref, *refs):
    blocks, (packed, high_out, low_out, whole, *parts) = refs[: len(starts)], refs[len(starts) :]
    add_gram(starts, place_ref, blocks, whole, [high_out, low_out, *parts], packed, None)


def late_kernel(starts, place_ref, base_ref, *refs):
    blocks, (mine_ref, theirs_ref, high_out, low_out) = refs[: len(starts)], refs[len(starts) : len(starts) + 4]
    packed, base, whole, *parts = refs[len(starts) + 4 :]
    add_gram(starts, place_ref, blocks, whole, [high_out, low_out, *parts], packed, (base_ref, base))
    half = mine_ref.shape[0]
    core = place_ref[1]
    mine_ref[...] = packed[pl.ds(pl.multiple_of(core * half, 8), half), :]
    theirs_ref[...] = packed[pl.ds(pl.multiple_of((1 - core) * half, 8), half), :]


def gram_part(place, base, blocks, starts, width):
    zs, deep = len(blocks), blocks[0].shape[0]
    n = zs * deep
    size = layout(n)[-1]
    vmem, hbm = pl.BlockSpec(memory_space=pltpu.VMEM), pl.BlockSpec(memory_space=pltpu.HBM)
    parts = [jax.ShapeDtypeStruct((n, width), jnp.bfloat16)] * 2
    scratch = [pltpu.VMEM((n, width), jnp.float32)] + [pltpu.VMEM((n, width), jnp.bfloat16)] * 2
    scratch += [pltpu.SemaphoreType.DMA((3 + zs,))]
    scratch += [pltpu.VMEM((zs, deep, width), jnp.float32)] if deep % 8 else []
    if base is None:
        kernel, sums, first = early_kernel, [jax.ShapeDtypeStruct((size, 128), jnp.float32)], []
    else:
        half = jax.ShapeDtypeStruct((size // 2, 128), jnp.float32)
        kernel, sums, first = late_kernel, [half, half], [base]
        scratch = [pltpu.VMEM((size, 128), jnp.float32)] * 2 + scratch
    return pl.pallas_call(
        functools.partial(kernel, starts),
        out_shape=[*sums, *parts],
        in_specs=[pl.BlockSpec(memory_space=pltpu.SMEM)] + [hbm] * (len(first) + len(blocks)),
        out_specs=[vmem] * len(sums) + [hbm] * 2,
        scratch_shapes=scratch,
        compiler_params=pltpu.CompilerParams(vmem_limit_bytes=48 * 2**20),
        cost_estimate=pl.CostEstimate(flops=6 * n * n * width, bytes_accessed=8 * n * width, transcendentals=0),
        name="gram_early" if base is None else "gram_late",
    )(place, *first, *blocks)


def lower_inverse(small):
    n = small.shape[0]
    lanes = 128
    full = (8, lanes)
    col = lax.broadcasted_iota(jnp.int32, full, 1)
    row = lax.broadcasted_iota(jnp.int32, full, 0)
    left = [small[8 * i : 8 * i + 8, :] for i in range(n // 8)]
    right = [(col == row + 8 * i).astype(jnp.float32) for i in range(n // 8)]
    done = []
    for p in range(n // 8):
        at = 8 * p
        d = {(a, b): jnp.broadcast_to(left[p][a : a + 1, at + b : at + b + 1], full) for a in range(8) for b in range(a + 1)}
        lrow = [jnp.broadcast_to(left[p][k : k + 1, :], full) for k in range(8)]
        rrow = [jnp.broadcast_to(right[p][k : k + 1, :], full) for k in range(8)]
        low, scale, y, v = {}, [], [], []
        for b in range(8):
            scale.append(lax.rsqrt(d[b, b]))
            y.append(lrow[b] * scale[b])
            v.append(rrow[b] * scale[b])
            for a in range(b + 1, 8):
                low[a, b] = d[a, b] * scale[b]
            for a in range(b + 1, 8):
                for c in range(b + 1, a + 1):
                    d[a, c] = d[a, c] - low[a, b] * low[c, b]
                lrow[a] = lrow[a] - low[a, b] * y[b]
                rrow[a] = rrow[a] - low[a, b] * v[b]
        out = v[0]
        for m in range(1, 8):
            out = jnp.where(row == m, v[m], out)
        done.append(out)
        for i in range(p + 1, n // 8):
            c = [jnp.broadcast_to(left[i][:, at + k : at + k + 1], full) for k in range(8)]
            li, ri = left[i], right[i]
            for m in range(8):
                f = c[m] * scale[m]
                li = li - f * y[m]
                ri = ri - f * v[m]
                for k in range(m + 1, 8):
                    c[k] = c[k] - low[k, m] * f
            left[i], right[i] = li, ri
    return jnp.concatenate(done, 0)


def iterations_kernel(iters, zs, place_ref, mine_ref, other_ref, start_ref, *refs):
    kept, (factor_ref, *outs) = refs[:4], refs[4 : 5 + 2 * zs]
    packed, gram, high, low, columns_high, columns_low, share, sems = refs[5 + 2 * zs :]
    early = kept[0].shape[1]
    fetches = [
        pltpu.make_async_copy(kept[0], columns_high.at[:, :early], sems.at[0]),
        pltpu.make_async_copy(kept[1], columns_low.at[:, :early], sems.at[1]),
        pltpu.make_async_copy(kept[2], columns_high.at[:, early:], sems.at[2]),
        pltpu.make_async_copy(kept[3], columns_low.at[:, early:], sems.at[3]),
    ]
    for fetch in fetches:
        fetch.start()

    n = gram.shape[0]
    above, strips, folded, diagonals, corner, size = layout(n)
    edge = n // 128 * 128
    half = size // 2
    core = place_ref[1]
    packed[pl.ds(pl.multiple_of(core * half, 8), half), :] = mine_ref[...]
    packed[pl.ds(pl.multiple_of((1 - core) * half, 8), half), :] = other_ref[...]
    for j, (at, strip) in enumerate(zip(above, strips)):
        cols = slice(128 * j, 128 * j + 128)
        if j:
            gram[: 128 * j, cols] = packed[at : at + 128 * j, :]
        for i in range(j):
            gram[cols, 128 * i : 128 * i + 128] = packed[at + 128 * i : at + 128 * i + 128, :].T
        fold = packed[folded[j // 2] : folded[j // 2] + 128, :]
        if j % 2 == 0:
            gram[cols, cols] = jnp.where(square(jnp.less_equal), fold, fold.T)
        else:
            diagonal = packed[diagonals : diagonals + 8, :][j // 2 : j // 2 + 1, :]
            fold = jnp.where(square(jnp.greater), fold, fold.T)
            gram[cols, cols] = jnp.where(square(jnp.equal), diagonal, fold)
        if n > edge:
            gram[edge:, cols] = packed[strip : strip + n - edge, :]
            gram[cols, edge:] = packed[strip : strip + n - edge, :].T
    if n > edge:
        gram[edge:, edge:] = packed[corner : corner + n - edge, : n - edge]

    high[...], low[...] = split(gram[...])

    rank = start_ref.shape[0]
    x_high, x_low = split(jnp.pad(start_ref[...], ((0, 128 - rank), (0, 0))))
    both = contract(high[...], jnp.concatenate([x_high, x_low], 0), 1, 1)
    image = both[:, :128] + both[:, 128:] + contract(low[...], x_high, 1, 1)
    for step in range(iters):
        parts = split3(image)
        first = side_by_side(parts[0], parts[1])
        cross = contract(parts[0], parts[2], 0, 0)
        small = quarters(contract(first, first, 0, 0)) + (cross + cross.T)
        inverse = jnp.pad(lower_inverse(small[:rank]), ((0, 128 - rank), (0, 0)))
        inv = split3(inverse)
        if step < iters - 1:
            both = contract(high[...], first, 1, 0)
            image = both[:, :128] + both[:, 128:] + contract(low[...], parts[0], 1, 0)
            parts = split3(image)
            twice = [side_by_side(inv[0], inv[0]), side_by_side(inv[1], inv[1])]
            both = contract(side_by_side(parts[0], parts[1]), jnp.concatenate(twice, 0), 1, 1)
            last = contract(side_by_side(parts[0], parts[2]), side_by_side(inv[2], inv[0]), 1, 1)
            image = both[:, :128] + both[:, 128:] + last
        else:
            basis = contract(side_by_side(inv[0], inv[2]), side_by_side(parts[2], parts[0]), 1, 1)
            basis += contract(side_by_side(inv[0], inv[1]), side_by_side(parts[1], parts[1]), 1, 1)
            basis += contract(side_by_side(inv[0], inv[1]), side_by_side(parts[0], parts[0]), 1, 1)

    basis = basis[:rank]
    factor_ref[...] = basis
    basis_high, basis_low = split(basis)
    for fetch in fetches:
        fetch.wait()
    both = contract(jnp.concatenate([basis_high, basis_low], 0), columns_high[...], 1, 0)
    share[...] = both[:rank] + both[rank:] + contract(basis_high, columns_low[...], 1, 0)
    own, wide = outs[0].shape[0] // 2, outs[0].shape[1]
    for here in range(2 * zs):

        @pl.when(2 * place_ref[0] + place_ref[1] == here)
        def _():
            for bits, out in enumerate(outs):
                rows = slice(own * (here ^ bits), own * (here ^ bits) + own)
                out[:own, :] = share[rows, :wide]
                out[own:, :] = share[rows, wide:]


def iterations(place, mine, other, start, parts, iters, zs):
    rank, n = start.shape
    part = parts[0].shape[1] + parts[2].shape[1]
    vmem, hbm = pl.BlockSpec(memory_space=pltpu.VMEM), pl.BlockSpec(memory_space=pltpu.HBM)
    return pl.pallas_call(
        functools.partial(iterations_kernel, iters, zs),
        out_shape=[jax.ShapeDtypeStruct(start.shape, jnp.float32)]
        + [jax.ShapeDtypeStruct((rank // zs, part // 2), jnp.float32)] * (2 * zs),
        in_specs=[pl.BlockSpec(memory_space=pltpu.SMEM)] + [vmem] * 3 + [hbm] * 4,
        out_specs=[vmem] * (1 + 2 * zs),
        scratch_shapes=[pltpu.VMEM((layout(n)[-1], 128), jnp.float32), pltpu.VMEM((n, n), jnp.float32)]
        + [pltpu.VMEM((n, n), jnp.bfloat16)] * 2
        + [pltpu.VMEM((n, part), jnp.bfloat16)] * 2
        + [pltpu.VMEM((rank, part), jnp.float32), pltpu.SemaphoreType.DMA((4,))],
        compiler_params=pltpu.CompilerParams(vmem_limit_bytes=50 * 2**20),
        name="iterations",
    )(place, mine, other, start, *parts)


def farthest_first(size):
    return [size - 1, *range(1, size - 1)]


def mirrored(bits, rest):
    side = int(rest**0.5)
    return bits % side * side + bits // side if side * side == rest else bits


def swap_rest(x, fibre, rest, bits):
    other = mirrored(bits, rest)
    pairs = [(f * rest + r, f * rest + (r ^ (other if f % 2 else bits))) for f in range(fibre) for r in range(rest)]
    return lax.ppermute(x, ("fibre", "rest"), pairs)


def sum_everywhere(core, mine, theirs, fibre, rest):
    r = lax.axis_index("rest")
    half, width = mine.shape
    piece = -(-half // (8 * rest)) * 8
    mine = mine + swap(theirs, "fibre", fibre, 1)
    mine = jnp.pad(mine, ((0, piece * rest - half), (0, 0)))
    peers = {bits: r ^ jnp.where(core == 0, bits, mirrored(bits, rest)) for bits in farthest_first(rest)}
    out = jnp.zeros((rest, piece, width), jnp.float32)
    cut = -(-piece // 16) * 8
    for start, rows in ((0, cut), (cut, piece - cut)):
        total = lax.dynamic_slice(mine, (r * piece + start, 0), (rows, width))
        for bits, peer in peers.items():
            part = lax.dynamic_slice(mine, (peer * piece + start, 0), (rows, width))
            total = total + swap_rest(part, fibre, rest, bits)
        terms = {bits: swap(total, "fibre", fibre, 2 * bits) for bits in farthest_first(fibre // 2)}
        terms = [terms.get(bits, total) for bits in range(fibre // 2)]
        while len(terms) > 1:
            last = len(terms) - 1
            terms = [terms[i] + terms[last - i] for i in range(1, len(terms) // 2)] + [terms[last] + terms[0]]
        total = terms[0]
        out = lax.dynamic_update_slice(out, total[None], (r, start, 0))
        for bits, peer in peers.items():
            out = lax.dynamic_update_slice(out, swap_rest(total, fibre, rest, bits)[None], (peer, start, 0))
    out = out.reshape(rest * piece, width)[:half]
    return out, swap(out, "fibre", fibre, 1)


def assemble_kernel(distances, place_ref, *refs):
    blocks, out_ref = refs[:-1], refs[-1]
    f = 2 * place_ref[0] + place_ref[1]
    own, wide = out_ref.shape[0], blocks[0].shape[1]
    half = out_ref.shape[1] // 2
    for bits, block in zip(distances, blocks):
        source = f ^ bits
        at = pl.multiple_of((source % 2) * half + (source // 2) * (2 * wide), 128)
        out_ref[:, pl.ds(at, wide)] = block[:own, :]
        out_ref[:, pl.ds(at + wide, wide)] = block[own:, :]


def assemble(place, moved, cols):
    blocks = list(moved.values())
    vmem = pl.BlockSpec(memory_space=pltpu.VMEM)
    return pl.pallas_call(
        functools.partial(assemble_kernel, tuple(moved)),
        out_shape=jax.ShapeDtypeStruct((blocks[0].shape[0] // 2, cols), jnp.float32),
        in_specs=[pl.BlockSpec(memory_space=pltpu.SMEM)] + [vmem] * len(blocks),
        out_specs=vmem,
        compiler_params=pltpu.CompilerParams(vmem_limit_bytes=24 * 2**20),
        name="assemble",
    )(place, *blocks)


def shards(fibre, rest, slab, start_basis):
    rows, cols = slab.shape
    zs = fibre // 2
    f = lax.axis_index("fibre")
    z, core = f // 2, f % 2
    place = jnp.stack([z, core])
    half = cols // 2
    part = half // zs
    early = part * 3 // 4

    def cut(slab, whose, bits, start, width):
        return lax.dynamic_slice(slab, (0, whose * half + (z ^ bits) * part + start), (rows, width))

    far = zs - 1
    theirs, mine = cut(slab, 1 - core, far, 0, part), cut(slab, core, far, 0, part)
    slab, theirs, mine = lax.optimization_barrier((slab, theirs, mine))
    cuts = [(bits, 0, part) for bits in range(far - 1, -1, -1)]
    others = jnp.concatenate([cut(slab, 1 - core, *c) for c in cuts], 1)
    block = in_order(core, mine, swap(theirs, "fibre", fibre, 1), 0)
    others, block = lax.optimization_barrier((others, block))
    arrived = {far: swap(block, "fibre", fibre, 2 * far)}
    got = swap(others, "fibre", fibre, 1)
    pieces = []
    for bits, start, width in cuts:
        split_here = bits > 1
        pieces += [(bits, 0, early), (bits, early, part - early)] if split_here else [(bits, start, width)]
    late = {}
    for (bits, start, _), block in zip(pieces, prepare(place, slab, got, part, zs, cuts, pieces)):
        if start:
            block, arrived[far] = lax.optimization_barrier((block, arrived[far]))
        into = late if start else arrived
        into[bits] = swap(block, "fibre", fibre, 2 * bits) if bits else block
    first = [arrived[bits] for bits in range(zs)]
    last = [late.get(bits, arrived[bits]) for bits in range(zs)]
    last_from = tuple(0 if bits in late else early for bits in range(zs))
    packed, *parts = gram_part(place, None, first, (0,) * zs, early)
    mine, theirs, *more = gram_part(place, packed, last, last_from, part - early)
    mine, other = sum_everywhere(core, mine, theirs, fibre, rest)
    factor, *blocks = iterations(place, mine, other, start_basis.T, [*parts, *more], ITERS, zs)
    order = [2 * bits + d for bits in farthest_first(zs) for d in range(2)]
    order.insert(2, 1)
    moved = {bits: swap(blocks[bits], "fibre", fibre, bits) for bits in order}
    moved[0] = blocks[0]
    return (factor.T, assemble(place, moved, cols))


def solution(mesh):
    fibre, rest = mesh.shape["fibre"], mesh.shape["rest"]
    return jax.shard_map(
        lambda slab, start_basis: shards(fibre, rest, slab, start_basis),
        mesh=mesh,
        in_specs=(P("fibre", "rest"), P()),
        out_specs=(P(), P("fibre", "rest")),
        check_vma=False,
    )
```

```python
import functools

import jax
import jax.numpy as jnp
from jax import lax
from jax.experimental import pallas as pl
from jax.experimental.pallas import tpu as pltpu
from jax.sharding import PartitionSpec as P

ITERS = 3


def swap(x, axis, size, bits):
    return lax.ppermute(x, axis, [(i, i ^ bits) for i in range(size)])


def in_order(core, mine, other, axis):
    return jnp.where(core == 0, jnp.concatenate([mine, other], axis), jnp.concatenate([other, mine], axis))


def prepare_kernel(cuts, pieces, place_ref, slab_ref, got_ref, *refs):
    outs, (own, sems) = refs[:-2], refs[-2:]
    zs, rows, part = own.shape
    z, core = place_ref[0], place_ref[1]

    def fetch(bits):
        at = pl.multiple_of(core * (zs * part) + (z ^ bits) * part, 128)
        return pltpu.make_async_copy(slab_ref.at[:, pl.ds(at, part)], own.at[bits], sems.at[bits])

    for bits, _, _ in cuts:
        fetch(bits).start()
    begin = 0
    for bits, from_, depth in cuts:
        fetch(bits).wait()
        for out, (which, start, width) in zip(outs, pieces):
            if which != bits:
                continue
            columns = slice(start, start + width)
            other = slice(begin + start - from_, begin + start - from_ + width)

            @pl.when(core == 0)
            def _():
                out[:rows, :] = own[bits, :, columns]
                out[rows:, :] = got_ref[:, other]

            @pl.when(core == 1)
            def _():
                out[:rows, :] = got_ref[:, other]
                out[rows:, :] = own[bits, :, columns]

        begin += depth


def prepare(place, slab, got, part, zs, cuts, pieces):
    rows = got.shape[0]
    vmem = pl.BlockSpec(memory_space=pltpu.VMEM)
    return pl.pallas_call(
        functools.partial(prepare_kernel, cuts, pieces),
        out_shape=[jax.ShapeDtypeStruct((2 * rows, width), jnp.float32) for _, _, width in pieces],
        in_specs=[pl.BlockSpec(memory_space=pltpu.SMEM), pl.BlockSpec(memory_space=pltpu.HBM), vmem],
        out_specs=[vmem] * len(pieces),
        scratch_shapes=[pltpu.VMEM((zs, rows, part), jnp.float32), pltpu.SemaphoreType.DMA((zs,))],
        compiler_params=pltpu.CompilerParams(vmem_limit_bytes=50 * 2**20),
        cost_estimate=pl.CostEstimate(flops=0, bytes_accessed=100_000_000, transcendentals=0),
        name="prepare",
    )(place, slab, got)


def split(x):
    high = x.astype(jnp.bfloat16)
    return high, (x - high.astype(jnp.float32)).astype(jnp.bfloat16)


def split3(x):
    high = x.astype(jnp.bfloat16)
    rest = x - high.astype(jnp.float32)
    middle = rest.astype(jnp.bfloat16)
    return high, middle, (rest - middle.astype(jnp.float32)).astype(jnp.bfloat16)


def contract(a, b, over_a, over_b):
    return lax.dot_general(a, b, (((over_a,), (over_b,)), ((), ())), preferred_element_type=jnp.float32)


def side_by_side(*parts):
    return jnp.concatenate(parts, 1)


def quarters(x):
    return (x[:128, :128] + x[128:, 128:]) + (x[:128, 128:] + x[128:, :128])


def layout(n):
    blocks, strip = n // 128, n % 128
    above, strips, at = [], [], 0
    for j in range(blocks):
        above.append(at)
        strips.append(at + 128 * j)
        at += 128 * j + strip
    folded = [at + 128 * k for k in range((blocks + 1) // 2)]
    diagonals = at + 128 * len(folded)
    corner = diagonals + 8
    if blocks % 2 and strip <= 64:
        return above, strips, folded, diagonals, folded[-1] + 128 - strip, -(-corner // 64) * 64
    return above, strips, folded, diagonals, corner, -(-(corner + strip) // 64) * 64


def square(op):
    return op(lax.broadcasted_iota(jnp.int32, (128, 128), 0), lax.broadcasted_iota(jnp.int32, (128, 128), 1))


def add_gram(starts, place_ref, blocks, whole, parts, packed, base):
    high_out, low_out, high_ref, low_ref, sems, *staged = parts
    zs = len(blocks)
    n, width = whole.shape
    deep = n // zs
    z = place_ref[0]

    def fetch(bits):
        source = blocks[bits].at[:, pl.ds(starts[bits], width)]
        target = staged[0].at[bits] if staged else whole.at[pl.ds(pl.multiple_of((z ^ bits) * deep, 8), deep)]
        return pltpu.make_async_copy(source, target, sems.at[2 + bits])

    fetches = [fetch(bits) for bits in range(zs)]
    for copy in fetches:
        copy.start()
    if base is not None:
        base_copy = pltpu.make_async_copy(base[0], base[1], sems.at[2 + zs])
        base_copy.start()
    for copy in fetches:
        copy.wait()
    for here in range(zs if staged else 0):

        @pl.when(z == here)
        def _():
            for bits in range(zs):
                whole[(here ^ bits) * deep : (here ^ bits) * deep + deep, :] = staged[0][bits]

    above, strips, folded, diagonals, corner, size = layout(n)
    edge = n // 128 * 128
    high_ref[...], low_ref[...] = split(whole[...])
    saves = [
        pltpu.make_async_copy(high_ref, high_out, sems.at[0]),
        pltpu.make_async_copy(low_ref, low_out, sems.at[1]),
    ]
    for save in saves:
        save.start()

    def product(r0, r1, c0, c1):
        def times(a, b):
            return lax.dot_general(a[r0:r1, :], b[c0:c1, :], (((1,), (1,)), ((), ())), preferred_element_type=jnp.float32)

        return times(high_ref, low_ref) + times(low_ref, high_ref) + times(high_ref, high_ref)

    def put(at, value):
        rows = slice(at, at + value.shape[0])
        packed[rows, :] = value if base is None else value + base[1][rows, :]

    if base is not None:
        base_copy.wait()
    squares = []
    for start in range(0, edge, 256):
        last = start + 256 >= edge
        stop = min(start + 256, edge)
        upper = product(0, n if last else stop, start, n if last else stop)
        for j in range(start // 128, stop // 128):
            columns = slice(128 * j - start, 128 * j - start + 128)
            if j:
                put(above[j], upper[: 128 * j, columns])
            squares.append(upper[128 * j : 128 * j + 128, columns])
    rest = jnp.zeros((0, 128), jnp.float32)
    if n > edge:
        strip = upper[:, edge - start :]
        for j, at in enumerate(strips):
            put(at, strip[128 * j : 128 * j + 128].T)
        rest = jnp.pad(strip[edge:], ((0, 0), (0, 128 - (n - edge))))
    diagonal_rows = jnp.zeros((8, 128), jnp.float32)
    row = lax.broadcasted_iota(jnp.int32, (8, 128), 0)
    for k, at in enumerate(folded):
        value = squares[2 * k]
        if 2 * k + 1 < len(squares):
            other = squares[2 * k + 1]
            value = jnp.where(square(jnp.less_equal), value, other)
            diagonal = jnp.sum(jnp.where(square(jnp.equal), other, 0.0), axis=0, keepdims=True)
            diagonal_rows = jnp.where(row == k, diagonal, diagonal_rows)
        elif corner < diagonals:
            value = jnp.where(square(jnp.less_equal), value, jnp.pad(rest, ((128 - (n - edge), 0), (0, 0))))
        put(at, value)
    put(diagonals, diagonal_rows)
    if n > edge and corner > diagonals:
        put(corner, rest)
    filled = diagonals + 8 if corner < diagonals else corner + n - edge
    if filled < size:
        packed[filled:size, :] = jnp.zeros((size - filled, 128), jnp.float32)
    for save in saves:
        save.wait()


def early_kernel(starts, place_ref, *refs):
    blocks, (packed, high_out, low_out, whole, *parts) = refs[: len(starts)], refs[len(starts) :]
    add_gram(starts, place_ref, blocks, whole, [high_out, low_out, *parts], packed, None)


def late_kernel(starts, place_ref, base_ref, *refs):
    blocks, (mine_ref, theirs_ref, high_out, low_out) = refs[: len(starts)], refs[len(starts) : len(starts) + 4]
    packed, base, whole, *parts = refs[len(starts) + 4 :]
    add_gram(starts, place_ref, blocks, whole, [high_out, low_out, *parts], packed, (base_ref, base))
    half = mine_ref.shape[0]
    core = place_ref[1]
    mine_ref[...] = packed[pl.ds(pl.multiple_of(core * half, 8), half), :]
    theirs_ref[...] = packed[pl.ds(pl.multiple_of((1 - core) * half, 8), half), :]


def gram_part(place, base, blocks, starts, width):
    zs, deep = len(blocks), blocks[0].shape[0]
    n = zs * deep
    size = layout(n)[-1]
    vmem, hbm = pl.BlockSpec(memory_space=pltpu.VMEM), pl.BlockSpec(memory_space=pltpu.HBM)
    parts = [jax.ShapeDtypeStruct((n, width), jnp.bfloat16)] * 2
    scratch = [pltpu.VMEM((n, width), jnp.float32)] + [pltpu.VMEM((n, width), jnp.bfloat16)] * 2
    scratch += [pltpu.SemaphoreType.DMA((3 + zs,))]
    scratch += [pltpu.VMEM((zs, deep, width), jnp.float32)] if deep % 8 else []
    if base is None:
        kernel, sums, first = early_kernel, [jax.ShapeDtypeStruct((size, 128), jnp.float32)], []
    else:
        half = jax.ShapeDtypeStruct((size // 2, 128), jnp.float32)
        kernel, sums, first = late_kernel, [half, half], [base]
        scratch = [pltpu.VMEM((size, 128), jnp.float32)] * 2 + scratch
    return pl.pallas_call(
        functools.partial(kernel, starts),
        out_shape=[*sums, *parts],
        in_specs=[pl.BlockSpec(memory_space=pltpu.SMEM)] + [hbm] * (len(first) + len(blocks)),
        out_specs=[vmem] * len(sums) + [hbm] * 2,
        scratch_shapes=scratch,
        compiler_params=pltpu.CompilerParams(vmem_limit_bytes=48 * 2**20),
        cost_estimate=pl.CostEstimate(flops=6 * n * n * width, bytes_accessed=8 * n * width, transcendentals=0),
        name="gram_early" if base is None else "gram_late",
    )(place, *first, *blocks)


def lower_inverse(small):
    n = small.shape[0]
    lanes = 128
    full = (8, lanes)
    col = lax.broadcasted_iota(jnp.int32, full, 1)
    row = lax.broadcasted_iota(jnp.int32, full, 0)
    left = [small[8 * i : 8 * i + 8, :] for i in range(n // 8)]
    right = [(col == row + 8 * i).astype(jnp.float32) for i in range(n // 8)]
    done = []
    for p in range(n // 8):
        at = 8 * p
        d = {(a, b): jnp.broadcast_to(left[p][a : a + 1, at + b : at + b + 1], full) for a in range(8) for b in range(a + 1)}
        lrow = [jnp.broadcast_to(left[p][k : k + 1, :], full) for k in range(8)]
        rrow = [jnp.broadcast_to(right[p][k : k + 1, :], full) for k in range(8)]
        low, scale, y, v = {}, [], [], []
        for b in range(8):
            scale.append(lax.rsqrt(d[b, b]))
            y.append(lrow[b] * scale[b])
            v.append(rrow[b] * scale[b])
            for a in range(b + 1, 8):
                low[a, b] = d[a, b] * scale[b]
            for a in range(b + 1, 8):
                for c in range(b + 1, a + 1):
                    d[a, c] = d[a, c] - low[a, b] * low[c, b]
                lrow[a] = lrow[a] - low[a, b] * y[b]
                rrow[a] = rrow[a] - low[a, b] * v[b]
        out = v[0]
        for m in range(1, 8):
            out = jnp.where(row == m, v[m], out)
        done.append(out)
        for i in range(p + 1, n // 8):
            c = [jnp.broadcast_to(left[i][:, at + k : at + k + 1], full) for k in range(8)]
            li, ri = left[i], right[i]
            for m in range(8):
                f = c[m] * scale[m]
                li = li - f * y[m]
                ri = ri - f * v[m]
                for k in range(m + 1, 8):
                    c[k] = c[k] - low[k, m] * f
            left[i], right[i] = li, ri
    return jnp.concatenate(done, 0)


def iterations_kernel(iters, zs, place_ref, mine_ref, other_ref, start_ref, *refs):
    kept, (factor_ref, *outs) = refs[:4], refs[4 : 5 + 2 * zs]
    packed, gram, high, low, columns_high, columns_low, share, sems = refs[5 + 2 * zs :]
    early = kept[0].shape[1]
    fetches = [
        pltpu.make_async_copy(kept[0], columns_high.at[:, :early], sems.at[0]),
        pltpu.make_async_copy(kept[1], columns_low.at[:, :early], sems.at[1]),
        pltpu.make_async_copy(kept[2], columns_high.at[:, early:], sems.at[2]),
        pltpu.make_async_copy(kept[3], columns_low.at[:, early:], sems.at[3]),
    ]
    for fetch in fetches:
        fetch.start()

    n = gram.shape[0]
    above, strips, folded, diagonals, corner, size = layout(n)
    edge = n // 128 * 128
    half = size // 2
    core = place_ref[1]
    packed[pl.ds(pl.multiple_of(core * half, 8), half), :] = mine_ref[...]
    packed[pl.ds(pl.multiple_of((1 - core) * half, 8), half), :] = other_ref[...]
    for j, (at, strip) in enumerate(zip(above, strips)):
        cols = slice(128 * j, 128 * j + 128)
        if j:
            gram[: 128 * j, cols] = packed[at : at + 128 * j, :]
        for i in range(j):
            gram[cols, 128 * i : 128 * i + 128] = packed[at + 128 * i : at + 128 * i + 128, :].T
        fold = packed[folded[j // 2] : folded[j // 2] + 128, :]
        if j % 2 == 0:
            gram[cols, cols] = jnp.where(square(jnp.less_equal), fold, fold.T)
        else:
            diagonal = packed[diagonals : diagonals + 8, :][j // 2 : j // 2 + 1, :]
            fold = jnp.where(square(jnp.greater), fold, fold.T)
            gram[cols, cols] = jnp.where(square(jnp.equal), diagonal, fold)
        if n > edge:
            gram[edge:, cols] = packed[strip : strip + n - edge, :]
            gram[cols, edge:] = packed[strip : strip + n - edge, :].T
    if n > edge:
        gram[edge:, edge:] = packed[corner : corner + n - edge, : n - edge]

    high[...], low[...] = split(gram[...])

    rank = start_ref.shape[0]
    x_high, x_low = split(jnp.pad(start_ref[...], ((0, 128 - rank), (0, 0))))
    both = contract(high[...], jnp.concatenate([x_high, x_low], 0), 1, 1)
    image = both[:, :128] + both[:, 128:] + contract(low[...], x_high, 1, 1)
    for step in range(iters):
        parts = split3(image)
        first = side_by_side(parts[0], parts[1])
        cross = contract(parts[0], parts[2], 0, 0)
        small = quarters(contract(first, first, 0, 0)) + (cross + cross.T)
        inverse = jnp.pad(lower_inverse(small[:rank]), ((0, 128 - rank), (0, 0)))
        inv = split3(inverse)
        if step < iters - 1:
            both = contract(high[...], first, 1, 0)
            image = both[:, :128] + both[:, 128:] + contract(low[...], parts[0], 1, 0)
            parts = split3(image)
            twice = [side_by_side(inv[0], inv[0]), side_by_side(inv[1], inv[1])]
            both = contract(side_by_side(parts[0], parts[1]), jnp.concatenate(twice, 0), 1, 1)
            last = contract(side_by_side(parts[0], parts[2]), side_by_side(inv[2], inv[0]), 1, 1)
            image = both[:, :128] + both[:, 128:] + last
        else:
            basis = contract(side_by_side(inv[0], inv[2]), side_by_side(parts[2], parts[0]), 1, 1)
            basis += contract(side_by_side(inv[0], inv[1]), side_by_side(parts[1], parts[1]), 1, 1)
            basis += contract(side_by_side(inv[0], inv[1]), side_by_side(parts[0], parts[0]), 1, 1)

    basis = basis[:rank]
    factor_ref[...] = basis
    basis_high, basis_low = split(basis)
    for fetch in fetches:
        fetch.wait()
    both = contract(jnp.concatenate([basis_high, basis_low], 0), columns_high[...], 1, 0)
    share[...] = both[:rank] + both[rank:] + contract(basis_high, columns_low[...], 1, 0)
    own, wide = outs[0].shape[0] // 2, outs[0].shape[1]
    for here in range(2 * zs):

        @pl.when(2 * place_ref[0] + place_ref[1] == here)
        def _():
            for bits, out in enumerate(outs):
                rows = slice(own * (here ^ bits), own * (here ^ bits) + own)
                out[:own, :] = share[rows, :wide]
                out[own:, :] = share[rows, wide:]


def iterations(place, mine, other, start, parts, iters, zs):
    rank, n = start.shape
    part = parts[0].shape[1] + parts[2].shape[1]
    vmem, hbm = pl.BlockSpec(memory_space=pltpu.VMEM), pl.BlockSpec(memory_space=pltpu.HBM)
    return pl.pallas_call(
        functools.partial(iterations_kernel, iters, zs),
        out_shape=[jax.ShapeDtypeStruct(start.shape, jnp.float32)]
        + [jax.ShapeDtypeStruct((rank // zs, part // 2), jnp.float32)] * (2 * zs),
        in_specs=[pl.BlockSpec(memory_space=pltpu.SMEM)] + [vmem] * 3 + [hbm] * 4,
        out_specs=[vmem] * (1 + 2 * zs),
        scratch_shapes=[pltpu.VMEM((layout(n)[-1], 128), jnp.float32), pltpu.VMEM((n, n), jnp.float32)]
        + [pltpu.VMEM((n, n), jnp.bfloat16)] * 2
        + [pltpu.VMEM((n, part), jnp.bfloat16)] * 2
        + [pltpu.VMEM((rank, part), jnp.float32), pltpu.SemaphoreType.DMA((4,))],
        compiler_params=pltpu.CompilerParams(vmem_limit_bytes=50 * 2**20),
        name="iterations",
    )(place, mine, other, start, *parts)


def farthest_first(size):
    return [size - 1, *range(1, size - 1)]


def mirrored(bits, rest):
    side = int(rest**0.5)
    return bits % side * side + bits // side if side * side == rest else bits


def swap_rest(x, fibre, rest, bits):
    other = mirrored(bits, rest)
    pairs = [(f * rest + r, f * rest + (r ^ (other if f % 2 else bits))) for f in range(fibre) for r in range(rest)]
    return lax.ppermute(x, ("fibre", "rest"), pairs)


def sum_everywhere(core, mine, theirs, fibre, rest):
    r = lax.axis_index("rest")
    half, width = mine.shape
    piece = -(-half // (8 * rest)) * 8
    mine = mine + swap(theirs, "fibre", fibre, 1)
    mine = jnp.pad(mine, ((0, piece * rest - half), (0, 0)))
    peers = {bits: r ^ jnp.where(core == 0, bits, mirrored(bits, rest)) for bits in farthest_first(rest)}
    total = lax.dynamic_slice(mine, (r * piece, 0), (piece, width))
    for bits, peer in peers.items():
        part = lax.dynamic_slice(mine, (peer * piece, 0), (piece, width))
        total = total + swap_rest(part, fibre, rest, bits)
    terms = {bits: swap(total, "fibre", fibre, 2 * bits) for bits in farthest_first(fibre // 2)}
    terms = [terms.get(bits, total) for bits in range(fibre // 2)]
    while len(terms) > 1:
        last = len(terms) - 1
        terms = [terms[i] + terms[last - i] for i in range(1, len(terms) // 2)] + [terms[last] + terms[0]]
    total = terms[0]
    out = lax.dynamic_update_slice(jnp.zeros((rest, piece, width), jnp.float32), total[None], (r, 0, 0))
    for bits, peer in peers.items():
        out = lax.dynamic_update_slice(out, swap_rest(total, fibre, rest, bits)[None], (peer, 0, 0))
    out = out.reshape(rest * piece, width)[:half]
    return out, swap(out, "fibre", fibre, 1)


def assemble_kernel(distances, place_ref, *refs):
    blocks, out_ref = refs[:-1], refs[-1]
    f = 2 * place_ref[0] + place_ref[1]
    own, wide = out_ref.shape[0], blocks[0].shape[1]
    half = out_ref.shape[1] // 2
    for bits, block in zip(distances, blocks):
        source = f ^ bits
        at = pl.multiple_of((source % 2) * half + (source // 2) * (2 * wide), 128)
        out_ref[:, pl.ds(at, wide)] = block[:own, :]
        out_ref[:, pl.ds(at + wide, wide)] = block[own:, :]


def assemble(place, moved, cols):
    blocks = list(moved.values())
    vmem = pl.BlockSpec(memory_space=pltpu.VMEM)
    return pl.pallas_call(
        functools.partial(assemble_kernel, tuple(moved)),
        out_shape=jax.ShapeDtypeStruct((blocks[0].shape[0] // 2, cols), jnp.float32),
        in_specs=[pl.BlockSpec(memory_space=pltpu.SMEM)] + [vmem] * len(blocks),
        out_specs=vmem,
        compiler_params=pltpu.CompilerParams(vmem_limit_bytes=24 * 2**20),
        name="assemble",
    )(place, *blocks)


def shards(fibre, rest, slab, start_basis):
    rows, cols = slab.shape
    zs = fibre // 2
    f = lax.axis_index("fibre")
    z, core = f // 2, f % 2
    place = jnp.stack([z, core])
    half = cols // 2
    part = half // zs
    early = part * 3 // 4

    def cut(slab, whose, bits, start, width):
        return lax.dynamic_slice(slab, (0, whose * half + (z ^ bits) * part + start), (rows, width))

    far = zs - 1
    theirs, mine = cut(slab, 1 - core, far, 0, part), cut(slab, core, far, 0, part)
    slab, theirs, mine = lax.optimization_barrier((slab, theirs, mine))
    cuts = [(bits, 0, part) for bits in range(far - 1, -1, -1)]
    others = jnp.concatenate([cut(slab, 1 - core, *c) for c in cuts], 1)
    block = in_order(core, mine, swap(theirs, "fibre", fibre, 1), 0)
    others, block = lax.optimization_barrier((others, block))
    arrived = {far: swap(block, "fibre", fibre, 2 * far)}
    got = swap(others, "fibre", fibre, 1)
    pieces = []
    for bits, start, width in cuts:
        split_here = bits > 1
        pieces += [(bits, 0, early), (bits, early, part - early)] if split_here else [(bits, start, width)]
    late = {}
    for (bits, start, _), block in zip(pieces, prepare(place, slab, got, part, zs, cuts, pieces)):
        if start:
            block, arrived[far] = lax.optimization_barrier((block, arrived[far]))
        into = late if start else arrived
        into[bits] = swap(block, "fibre", fibre, 2 * bits) if bits else block
    first = [arrived[bits] for bits in range(zs)]
    last = [late.get(bits, arrived[bits]) for bits in range(zs)]
    last_from = tuple(0 if bits in late else early for bits in range(zs))
    packed, *parts = gram_part(place, None, first, (0,) * zs, early)
    mine, theirs, *more = gram_part(place, packed, last, last_from, part - early)
    mine, other = sum_everywhere(core, mine, theirs, fibre, rest)
    factor, *blocks = iterations(place, mine, other, start_basis.T, [*parts, *more], ITERS, zs)
    order = [2 * bits + d for bits in farthest_first(zs) for d in range(2)]
    order.append(1)
    moved = {bits: swap(blocks[bits], "fibre", fibre, bits) for bits in order}
    moved[0] = blocks[0]
    return (factor.T, assemble(place, moved, cols))


def solution(mesh):
    fibre, rest = mesh.shape["fibre"], mesh.shape["rest"]
    return jax.shard_map(
        lambda slab, start_basis: shards(fibre, rest, slab, start_basis),
        mesh=mesh,
        in_specs=(P("fibre", "rest"), P()),
        out_specs=(P(), P("fibre", "rest")),
        check_vma=False,
    )
```

```python
import functools

import jax
import jax.numpy as jnp
from jax import lax
from jax.experimental import pallas as pl
from jax.experimental.pallas import tpu as pltpu
from jax.sharding import PartitionSpec as P

ITERS = 3


def swap(x, axis, size, bits):
    return lax.ppermute(x, axis, [(i, i ^ bits) for i in range(size)])


def in_order(core, mine, other, axis):
    return jnp.where(core == 0, jnp.concatenate([mine, other], axis), jnp.concatenate([other, mine], axis))


def prepare_kernel(cuts, pieces, place_ref, slab_ref, got_ref, *refs):
    outs, (own, sems) = refs[:-2], refs[-2:]
    zs, rows, part = own.shape
    z, core = place_ref[0], place_ref[1]

    def fetch(bits):
        at = pl.multiple_of(core * (zs * part) + (z ^ bits) * part, 128)
        return pltpu.make_async_copy(slab_ref.at[:, pl.ds(at, part)], own.at[bits], sems.at[bits])

    for bits, _, _ in cuts:
        fetch(bits).start()
    begin = 0
    for bits, from_, depth in cuts:
        fetch(bits).wait()
        for out, (which, start, width) in zip(outs, pieces):
            if which != bits:
                continue
            columns = slice(start, start + width)
            other = slice(begin + start - from_, begin + start - from_ + width)

            @pl.when(core == 0)
            def _():
                out[:rows, :] = own[bits, :, columns]
                out[rows:, :] = got_ref[:, other]

            @pl.when(core == 1)
            def _():
                out[:rows, :] = got_ref[:, other]
                out[rows:, :] = own[bits, :, columns]

        begin += depth


def prepare(place, slab, got, part, zs, cuts, pieces):
    rows = got.shape[0]
    vmem = pl.BlockSpec(memory_space=pltpu.VMEM)
    return pl.pallas_call(
        functools.partial(prepare_kernel, cuts, pieces),
        out_shape=[jax.ShapeDtypeStruct((2 * rows, width), jnp.float32) for _, _, width in pieces],
        in_specs=[pl.BlockSpec(memory_space=pltpu.SMEM), pl.BlockSpec(memory_space=pltpu.HBM), vmem],
        out_specs=[vmem] * len(pieces),
        scratch_shapes=[pltpu.VMEM((zs, rows, part), jnp.float32), pltpu.SemaphoreType.DMA((zs,))],
        compiler_params=pltpu.CompilerParams(vmem_limit_bytes=50 * 2**20),
        cost_estimate=pl.CostEstimate(flops=0, bytes_accessed=100_000_000, transcendentals=0),
        name="prepare",
    )(place, slab, got)


def split(x):
    high = x.astype(jnp.bfloat16)
    return high, (x - high.astype(jnp.float32)).astype(jnp.bfloat16)


def split3(x):
    high = x.astype(jnp.bfloat16)
    rest = x - high.astype(jnp.float32)
    middle = rest.astype(jnp.bfloat16)
    return high, middle, (rest - middle.astype(jnp.float32)).astype(jnp.bfloat16)


def contract(a, b, over_a, over_b):
    return lax.dot_general(a, b, (((over_a,), (over_b,)), ((), ())), preferred_element_type=jnp.float32)


def side_by_side(*parts):
    return jnp.concatenate(parts, 1)


def quarters(x):
    return (x[:128, :128] + x[128:, 128:]) + (x[:128, 128:] + x[128:, :128])


def layout(n):
    blocks, strip = n // 128, n % 128
    above, strips, at = [], [], 0
    for j in range(blocks):
        above.append(at)
        strips.append(at + 128 * j)
        at += 128 * j + strip
    folded = [at + 128 * k for k in range((blocks + 1) // 2)]
    diagonals = at + 128 * len(folded)
    corner = diagonals + 8
    if blocks % 2 and strip <= 64:
        return above, strips, folded, diagonals, folded[-1] + 128 - strip, -(-corner // 64) * 64
    return above, strips, folded, diagonals, corner, -(-(corner + strip) // 64) * 64


def square(op):
    return op(lax.broadcasted_iota(jnp.int32, (128, 128), 0), lax.broadcasted_iota(jnp.int32, (128, 128), 1))


def add_gram(starts, place_ref, blocks, whole, parts, packed, base):
    high_out, low_out, high_ref, low_ref, sems, *staged = parts
    zs = len(blocks)
    n, width = whole.shape
    deep = n // zs
    z = place_ref[0]

    def fetch(bits):
        source = blocks[bits].at[:, pl.ds(starts[bits], width)]
        target = staged[0].at[bits] if staged else whole.at[pl.ds(pl.multiple_of((z ^ bits) * deep, 8), deep)]
        return pltpu.make_async_copy(source, target, sems.at[2 + bits])

    fetches = [fetch(bits) for bits in range(zs)]
    for copy in fetches:
        copy.start()
    if base is not None:
        base_copy = pltpu.make_async_copy(base[0], base[1], sems.at[2 + zs])
        base_copy.start()
    for copy in fetches:
        copy.wait()
    for here in range(zs if staged else 0):

        @pl.when(z == here)
        def _():
            for bits in range(zs):
                whole[(here ^ bits) * deep : (here ^ bits) * deep + deep, :] = staged[0][bits]

    above, strips, folded, diagonals, corner, size = layout(n)
    edge = n // 128 * 128
    high_ref[...], low_ref[...] = split(whole[...])
    saves = [
        pltpu.make_async_copy(high_ref, high_out, sems.at[0]),
        pltpu.make_async_copy(low_ref, low_out, sems.at[1]),
    ]
    for save in saves:
        save.start()

    def product(r0, r1, c0, c1):
        def times(a, b):
            return lax.dot_general(a[r0:r1, :], b[c0:c1, :], (((1,), (1,)), ((), ())), preferred_element_type=jnp.float32)

        return times(high_ref, low_ref) + times(low_ref, high_ref) + times(high_ref, high_ref)

    def put(at, value):
        rows = slice(at, at + value.shape[0])
        packed[rows, :] = value if base is None else value + base[1][rows, :]

    if base is not None:
        base_copy.wait()
    squares = []
    for start in range(0, edge, 256):
        last = start + 256 >= edge
        stop = min(start + 256, edge)
        upper = product(0, n if last else stop, start, n if last else stop)
        for j in range(start // 128, stop // 128):
            columns = slice(128 * j - start, 128 * j - start + 128)
            if j:
                put(above[j], upper[: 128 * j, columns])
            squares.append(upper[128 * j : 128 * j + 128, columns])
    rest = jnp.zeros((0, 128), jnp.float32)
    if n > edge:
        strip = upper[:, edge - start :]
        for j, at in enumerate(strips):
            put(at, strip[128 * j : 128 * j + 128].T)
        rest = jnp.pad(strip[edge:], ((0, 0), (0, 128 - (n - edge))))
    diagonal_rows = jnp.zeros((8, 128), jnp.float32)
    row = lax.broadcasted_iota(jnp.int32, (8, 128), 0)
    for k, at in enumerate(folded):
        value = squares[2 * k]
        if 2 * k + 1 < len(squares):
            other = squares[2 * k + 1]
            value = jnp.where(square(jnp.less_equal), value, other)
            diagonal = jnp.sum(jnp.where(square(jnp.equal), other, 0.0), axis=0, keepdims=True)
            diagonal_rows = jnp.where(row == k, diagonal, diagonal_rows)
        elif corner < diagonals:
            value = jnp.where(square(jnp.less_equal), value, jnp.pad(rest, ((128 - (n - edge), 0), (0, 0))))
        put(at, value)
    put(diagonals, diagonal_rows)
    if n > edge and corner > diagonals:
        put(corner, rest)
    filled = diagonals + 8 if corner < diagonals else corner + n - edge
    if filled < size:
        packed[filled:size, :] = jnp.zeros((size - filled, 128), jnp.float32)
    for save in saves:
        save.wait()


def early_kernel(starts, place_ref, *refs):
    blocks, (packed, high_out, low_out, whole, *parts) = refs[: len(starts)], refs[len(starts) :]
    add_gram(starts, place_ref, blocks, whole, [high_out, low_out, *parts], packed, None)


def late_kernel(starts, place_ref, base_ref, *refs):
    blocks, (mine_ref, theirs_ref, high_out, low_out) = refs[: len(starts)], refs[len(starts) : len(starts) + 4]
    packed, base, whole, *parts = refs[len(starts) + 4 :]
    add_gram(starts, place_ref, blocks, whole, [high_out, low_out, *parts], packed, (base_ref, base))
    half = mine_ref.shape[0]
    core = place_ref[1]
    mine_ref[...] = packed[pl.ds(pl.multiple_of(core * half, 8), half), :]
    theirs_ref[...] = packed[pl.ds(pl.multiple_of((1 - core) * half, 8), half), :]


def gram_part(place, base, blocks, starts, width):
    zs, deep = len(blocks), blocks[0].shape[0]
    n = zs * deep
    size = layout(n)[-1]
    vmem, hbm = pl.BlockSpec(memory_space=pltpu.VMEM), pl.BlockSpec(memory_space=pltpu.HBM)
    parts = [jax.ShapeDtypeStruct((n, width), jnp.bfloat16)] * 2
    scratch = [pltpu.VMEM((n, width), jnp.float32)] + [pltpu.VMEM((n, width), jnp.bfloat16)] * 2
    scratch += [pltpu.SemaphoreType.DMA((3 + zs,))]
    scratch += [pltpu.VMEM((zs, deep, width), jnp.float32)] if deep % 8 else []
    if base is None:
        kernel, sums, first = early_kernel, [jax.ShapeDtypeStruct((size, 128), jnp.float32)], []
    else:
        half = jax.ShapeDtypeStruct((size // 2, 128), jnp.float32)
        kernel, sums, first = late_kernel, [half, half], [base]
        scratch = [pltpu.VMEM((size, 128), jnp.float32)] * 2 + scratch
    return pl.pallas_call(
        functools.partial(kernel, starts),
        out_shape=[*sums, *parts],
        in_specs=[pl.BlockSpec(memory_space=pltpu.SMEM)] + [hbm] * (len(first) + len(blocks)),
        out_specs=[vmem] * len(sums) + [hbm] * 2,
        scratch_shapes=scratch,
        compiler_params=pltpu.CompilerParams(vmem_limit_bytes=48 * 2**20),
        cost_estimate=pl.CostEstimate(flops=6 * n * n * width, bytes_accessed=8 * n * width, transcendentals=0),
        name="gram_early" if base is None else "gram_late",
    )(place, *first, *blocks)


def lower_inverse(small):
    n = small.shape[0]
    lanes = 128
    full = (8, lanes)
    col = lax.broadcasted_iota(jnp.int32, full, 1)
    row = lax.broadcasted_iota(jnp.int32, full, 0)
    left = [small[8 * i : 8 * i + 8, :] for i in range(n // 8)]
    right = [(col == row + 8 * i).astype(jnp.float32) for i in range(n // 8)]
    done = []
    for p in range(n // 8):
        at = 8 * p
        d = {(a, b): jnp.broadcast_to(left[p][a : a + 1, at + b : at + b + 1], full) for a in range(8) for b in range(a + 1)}
        lrow = [jnp.broadcast_to(left[p][k : k + 1, :], full) for k in range(8)]
        rrow = [jnp.broadcast_to(right[p][k : k + 1, :], full) for k in range(8)]
        low, scale, y, v = {}, [], [], []
        for b in range(8):
            scale.append(lax.rsqrt(d[b, b]))
            y.append(lrow[b] * scale[b])
            v.append(rrow[b] * scale[b])
            for a in range(b + 1, 8):
                low[a, b] = d[a, b] * scale[b]
            for a in range(b + 1, 8):
                for c in range(b + 1, a + 1):
                    d[a, c] = d[a, c] - low[a, b] * low[c, b]
                lrow[a] = lrow[a] - low[a, b] * y[b]
                rrow[a] = rrow[a] - low[a, b] * v[b]
        out = v[0]
        for m in range(1, 8):
            out = jnp.where(row == m, v[m], out)
        done.append(out)
        for i in range(p + 1, n // 8):
            c = [jnp.broadcast_to(left[i][:, at + k : at + k + 1], full) for k in range(8)]
            li, ri = left[i], right[i]
            for m in range(8):
                f = c[m] * scale[m]
                li = li - f * y[m]
                ri = ri - f * v[m]
                for k in range(m + 1, 8):
                    c[k] = c[k] - low[k, m] * f
            left[i], right[i] = li, ri
    return jnp.concatenate(done, 0)


def iterations_kernel(iters, zs, place_ref, mine_ref, other_ref, start_ref, *refs):
    kept, (factor_ref, *outs) = refs[:4], refs[4 : 5 + 2 * zs]
    packed, gram, high, low, columns_high, columns_low, share, sems = refs[5 + 2 * zs :]
    early = kept[0].shape[1]
    fetches = [
        pltpu.make_async_copy(kept[0], columns_high.at[:, :early], sems.at[0]),
        pltpu.make_async_copy(kept[1], columns_low.at[:, :early], sems.at[1]),
        pltpu.make_async_copy(kept[2], columns_high.at[:, early:], sems.at[2]),
        pltpu.make_async_copy(kept[3], columns_low.at[:, early:], sems.at[3]),
    ]
    for fetch in fetches:
        fetch.start()

    n = gram.shape[0]
    above, strips, folded, diagonals, corner, size = layout(n)
    edge = n // 128 * 128
    half = size // 2
    core = place_ref[1]
    packed[pl.ds(pl.multiple_of(core * half, 8), half), :] = mine_ref[...]
    packed[pl.ds(pl.multiple_of((1 - core) * half, 8), half), :] = other_ref[...]
    for j, (at, strip) in enumerate(zip(above, strips)):
        cols = slice(128 * j, 128 * j + 128)
        if j:
            gram[: 128 * j, cols] = packed[at : at + 128 * j, :]
        for i in range(j):
            gram[cols, 128 * i : 128 * i + 128] = packed[at + 128 * i : at + 128 * i + 128, :].T
        fold = packed[folded[j // 2] : folded[j // 2] + 128, :]
        if j % 2 == 0:
            gram[cols, cols] = jnp.where(square(jnp.less_equal), fold, fold.T)
        else:
            diagonal = packed[diagonals : diagonals + 8, :][j // 2 : j // 2 + 1, :]
            fold = jnp.where(square(jnp.greater), fold, fold.T)
            gram[cols, cols] = jnp.where(square(jnp.equal), diagonal, fold)
        if n > edge:
            gram[edge:, cols] = packed[strip : strip + n - edge, :]
            gram[cols, edge:] = packed[strip : strip + n - edge, :].T
    if n > edge:
        gram[edge:, edge:] = packed[corner : corner + n - edge, : n - edge]

    high[...], low[...] = split(gram[...])

    rank = start_ref.shape[0]
    x_high, x_low = split(jnp.pad(start_ref[...], ((0, 128 - rank), (0, 0))))
    both = contract(high[...], jnp.concatenate([x_high, x_low], 0), 1, 1)
    image = both[:, :128] + both[:, 128:] + contract(low[...], x_high, 1, 1)
    for step in range(iters):
        parts = split3(image)
        first = side_by_side(parts[0], parts[1])
        cross = contract(parts[0], parts[2], 0, 0)
        small = quarters(contract(first, first, 0, 0)) + (cross + cross.T)
        inverse = jnp.pad(lower_inverse(small[:rank]), ((0, 128 - rank), (0, 0)))
        inv = split3(inverse)
        if step < iters - 1:
            both = contract(high[...], first, 1, 0)
            image = both[:, :128] + both[:, 128:] + contract(low[...], parts[0], 1, 0)
            parts = split3(image)
            twice = [side_by_side(inv[0], inv[0]), side_by_side(inv[1], inv[1])]
            both = contract(side_by_side(parts[0], parts[1]), jnp.concatenate(twice, 0), 1, 1)
            last = contract(side_by_side(parts[0], parts[2]), side_by_side(inv[2], inv[0]), 1, 1)
            image = both[:, :128] + both[:, 128:] + last
        else:
            basis = contract(side_by_side(inv[0], inv[2]), side_by_side(parts[2], parts[0]), 1, 1)
            basis += contract(side_by_side(inv[0], inv[1]), side_by_side(parts[1], parts[1]), 1, 1)
            basis += contract(side_by_side(inv[0], inv[1]), side_by_side(parts[0], parts[0]), 1, 1)

    basis = basis[:rank]
    factor_ref[...] = basis
    basis_high, basis_low = split(basis)
    for fetch in fetches:
        fetch.wait()
    both = contract(jnp.concatenate([basis_high, basis_low], 0), columns_high[...], 1, 0)
    share[...] = both[:rank] + both[rank:] + contract(basis_high, columns_low[...], 1, 0)
    own, wide = outs[0].shape[0] // 2, outs[0].shape[1]
    for here in range(2 * zs):

        @pl.when(2 * place_ref[0] + place_ref[1] == here)
        def _():
            for bits, out in enumerate(outs):
                rows = slice(own * (here ^ bits), own * (here ^ bits) + own)
                out[:own, :] = share[rows, :wide]
                out[own:, :] = share[rows, wide:]


def iterations(place, mine, other, start, parts, iters, zs):
    rank, n = start.shape
    part = parts[0].shape[1] + parts[2].shape[1]
    vmem, hbm = pl.BlockSpec(memory_space=pltpu.VMEM), pl.BlockSpec(memory_space=pltpu.HBM)
    return pl.pallas_call(
        functools.partial(iterations_kernel, iters, zs),
        out_shape=[jax.ShapeDtypeStruct(start.shape, jnp.float32)]
        + [jax.ShapeDtypeStruct((rank // zs, part // 2), jnp.float32)] * (2 * zs),
        in_specs=[pl.BlockSpec(memory_space=pltpu.SMEM)] + [vmem] * 3 + [hbm] * 4,
        out_specs=[vmem] * (1 + 2 * zs),
        scratch_shapes=[pltpu.VMEM((layout(n)[-1], 128), jnp.float32), pltpu.VMEM((n, n), jnp.float32)]
        + [pltpu.VMEM((n, n), jnp.bfloat16)] * 2
        + [pltpu.VMEM((n, part), jnp.bfloat16)] * 2
        + [pltpu.VMEM((rank, part), jnp.float32), pltpu.SemaphoreType.DMA((4,))],
        compiler_params=pltpu.CompilerParams(vmem_limit_bytes=50 * 2**20),
        name="iterations",
    )(place, mine, other, start, *parts)


def farthest_first(size):
    return [size - 1, *range(1, size - 1)]


def mirrored(bits, rest):
    side = int(rest**0.5)
    return bits % side * side + bits // side if side * side == rest else bits


def swap_rest(x, fibre, rest, bits):
    other = mirrored(bits, rest)
    pairs = [(f * rest + r, f * rest + (r ^ (other if f % 2 else bits))) for f in range(fibre) for r in range(rest)]
    return lax.ppermute(x, ("fibre", "rest"), pairs)


def sum_everywhere(core, mine, theirs, fibre, rest):
    r = lax.axis_index("rest")
    half, width = mine.shape
    piece = -(-half // (8 * rest)) * 8
    mine = mine + swap(theirs, "fibre", fibre, 1)
    mine = jnp.pad(mine, ((0, piece * rest - half), (0, 0)))
    peers = {bits: r ^ jnp.where(core == 0, bits, mirrored(bits, rest)) for bits in farthest_first(rest)}
    total = lax.dynamic_slice(mine, (r * piece, 0), (piece, width))
    for bits, peer in peers.items():
        part = lax.dynamic_slice(mine, (peer * piece, 0), (piece, width))
        total = total + swap_rest(part, fibre, rest, bits)
    terms = {bits: swap(total, "fibre", fibre, 2 * bits) for bits in farthest_first(fibre // 2)}
    terms = [terms.get(bits, total) for bits in range(fibre // 2)]
    while len(terms) > 1:
        last = len(terms) - 1
        terms = [terms[i] + terms[last - i] for i in range(1, len(terms) // 2)] + [terms[last] + terms[0]]
    total = terms[0]
    out = lax.dynamic_update_slice(jnp.zeros((rest, piece, width), jnp.float32), total[None], (r, 0, 0))
    for bits, peer in peers.items():
        out = lax.dynamic_update_slice(out, swap_rest(total, fibre, rest, bits)[None], (peer, 0, 0))
    out = out.reshape(rest * piece, width)[:half]
    return out, swap(out, "fibre", fibre, 1)


def assemble_kernel(distances, place_ref, *refs):
    blocks, out_ref = refs[:-1], refs[-1]
    f = 2 * place_ref[0] + place_ref[1]
    own, wide = out_ref.shape[0], blocks[0].shape[1]
    half = out_ref.shape[1] // 2
    for bits, block in zip(distances, blocks):
        source = f ^ bits
        at = pl.multiple_of((source % 2) * half + (source // 2) * (2 * wide), 128)
        out_ref[:, pl.ds(at, wide)] = block[:own, :]
        out_ref[:, pl.ds(at + wide, wide)] = block[own:, :]


def assemble(place, moved, cols):
    blocks = list(moved.values())
    vmem = pl.BlockSpec(memory_space=pltpu.VMEM)
    return pl.pallas_call(
        functools.partial(assemble_kernel, tuple(moved)),
        out_shape=jax.ShapeDtypeStruct((blocks[0].shape[0] // 2, cols), jnp.float32),
        in_specs=[pl.BlockSpec(memory_space=pltpu.SMEM)] + [vmem] * len(blocks),
        out_specs=vmem,
        compiler_params=pltpu.CompilerParams(vmem_limit_bytes=24 * 2**20),
        name="assemble",
    )(place, *blocks)


def shards(fibre, rest, slab, start_basis):
    rows, cols = slab.shape
    zs = fibre // 2
    f = lax.axis_index("fibre")
    z, core = f // 2, f % 2
    place = jnp.stack([z, core])
    half = cols // 2
    part = half // zs
    early = part * 3 // 4

    def cut(slab, whose, bits, start, width):
        return lax.dynamic_slice(slab, (0, whose * half + (z ^ bits) * part + start), (rows, width))

    far = zs - 1
    slab, theirs = lax.optimization_barrier((slab, cut(slab, 1 - core, far, 0, part)))
    mine = cut(slab, core, far, 0, part)
    cuts = [(bits, 0, part) for bits in range(far - 1, -1, -1)]
    others = jnp.concatenate([cut(slab, 1 - core, *c) for c in cuts], 1)
    block = in_order(core, mine, swap(theirs, "fibre", fibre, 1), 0)
    others, block = lax.optimization_barrier((others, block))
    arrived = {far: swap(block, "fibre", fibre, 2 * far)}
    got = swap(others, "fibre", fibre, 1)
    pieces = []
    for bits, start, width in cuts:
        split_here = bits > 1
        pieces += [(bits, 0, early), (bits, early, part - early)] if split_here else [(bits, start, width)]
    late = {}
    for (bits, start, _), block in zip(pieces, prepare(place, slab, got, part, zs, cuts, pieces)):
        if start:
            block, arrived[far] = lax.optimization_barrier((block, arrived[far]))
        into = late if start else arrived
        into[bits] = swap(block, "fibre", fibre, 2 * bits) if bits else block
    first = [arrived[bits] for bits in range(zs)]
    last = [late.get(bits, arrived[bits]) for bits in range(zs)]
    last_from = tuple(0 if bits in late else early for bits in range(zs))
    packed, *parts = gram_part(place, None, first, (0,) * zs, early)
    mine, theirs, *more = gram_part(place, packed, last, last_from, part - early)
    mine, other = sum_everywhere(core, mine, theirs, fibre, rest)
    factor, *blocks = iterations(place, mine, other, start_basis.T, [*parts, *more], ITERS, zs)
    order = [2 * bits + d for bits in farthest_first(zs) for d in range(2)]
    order.append(1)
    moved = {bits: swap(blocks[bits], "fibre", fibre, bits) for bits in order}
    moved[0] = blocks[0]
    return (factor.T, assemble(place, moved, cols))


def solution(mesh):
    fibre, rest = mesh.shape["fibre"], mesh.shape["rest"]
    return jax.shard_map(
        lambda slab, start_basis: shards(fibre, rest, slab, start_basis),
        mesh=mesh,
        in_specs=(P("fibre", "rest"), P()),
        out_specs=(P(), P("fibre", "rest")),
        check_vma=False,
    )
```
